256 devices in a mesh: trow: 16 (over x, y_lo, core), tcol: 16 (over y_hi, z).
Axes of the slice: x: 4, y: 4 (y_hi: 2, y_lo: 2; y = y_hi * 2 + y_lo), z: 8, core: 2. Of those that a mesh axis runs over, the one named last changes fastest.
Arguments:
- theta: float32 [25, 256, 4096], P(None, 'trow', 'tcol'), may hold values from -6 to 6
- salt: float32 [25, 256, 4096], P(None, 'trow', 'tcol'), may hold values from -6 to 6
- velocity_x: float32 [25, 256, 4096], P(None, 'trow', 'tcol'), may hold values from -0.5 to 0.5
- velocity_y: float32 [25, 256, 4096], P(None, 'trow', 'tcol'), may hold values from -0.5 to 0.5
- land_mask: int32 [25, 256, 4096], P(None, 'trow', 'tcol'), may hold values 0 or 1
- kappa: float32 [24, 256, 4096], P(None, 'trow', 'tcol'), may hold values from 0.02 to 5
- forcing: float32 [256, 4096], P('trow', 'tcol'), may hold values from -6 to 6
- bottom: int32 [256, 4096], P('trow', 'tcol'), may hold values from 0 to 25
- theta_cot: float32 [25, 256, 4096], P(None, 'trow', 'tcol'), may hold values from -6 to 6
- salt_cot: float32 [25, 256, 4096], P(None, 'trow', 'tcol'), may hold values from -6 to 6
- surface_cot: float32 [256, 4096], P('trow', 'tcol'), may hold values from -24 to 24
Outputs:
- theta_grad: float32 [25, 256, 4096], P(None, 'trow', 'tcol')
- salt_grad: float32 [25, 256, 4096], P(None, 'trow', 'tcol')
- kappa_grad: float32 [24, 256, 4096], P(None, 'trow', 'tcol')
- forcing_grad: float32 [256, 4096], P('trow', 'tcol')
The draws below stay inside these ranges and needn't reach their ends.
All inputs are finite; a program needn't handle non-finite values. No bound on the sum of `land_mask` on one device may be relied on, other than what follows from the above.
Results may differ from the reference program's by a relative error of at most 0.0001.
Values sent between devices are 32-bit elements; how exact they have to be, the bound alone decides.
No kernel may reach another device: no remote copies, remote signals or barrier semaphores. Data moves between devices by JAX's collectives and lax.ppermute only.
A program may use at most 64 MiB of HBM per device.

```python
import math
import jax
import jax.numpy as jnp
from jax import lax

NZ = 25
KZ = 24
ITERS = 4
NX = 256
NY = 4096


def draw_surface_cot(key, part):
    row_position = jnp.arange(NX, dtype=jnp.float32) / NX
    col_position = jnp.arange(NY, dtype=jnp.float32) / NY
    rising = (3.0 ** row_position)[:, None] * (3.0 ** col_position)[None, :] / 3.0
    key_first = jax.random.fold_in(key, 0)
    values = jax.random.normal(key_first, (NX, NY), jnp.float32) * rising
    return jnp.clip(values, -24.0, 24.0)


def place_ends(result, stream_key, smallest, top_value):
    spot = [jax.random.randint(jax.random.fold_in(stream_key, axis), (), 0, length) for axis, length in enumerate(result.shape)]
    main_axis = result.shape.index(max(result.shape))
    next_to = spot[:main_axis] + [(spot[main_axis] + 1) % result.shape[main_axis]] + spot[main_axis + 1:]
    return result.at[tuple(spot)].set(smallest).at[tuple(next_to)].set(top_value)


def level_of(rng, extent, cuts, least, top_value):
    loudness = 1.0
    for position, parts in cuts:
        steps = jax.random.uniform(jax.random.fold_in(jax.random.fold_in(rng, 6), position), (parts,), jnp.float32, least / len(cuts), top_value / len(cuts))
        loudness = loudness * jnp.repeat(jnp.exp(steps), extent[position] // parts).reshape((-1,) + (1,) * (len(extent) - 1 - position))
    return loudness


def scatter_about(key, extent, scale, bound, cuts=(), kind=jnp.bfloat16):
    gain = level_of(key, extent, cuts, -0.22, 0.18) if cuts else 1.0
    drawn = jax.random.normal(key, extent, jnp.float32) * scale * gain
    return jnp.minimum(jnp.maximum(drawn, -bound), bound).astype(kind)


def setup_inputs(seed: int = 0) -> dict:
    streams_of = jax.random.split(jax.random.key(seed), 12)
    theta = scatter_about(streams_of[0], (NZ, NX, NY), 1.0, 6.0, ((1, 16), (2, 16)), jnp.float32)
    salt = scatter_about(streams_of[1], (NZ, NX, NY), 1.0, 6.0, ((1, 16), (2, 16)), jnp.float32)
    velocity_x = jnp.clip(jax.random.uniform(streams_of[2], (NZ, NX, NY), jnp.float32, -0.5, 0.5) * level_of(streams_of[2], (NZ, NX, NY), ((1, 16), (2, 16)), -0.4, 0.0), -0.5, 0.5)
    velocity_y = jnp.clip(jax.random.uniform(streams_of[3], (NZ, NX, NY), jnp.float32, -0.5, 0.5) * level_of(streams_of[3], (NZ, NX, NY), ((1, 16), (2, 16)), -0.4, 0.0), -0.5, 0.5)
    land_mask = place_ends((jax.random.randint(streams_of[4], (NZ, NX, NY), 0, 8) < 7).astype(jnp.int32), jax.random.fold_in(streams_of[4], 1), 0, 1)
    kappa = jnp.clip(jnp.exp(math.log(5.0) - 5.521461 * jax.random.uniform(streams_of[5], (KZ, NX, NY), jnp.float32) ** level_of(streams_of[5], (KZ, NX, NY), ((1, 16), (2, 16)), -0.2, 0.2)), 0.02, 5.0)
    forcing = scatter_about(streams_of[6], (NX, NY), 1.0, 6.0, ((0, 16), (1, 16)), jnp.float32)
    bottom = place_ends(jax.random.randint(streams_of[7], (NX, NY), 0, NZ + 1), jax.random.fold_in(streams_of[7], 1), 0, NZ).astype(jnp.int32)
    theta_cot = scatter_about(streams_of[8], (NZ, NX, NY), 1.0, 6.0, ((1, 16), (2, 16)), jnp.float32)
    salt_cot = scatter_about(streams_of[9], (NZ, NX, NY), 1.0, 6.0, ((1, 16), (2, 16)), jnp.float32)
    surface_cot = draw_surface_cot(jax.random.fold_in(streams_of[11], 71), 0)
    return {"theta": theta, "salt": salt, "velocity_x": velocity_x, "velocity_y": velocity_y, "land_mask": land_mask, "kappa": kappa, "forcing": forcing, "bottom": bottom, "theta_cot": theta_cot, "salt_cot": salt_cot, "surface_cot": surface_cot}


def cut_along(array, start, count, axis_index):
    return lax.slice_in_dim(array, start, start + count, axis=axis_index)


def forward_change(padded_tracer, padded_velocity, padded_wet, axis_index, length):
    opened = cut_along(padded_velocity, 1, length + 1, axis_index) * cut_along(padded_wet, 1, length + 1, axis_index) * cut_along(padded_wet, 2, length + 1, axis_index)
    centre = cut_along(padded_tracer, 1, length + 1, axis_index) + cut_along(padded_tracer, 2, length + 1, axis_index)
    outer = cut_along(padded_tracer, 0, length + 1, axis_index) + cut_along(padded_tracer, 3, length + 1, axis_index)
    fluxes = opened * (7.0 * centre - outer) / 12.0
    return cut_along(fluxes, 1, length, axis_index) - cut_along(fluxes, 0, length, axis_index)


def adjoint_change(padded_lambda, padded_velocity, padded_wet, axis_index, length):
    opened = cut_along(padded_velocity, 0, length + 3, axis_index) * cut_along(padded_wet, 0, length + 3, axis_index) * cut_along(padded_wet, 1, length + 3, axis_index)
    faces = opened * (cut_along(padded_lambda, 0, length + 3, axis_index) - cut_along(padded_lambda, 1, length + 3, axis_index))
    return (7.0 * (cut_along(faces, 2, length, axis_index) + cut_along(faces, 1, length, axis_index)) - cut_along(faces, 3, length, axis_index) - cut_along(faces, 0, length, axis_index)) / 12.0


def advect(padded_tracer, padded_ux, padded_uy, padded_wet, tracer):
    row_count = padded_tracer.shape[1] - 4
    col_count = padded_tracer.shape[2] - 4
    along_rows = forward_change(padded_tracer[:, :, 2:-2], padded_ux[:, :, 2:-2], padded_wet[:, :, 2:-2], 1, row_count)
    along_cols = forward_change(padded_tracer[:, 2:-2, :], padded_uy[:, 2:-2, :], padded_wet[:, 2:-2, :], 2, col_count)
    return tracer - along_rows - along_cols


def advect_adjoint(padded_lambda, padded_ux, padded_uy, padded_wet, lambda_field, wet):
    row_count = padded_lambda.shape[1] - 4
    col_count = padded_lambda.shape[2] - 4
    along_rows = adjoint_change(padded_lambda[:, :, 2:-2], padded_ux[:, :, 2:-2], padded_wet[:, :, 2:-2], 1, row_count)
    along_cols = adjoint_change(padded_lambda[:, 2:-2, :], padded_uy[:, 2:-2, :], padded_wet[:, 2:-2, :], 2, col_count)
    return lambda_field - wet * (along_rows + along_cols)


def factorize(couple, depth):
    inverses = []
    ratios = []
    for depth_index in range(depth):
        diagonal = jnp.ones_like(couple[0])
        if depth_index > 0:
            diagonal = diagonal + couple[depth_index - 1] - couple[depth_index - 1] * ratios[depth_index - 1]
        if depth_index < depth - 1:
            diagonal = diagonal + couple[depth_index]
        inverse = 1.0 / diagonal
        inverses.append(inverse)
        if depth_index < depth - 1:
            ratios.append(couple[depth_index] * inverse)
    return inverses, ratios


def solve_columns(inverses, ratios, couple, rhs):
    depth = rhs.shape[0]
    sweeps = []
    carried = rhs[0] * inverses[0]
    sweeps.append(carried)
    for depth_index in range(1, depth):
        carried = (rhs[depth_index] + couple[depth_index - 1] * carried) * inverses[depth_index]
        sweeps.append(carried)
    results = [sweeps[depth - 1]]
    for depth_index in range(depth - 2, -1, -1):
        results.append(sweeps[depth_index] + ratios[depth_index] * results[-1])
    return jnp.stack(results[::-1])


def pad_rims(array):
    return jnp.pad(array, ((0, 0), (2, 2), (2, 2)))


def surface_apply(field, diagonal):
    padded = jnp.pad(field, 1)
    beside = padded[2:, 1:-1] + padded[:-2, 1:-1] + padded[1:-1, 2:] + padded[1:-1, :-2]
    return diagonal * field - beside


def conjugate(target, diagonal):
    solution = jnp.zeros_like(target)
    residual = target
    direction = target
    norm_now = jnp.sum(residual * residual)
    for iteration in range(ITERS):
        image = surface_apply(direction, diagonal)
        step_size = norm_now / jnp.sum(direction * image)
        solution = solution + step_size * direction
        residual = residual - step_size * image
        if iteration + 1 < ITERS:
            norm_next = jnp.sum(residual * residual)
            direction = residual + (norm_next / norm_now) * direction
            norm_now = norm_next
    return solution


def reference(theta, salt, velocity_x, velocity_y, land_mask, kappa, forcing, bottom, theta_cot, salt_cot, surface_cot):
    depth = theta.shape[0]
    levels = jnp.arange(depth, dtype=jnp.int32)[:, None, None]
    wet = land_mask.astype(jnp.float32) * (levels < bottom[None]).astype(jnp.float32)
    padded_ux = pad_rims(velocity_x)
    padded_uy = pad_rims(velocity_y)
    padded_wet = pad_rims(wet)
    theta_adv = advect(pad_rims(theta * wet), padded_ux, padded_uy, padded_wet, theta)
    salt_adv = advect(pad_rims(salt * wet), padded_ux, padded_uy, padded_wet, salt)
    couple = [kappa[depth_index] * wet[depth_index] * wet[depth_index + 1] for depth_index in range(depth - 1)]
    inverses, ratios = factorize(couple, depth)
    source = jnp.concatenate([theta_adv[:1] + (forcing * wet[0])[None], theta_adv[1:]], axis=0)
    theta_mix = solve_columns(inverses, ratios, couple, source)
    salt_mix = solve_columns(inverses, ratios, couple, salt_adv)
    diagonal = 4.2 + bottom.astype(jnp.float32) / depth
    zeta = conjugate(surface_cot, diagonal)
    theta_total = theta_cot + 0.2 * wet * zeta[None]
    salt_total = salt_cot - 0.15 * wet * zeta[None]
    theta_mu = solve_columns(inverses, ratios, couple, theta_total)
    salt_mu = solve_columns(inverses, ratios, couple, salt_total)
    opened = wet[:-1] * wet[1:]
    kappa_grad = -opened * ((theta_mu[:-1] - theta_mu[1:]) * (theta_mix[:-1] - theta_mix[1:]) + (salt_mu[:-1] - salt_mu[1:]) * (salt_mix[:-1] - salt_mix[1:]))
    forcing_grad = zeta + wet[0] * theta_mu[0]
    theta_grad = advect_adjoint(pad_rims(theta_mu), padded_ux, padded_uy, padded_wet, theta_mu, wet)
    salt_grad = advect_adjoint(pad_rims(salt_mu), padded_ux, padded_uy, padded_wet, salt_mu, wet)
    return theta_grad, salt_grad, kappa_grad, forcing_grad
```

```python
import functools

import jax
import jax.numpy as jnp
from jax import lax
from jax.experimental import pallas as pl
from jax.experimental.pallas import tpu as pltpu
from jax.sharding import Mesh
from jax.sharding import PartitionSpec as P

TROW = ("trow_0", "trow_1", "trow_2")
TCOL = ("tcol_0", "tcol_1")
ALL = TROW + TCOL
CENTRE = 4.75
KRYLOV = 4
PAIRS = [(i, j) for i in range(KRYLOV) for j in range(i, KRYLOV)]
F32 = jnp.float32
VM = pl.BlockSpec(memory_space=pltpu.VMEM)
SM = pl.BlockSpec(memory_space=pltpu.SMEM)
PARAMS = pltpu.CompilerParams(vmem_limit_bytes=24 * 1024 * 1024)


def iota(shape, dim):
    return lax.broadcasted_iota(jnp.int32, shape, dim)


def two_sum(a, b):
    s = a + b
    t = s - a
    return s, (a - (s - t)) + (b - t)


def quick_two_sum(a, b):
    s = a + b
    return s, b - (s - a)


def halves(a):
    t = a * 4097.0
    high = t - (t - a)
    return high, a - high


def two_prod(a, b, a_parts, b_parts):
    p = a * b
    ah, al = a_parts
    bh, bl = b_parts
    return p, ((ah * bh - p) + ah * bl + al * bh) + al * bl


def df_add(a, b):
    s, e = two_sum(a[0], b[0])
    return quick_two_sum(s, e + (a[1] + b[1]))


def df_mul(a, b):
    p, e = two_prod(a[0], b[0], halves(a[0]), halves(b[0]))
    return quick_two_sum(p, e + (a[0] * b[1] + a[1] * b[0]))


def df_div(a, b):
    inverse = 1.0 / b[0]
    q1 = a[0] * inverse
    back = df_mul((q1, jnp.zeros_like(q1)), b)
    rest = df_add(a, (-back[0], -back[1]))
    return quick_two_sum(q1, rest[0] * inverse)


def edges_kernel(cot_ref, bottom_ref, rows_ref, cols_ref, corner_ref):
    cot = cot_ref[...]
    bottom = bottom_ref[...].astype(F32)
    rows_ref[0:8] = cot[8:16]
    rows_ref[8:16] = bottom[8:16]
    cols_ref[0:16] = cot[:, 128:256]
    cols_ref[16:32] = bottom[:, 128:256]
    corner_ref[0:8] = cot[8:16, 128:256]
    corner_ref[8:16] = bottom[8:16, 128:256]


def merge_rows(a, b, step):
    shape = a[0].shape
    first = (iota(shape, 0) & step) == 0

    def part(x, y):
        mixed = jnp.where(first, y, x)
        if step == 4:
            other = pltpu.roll(mixed, 4, 0)
        else:
            other = jnp.where(first, pltpu.roll(mixed, 8 - step, 0), pltpu.roll(mixed, step, 0))
        return jnp.where(first, x, y), other

    kept_high, other_high = part(a[0], b[0])
    kept_low, other_low = part(a[1], b[1])
    return df_add((kept_high, kept_low), (other_high, other_low))


def krylov_kernel(
    place_ref, cot_ref, bottom_ref, rows_ref, cols_ref, corner_ref, sums_ref, own_ref, up_ref, left_ref, diag_ref
):
    r = place_ref[0]
    c = place_ref[1]
    shape = (24, 384)
    row = iota(shape, 0)
    lane = iota(shape, 1)

    def window(main, at):
        top = jnp.concatenate([corner_ref[8 * at : 8 * at + 8], rows_ref[8 * at : 8 * at + 8]], axis=1)
        rest = jnp.concatenate([cols_ref[16 * at : 16 * at + 16], main], axis=1)
        return jnp.concatenate([top, rest], axis=0)

    inside = ((row >= 8) | (r > 0)) & ((lane >= 128) | (c > 0))
    start = jnp.where(inside, window(cot_ref[...], 0), 0.0)
    bottom = window(bottom_ref[...].astype(F32), 1)
    shifted = (4.2 + bottom / 25.0) - CENTRE

    def apply_shifted(v):
        below = jnp.where(row == 23, 0.0, pltpu.roll(v, 23, 0))
        right = jnp.where(lane == 383, 0.0, pltpu.roll(v, 383, 1))
        beside = below + pltpu.roll(v, 1, 0) + right + pltpu.roll(v, 1, 1)
        return jnp.where(inside, shifted * v - beside, 0.0)

    vectors = [start]
    images = []
    for step in range(KRYLOV):
        moved = apply_shifted(vectors[-1])
        images.append(moved + CENTRE * vectors[-1])
        if step == 0:
            vectors.append(moved * 0.25)
        elif step + 1 < KRYLOV:
            vectors.append(moved * 0.5 - vectors[-2])

    domain = (
        (row >= 4)
        & (row < jnp.where(r == 15, 24, 20))
        & (lane >= 124)
        & (lane < jnp.where(c == 15, 384, 380))
    )
    cut = [jnp.where(domain, v, 0.0) for v in vectors]
    cut_parts = [halves(v) for v in cut]
    image_parts = [halves(w) for w in images]

    def tile(x, at):
        i, j = divmod(at, 3)
        return x[8 * i : 8 * i + 8, 128 * j : 128 * j + 128]

    def dot(x, x_parts, y, y_parts):
        total = None
        for at in range(9):
            p, e = two_prod(
                tile(x, at),
                tile(y, at),
                [tile(h, at) for h in x_parts],
                [tile(h, at) for h in y_parts],
            )
            if total is None:
                total = (p, e)
            else:
                s, f = two_sum(total[0], p)
                total = (s, total[1] + (e + f))
        return total

    dots = [dot(cut[i], cut_parts[i], images[j], image_parts[j]) for i, j in PAIRS]
    start_parts = halves(start)
    dots += [dot(cut[i], cut_parts[i], start, start_parts) for i in range(KRYLOV)]
    zero = jnp.zeros((8, 128), F32)
    dots += [(zero, zero)] * (16 - len(dots))
    packed = []
    for base in (0, 8):
        group = dots[base : base + 8]
        for step in (4, 2, 1):
            group = [merge_rows(group[i], group[i + step], step) for i in range(step)]
        total = group[0]
        for step in (64, 32, 16, 8, 4, 2, 1):
            total = df_add(total, (pltpu.roll(total[0], step, 1), pltpu.roll(total[1], step, 1)))
        packed.append(total)
    small_row = iota((8, 128), 0)
    small_lane = iota((8, 128), 1)
    spread = zero
    for part in (0, 1):
        for base in (0, 1):
            chosen = jnp.zeros((8, 128), jnp.bool_)
            for i in range(KRYLOV):
                for j in range(KRYLOV + 1):
                    index = len(PAIRS) + i if j == KRYLOV else PAIRS.index((min(i, j), max(i, j)))
                    if index // 8 == base:
                        chosen = chosen | (
                            (small_row == index % 8) & (small_lane == 32 * part + 8 * i + j)
                        )
            spread = spread + jnp.where(chosen, packed[base][part], 0.0)
    line = jnp.sum(spread, axis=0, keepdims=True)
    sums_ref[...] = jnp.broadcast_to(line, (256, 128))

    for k, v in enumerate(vectors):
        own_ref[24 * k : 24 * k + 24] = v
        near = pltpu.roll(v[0:16], 12, 0)[0:8]
        up_ref[8 * k : 8 * k + 8] = near
        left_ref[24 * k : 24 * k + 24] = pltpu.roll(v[:, 0:256], 192, 1)[:, 0:128]
        diag_ref[8 * k : 8 * k + 8] = pltpu.roll(near[:, 0:256], 192, 1)[:, 0:128]


def columns_kernel(
    theta_ref,
    salt_ref,
    ux_ref,
    uy_ref,
    land_ref,
    kappa_ref,
    bottom_ref,
    tcot_ref,
    scot_ref,
    a_ref,
    c_ref,
    w_ref,
    inv_ref,
    ratio_ref,
    down_ref,
    up_ref,
    right_ref,
    left_ref,
):
    depth = theta_ref.shape[0]
    bottom = bottom_ref[...]

    def wet_at(k):
        return jnp.where(k < bottom, land_ref[k].astype(F32), 0.0)

    wet = wet_at(0)
    ratio = None
    couple_last = None
    state = None
    for k in range(depth):
        diagonal = jnp.ones((16, 256), F32)
        if k > 0:
            diagonal = diagonal + couple_last - couple_last * ratio
        if k < depth - 1:
            wet_next = wet_at(k + 1)
            couple = kappa_ref[k] * wet * wet_next
            diagonal = diagonal + couple
        inverse = 1.0 / diagonal
        rhs = (tcot_ref[k], scot_ref[k], wet)
        if k == 0:
            state = tuple(x * inverse for x in rhs)
        else:
            state = tuple((x + couple_last * s) * inverse for x, s in zip(rhs, state))
        a_ref[k], c_ref[k], w_ref[k] = state
        inv_ref[k] = inverse
        if k < depth - 1:
            ratio = couple * inverse
            ratio_ref[k] = ratio
            couple_last = couple
            wet = wet_next

    half = (8, 256)
    half_row = iota(half, 0)
    col = (16, 128)
    lane = iota(col, 1)

    def choose(parts, index, width):
        out = parts[-1]
        for n in range(len(parts) - 2, -1, -1):
            out = jnp.where(index < (n + 1) * width, parts[n], out)
        return out

    pending = None
    for k in range(depth - 1, -1, -1):
        wet = wet_at(k)
        if k < depth - 1:
            ratio = ratio_ref[k]
            state = tuple(x + ratio * s for x, s in zip((a_ref[k], c_ref[k], w_ref[k]), state))
            a_ref[k], c_ref[k], w_ref[k] = state
        fields = (theta_ref[k] * wet, salt_ref[k] * wet) + state
        ux = ux_ref[k]
        uy = uy_ref[k]
        low = [f[8:16] for f in fields]
        high = [f[0:8] for f in fields]
        down_ref[8 * k : 8 * k + 8] = choose(
            [pltpu.roll(low[n], (2 + 2 * n) % 8, 0) if n < 3 else low[n] for n in range(4)], half_row, 2
        )
        up_ref[8 * k : 8 * k + 8] = choose(
            [pltpu.roll(high[n], 2 * n, 0) if n else high[n] for n in range(4)], half_row, 2
        )
        flow = ux[8:16] * wet[8:16]
        flow_open = flow * pltpu.roll(wet[8:16], 7, 0)
        tail_down = choose(
            [pltpu.roll(low[4], 2, 0), jnp.where(half_row == 2, pltpu.roll(flow_open, 4, 0), pltpu.roll(flow, 4, 0))],
            half_row,
            2,
        )
        top_open = ux[0:8] * wet[0:8] * pltpu.roll(wet[0:8], 7, 0)
        tail_up = choose(
            [high[4], jnp.where(half_row == 2, pltpu.roll(top_open, 2, 0), pltpu.roll(wet[0:8], 3, 0))],
            half_row,
            2,
        )
        if k % 2:
            pending = (pltpu.roll(tail_down, 4, 0), pltpu.roll(tail_up, 4, 0))
        else:
            at = 8 * depth + 8 * (k // 2)
            if pending is None:
                pending = (tail_down, tail_up)
            down_ref[at : at + 8] = jnp.where(half_row < 4, tail_down, pending[0])
            up_ref[at : at + 8] = jnp.where(half_row < 4, tail_up, pending[1])
        last = [f[:, 128:256] for f in fields]
        first = [f[:, 0:128] for f in fields]
        edge_flow = uy[:, 128:256] * wet[:, 128:256]
        edge_open = edge_flow * pltpu.roll(wet[:, 128:256], 127, 1)
        last.append(jnp.where(lane == 126, edge_open, edge_flow))
        first_open = uy[:, 0:128] * wet[:, 0:128] * pltpu.roll(wet[:, 0:128], 127, 1)
        first.append(jnp.where(lane == 0, first_open, pltpu.roll(wet[:, 0:128], 1, 1)))
        right_ref[k] = choose(
            [pltpu.roll(last[n], 128 - 2 * n, 1) if n else last[n] for n in range(5, -1, -1)], lane - 116, 2
        )
        left_ref[k] = choose([pltpu.roll(first[n], 2 * n, 1) if n else first[n] for n in range(6)], lane, 2)


def final_kernel(
    place_ref,
    sums_ref,
    own_ref,
    from_below_ref,
    from_right_ref,
    from_corner_ref,
    theta_ref,
    salt_ref,
    ux_ref,
    uy_ref,
    land_ref,
    kappa_ref,
    forcing_ref,
    bottom_ref,
    a_ref,
    c_ref,
    w_ref,
    inv_ref,
    ratio_ref,
    above_ref,
    below_ref,
    west_ref,
    east_ref,
    theta_grad_ref,
    salt_grad_ref,
    kappa_grad_ref,
    forcing_grad_ref,
    theta_sweep_ref,
    salt_sweep_ref,
):
    depth = theta_ref.shape[0]
    r = place_ref[0]
    c = place_ref[1]
    has_up = jnp.where(r > 0, 1.0, 0.0)
    has_down = jnp.where(r < 15, 1.0, 0.0)
    has_left = jnp.where(c > 0, 1.0, 0.0)
    has_right = jnp.where(c < 15, 1.0, 0.0)

    small = (8, 128)
    small_row = iota(small, 0)
    total = (sums_ref[0:8], jnp.zeros(small, F32))
    for at in range(1, 32):
        s, e = two_sum(total[0], sums_ref[8 * at : 8 * at + 8])
        total = (s, total[1] + e)
    for step in (4, 2, 1):
        s, e = two_sum(total[0], pltpu.roll(total[0], step, 0))
        total = (s, (total[1] + pltpu.roll(total[1], step, 0)) + e)
    low = total[1] + pltpu.roll(total[0] + total[1], 96, 1)
    total = quick_two_sum(total[0], low)

    def as_rows(x):
        out = x
        for i in range(1, KRYLOV):
            out = jnp.where(small_row == i, pltpu.roll(x, 128 - 8 * i, 1), out)
        return out

    system = (as_rows(total[0]), as_rows(total[1]))

    def row_of(x, k):
        return jnp.broadcast_to(x[k : k + 1, :], small)

    def lane_of(x, k):
        return jnp.broadcast_to(x[:, k : k + 1], small)

    keep = []
    weights = []
    scales = [lane_of(row_of(system[0], k), k) for k in range(KRYLOV)]
    for k in range(KRYLOV):
        across = (row_of(system[0], k), row_of(system[1], k))
        pivot = (lane_of(across[0], k), lane_of(across[1], k))
        fine = pivot[0] > 1e-13 * scales[k]
        keep.append(fine)
        pivot = (jnp.where(fine, pivot[0], 1.0), jnp.where(fine, pivot[1], 0.0))
        factor = df_div((lane_of(system[0], k), lane_of(system[1], k)), pivot)
        used = fine & (small_row != k)
        factor = (jnp.where(used, factor[0], 0.0), jnp.where(used, factor[1], 0.0))
        product = df_mul(factor, across)
        system = df_add(system, (-product[0], -product[1]))
    for k in range(KRYLOV):
        pivot = lane_of(row_of(system[0], k), k)
        value = lane_of(row_of(system[0], k), KRYLOV)
        value = jnp.where(keep[k], value / jnp.where(keep[k], pivot, 1.0), 0.0)
        weights.append(value[0:1, 0:1])

    def combined(ref, rows):
        out = weights[0] * ref[0:rows]
        for k in range(1, KRYLOV):
            out = out + weights[k] * ref[rows * k : rows * k + rows]
        return out

    def rows_joined(upper, lower):
        turned = pltpu.roll(lower, 4, 0)
        row8 = iota(turned.shape, 0)
        middle = jnp.where((row8 >= 5) & (r < 15), turned, upper[16:24])
        return jnp.concatenate([upper[0:16], middle, turned * has_down], axis=0)

    joined = rows_joined(combined(own_ref, 24), combined(from_below_ref, 8))
    beside = pltpu.roll(rows_joined(combined(from_right_ref, 24), combined(from_corner_ref, 8)), 64, 1)
    lane_wide = iota((32, 128), 1)
    ending = jnp.where((lane_wide >= 125) & (c < 15), beside, joined[:, 256:384])
    surface = jnp.concatenate([joined[:, 128:256], ending], axis=1)
    zeta = surface[8:24]
    zeta_up = (surface[7:8], surface[6:7])
    zeta_down = (surface[24:25], surface[25:26])
    zeta_left = (joined[8:24, 127:128], joined[8:24, 126:127])
    zeta_right = (beside[8:24, 0:1] * has_right, beside[8:24, 1:2] * has_right)

    bottom = bottom_ref[...]
    shape = (16, 256)
    row = iota(shape, 0)
    lane = iota(shape, 1)
    first_row = row == 0
    last_row = row == 15
    first_lane = lane == 0
    last_lane = lane == 255

    def before(q, edge, axis):
        return jnp.where(first_row if axis == 0 else first_lane, edge, pltpu.roll(q, 1, axis))

    def after(q, edge, axis):
        return jnp.where(
            last_row if axis == 0 else last_lane, edge, pltpu.roll(q, shape[axis] - 1, axis)
        )

    def start_of(q, axis):
        return q[0:1, :] if axis == 0 else q[:, 0:1]

    def end_of(q, axis):
        return q[15:16, :] if axis == 0 else q[:, 255:256]

    def wet_at(k):
        return jnp.where(k < bottom, land_ref[k].astype(F32), 0.0)

    def row_edges(k, f):
        if f < 4:
            at = 8 * k + 2 * f
        else:
            at = 8 * depth + 8 * (k // 2) + 4 * (k % 2) + 2 * (f - 4)
        up = (above_ref[at + 1 : at + 2] * has_up, above_ref[at : at + 1] * has_up)
        down = (below_ref[at : at + 1] * has_down, below_ref[at + 1 : at + 2] * has_down)
        return up, down

    def col_edges(k, f):
        at = 126 - 2 * f
        left = (west_ref[k, :, at + 1 : at + 2] * has_left, west_ref[k, :, at : at + 1] * has_left)
        at = 2 * f
        right = (east_ref[k, :, at : at + 1] * has_right, east_ref[k, :, at + 1 : at + 2] * has_right)
        return left, right

    def edges(k, f, axis):
        return row_edges(k, f) if axis == 0 else col_edges(k, f)

    def open_faces(k, wet, axis):
        velocity = (ux_ref if axis == 0 else uy_ref)[k]
        (flow, outer), (far, wet_next) = edges(k, 5, axis)
        scale = 1.0 / 12.0
        main = velocity * wet * after(wet, wet_next, axis) * scale
        low = (flow * start_of(wet, axis) * scale, outer * scale)
        return main, low, far * scale

    def spread_of(k, q, f, faces, axis):
        main, low, _ = faces
        (q1, q2), (q3, q4) = edges(k, f, axis)
        pair = q + after(q, q3, axis)
        pair_low = q1 + start_of(q, axis)
        flux = main * (8.0 * pair - before(pair, pair_low, axis) - after(pair, q3 + q4, axis))
        flux_low = low[0] * (8.0 * pair_low - (q1 + q2) - start_of(pair, axis))
        return flux - before(flux, flux_low, axis)

    def gathered(m, m_low, m_high, faces, axis):
        main, low, far = faces
        h = main * (m - after(m, m_high[0], axis))
        h1 = low[0] * (m_low[0] - start_of(m, axis))
        h2 = low[1] * (m_low[1] - m_low[0])
        h3 = far * (m_high[0] - m_high[1])
        pair = h + before(h, h1, axis)
        return 8.0 * pair - before(pair, h1 + h2, axis) - after(pair, h3 + end_of(h, axis), axis)

    theta_state = None
    salt_state = None
    couple_last = None
    wet = wet_at(0)
    for k in range(depth):
        x_faces = open_faces(k, wet, 0)
        y_faces = open_faces(k, wet, 1)
        advected = []
        for f, ref in ((0, theta_ref), (1, salt_ref)):
            q = ref[k]
            masked = q * wet
            advected.append(q - spread_of(k, masked, f, x_faces, 0) - spread_of(k, masked, f, y_faces, 1))
        if k == 0:
            advected[0] = advected[0] + forcing_ref[...] * wet
        inverse = inv_ref[k]
        if k == 0:
            theta_state = advected[0] * inverse
            salt_state = advected[1] * inverse
        else:
            theta_state = (advected[0] + couple_last * theta_state) * inverse
            salt_state = (advected[1] + couple_last * salt_state) * inverse
        theta_sweep_ref[k] = theta_state
        salt_sweep_ref[k] = salt_state
        if k < depth - 1:
            wet_next = wet_at(k + 1)
            couple_last = kappa_ref[k] * wet * wet_next
            wet = wet_next

    weight = (0.2, -0.15)
    mu_later = None
    wet_later = None
    for k in range(depth - 1, -1, -1):
        wet = wet_at(k)
        w = w_ref[k]
        w_edges = (row_edges(k, 4), col_edges(k, 4))
        mu = (a_ref[k] + 0.2 * zeta * w, c_ref[k] - 0.15 * zeta * w)
        if k < depth - 1:
            ratio = ratio_ref[k]
            theta_new = theta_sweep_ref[k] + ratio * theta_state
            salt_new = salt_sweep_ref[k] + ratio * salt_state
            kappa_grad_ref[k] = -(wet * wet_later) * (
                (mu[0] - mu_later[0]) * (theta_new - theta_state)
                + (mu[1] - mu_later[1]) * (salt_new - salt_state)
            )
            theta_state = theta_new
            salt_state = salt_new
        faces = (open_faces(k, wet, 0), open_faces(k, wet, 1))
        for n, ref in ((0, theta_grad_ref), (1, salt_grad_ref)):
            total = None
            for axis in (0, 1):
                low, high = edges(k, 2 + n, axis)
                w_low, w_high = w_edges[axis]
                z_low, z_high = (zeta_up, zeta_down) if axis == 0 else (zeta_left, zeta_right)
                m_low = tuple(low[i] + weight[n] * z_low[i] * w_low[i] for i in (0, 1))
                m_high = tuple(high[i] + weight[n] * z_high[i] * w_high[i] for i in (0, 1))
                part = gathered(mu[n], m_low, m_high, faces[axis], axis)
                total = part if total is None else total + part
            ref[k] = mu[n] - wet * total
        if k == 0:
            forcing_grad_ref[...] = zeta + wet * mu[0]
        mu_later = mu
        wet_later = wet


def call(kernel, outs, args, scalars=0, scratch=()):
    return pl.pallas_call(
        kernel,
        out_shape=[jax.ShapeDtypeStruct(s, F32) for s in outs],
        in_specs=[SM] * scalars + [VM] * (len(args) - scalars),
        out_specs=[VM] * len(outs),
        scratch_shapes=[pltpu.VMEM(s, F32) for s in scratch],
        compiler_params=PARAMS,
    )(*args)


def around(count, step):
    return [(i, (i + step) % count) for i in range(count)]


def across(step):
    return [
        (16 * i + j, 16 * ((i + step) % 16) + (j + step) % 16) for i in range(16) for j in range(16)
    ]


def shards(
    theta,
    salt,
    velocity_x,
    velocity_y,
    land_mask,
    kappa,
    forcing,
    bottom,
    theta_cot,
    salt_cot,
    surface_cot,
):
    depth = theta.shape[0]
    whole = theta.shape
    place = jnp.stack([lax.axis_index(TROW), lax.axis_index(TCOL)]).astype(jnp.int32)
    rows, cols, corner = call(
        edges_kernel, [(16, 256), (32, 128), (16, 128)], (surface_cot, bottom)
    )
    rows = lax.ppermute(rows, TROW, around(16, 1))
    cols = lax.ppermute(cols, TCOL, around(16, 1))
    corner = lax.ppermute(corner, ALL, across(1))
    lines = 8 * depth + 8 * ((depth + 1) // 2)
    a, c, w, inv, ratio, down, up, right, left = call(
        columns_kernel,
        [whole] * 4 + [kappa.shape] + [(lines, 256)] * 2 + [(depth, 16, 128)] * 2,
        (theta, salt, velocity_x, velocity_y, land_mask, kappa, bottom, theta_cot, salt_cot),
    )
    above = lax.ppermute(down, TROW, around(16, 1))
    below = lax.ppermute(up, TROW, around(16, -1))
    west = lax.ppermute(right, TCOL, around(16, 1))
    east = lax.ppermute(left, TCOL, around(16, -1))
    sums, own, near, side, tip = call(
        krylov_kernel,
        [(256, 128), (96, 384), (32, 384), (96, 128), (32, 128)],
        (place, surface_cot, bottom, rows, cols, corner),
        scalars=1,
    )
    near = lax.ppermute(near, TROW, around(16, -1))
    side = lax.ppermute(side, TCOL, around(16, -1))
    tip = lax.ppermute(tip, ALL, across(-1))
    sums = lax.all_to_all(sums, ALL, 0, 0, tiled=True)
    return tuple(
        call(
            final_kernel,
            [whole, whole, kappa.shape, forcing.shape],
            (place, sums, own, near, side, tip, theta, salt, velocity_x, velocity_y, land_mask, kappa)
            + (forcing, bottom, a, c, w, inv, ratio, above, below, west, east),
            scalars=1,
            scratch=[whole, whole],
        )
    )


def solution(mesh):
    split = Mesh(mesh.devices.reshape(4, 2, 2, 2, 8), ALL)
    block = P(None, TROW, TCOL)
    flat = P(TROW, TCOL)
    return jax.shard_map(
        shards,
        mesh=split,
        in_specs=(block,) * 6 + (flat, flat, block, block, flat),
        out_specs=(block, block, block, flat),
        check_vma=False,
    )
```

```python
import functools

import jax
import jax.numpy as jnp
from jax import lax
from jax.experimental import pallas as pl
from jax.experimental.pallas import tpu as pltpu
from jax.sharding import Mesh
from jax.sharding import PartitionSpec as P

TROW = ("trow_0", "trow_1", "trow_2")
TCOL = ("tcol_0", "tcol_1")
ALL = TROW + TCOL
CENTRE = 4.75
KRYLOV = 4
PAIRS = [(i, j) for i in range(KRYLOV) for j in range(i, KRYLOV)]
F32 = jnp.float32
VM = pl.BlockSpec(memory_space=pltpu.VMEM)
SM = pl.BlockSpec(memory_space=pltpu.SMEM)
HB = pl.BlockSpec(memory_space=pltpu.HBM)
PARAMS = pltpu.CompilerParams(vmem_limit_bytes=24 * 1024 * 1024)


def iota(shape, dim):
    return lax.broadcasted_iota(jnp.int32, shape, dim)


def two_sum(a, b):
    s = a + b
    t = s - a
    return s, (a - (s - t)) + (b - t)


def quick_two_sum(a, b):
    s = a + b
    return s, b - (s - a)


def halves(a):
    t = a * 4097.0
    high = t - (t - a)
    return high, a - high


def two_prod(a, b, a_parts, b_parts):
    p = a * b
    ah, al = a_parts
    bh, bl = b_parts
    return p, ((ah * bh - p) + ah * bl + al * bh) + al * bl


def df_add(a, b):
    s, e = two_sum(a[0], b[0])
    return quick_two_sum(s, e + (a[1] + b[1]))


def df_mul(a, b):
    p, e = two_prod(a[0], b[0], halves(a[0]), halves(b[0]))
    return quick_two_sum(p, e + (a[0] * b[1] + a[1] * b[0]))


def df_div(a, b):
    inverse = 1.0 / b[0]
    q1 = a[0] * inverse
    back = df_mul((q1, jnp.zeros_like(q1)), b)
    rest = df_add(a, (-back[0], -back[1]))
    return quick_two_sum(q1, rest[0] * inverse)


class Loaded:
    def __init__(self, source, ref, sem):
        self.ref = ref
        self.copy = pltpu.make_async_copy(source, ref, sem)
        self.copy.start()
        self.waited = False

    def get(self):
        if not self.waited:
            self.copy.wait()
            self.waited = True
        return self.ref


class Stored:
    def __init__(self, target, ref, take_sem, pending):
        self.target, self.ref, self.take_sem, self.pending = target, ref, take_sem, pending

    def send(self, start=None, count=None):
        source, target = self.ref, self.target
        if start is not None:
            source, target = source.at[pl.ds(start, count)], target.at[pl.ds(start, count)]
        copy = pltpu.make_async_copy(source, target, self.take_sem())
        copy.start()
        self.pending.append(copy)


def staged(kernel, args, outs, place=None, scratch=(), sends=None, aliases=None, views=None):
    views = views or {}
    aliases = aliases or {}
    aliased = [args[i] for i in aliases]
    loaded_args = [a for i, a in enumerate(args) if i not in aliases]
    smem = [] if place is None else [place]
    n_in, n_alias, n_out = len(loaded_args), len(aliased), len(outs)
    sends = sends or n_out
    staging = [pltpu.VMEM(a.shape, a.dtype) for a in loaded_args]
    for n, shape in enumerate(outs):
        held = (views[n][1],) + tuple(shape[1:]) if n in views else shape
        staging.append(pltpu.VMEM(held, F32))

    def body(*refs):
        refs = list(refs)
        places = [refs.pop(0) for _ in smem]
        sources = [refs.pop(0) for _ in range(n_in)]
        for _ in range(n_alias):
            refs.pop(0)
        targets = [refs.pop(0) for _ in range(n_out)]
        buffers = [refs.pop(0) for _ in range(n_in)]
        holds = [refs.pop(0) for _ in range(n_out)]
        in_sems, out_sems = refs.pop(-2), refs.pop(-1)
        ins = [Loaded(s, b, in_sems.at[n]) for n, (s, b) in enumerate(zip(sources, buffers))]
        pending = []
        given = []
        for n in range(n_out):
            target = targets[n].at[pl.ds(*views[n])] if n in views else targets[n]
            given.append(Stored(target, holds[n], lambda: out_sems.at[len(pending)], pending))
        kernel(ins, given, *places, *refs)
        for x in ins:
            x.get()
        for copy in pending:
            copy.wait()

    return pl.pallas_call(
        body,
        out_shape=[jax.ShapeDtypeStruct(s, F32) for s in outs],
        in_specs=[SM] * len(smem) + [HB] * (n_in + n_alias),
        out_specs=[HB] * n_out,
        input_output_aliases={len(smem) + n_in + i: out for i, out in enumerate(aliases.values())},
        scratch_shapes=staging
        + [pltpu.VMEM(s, F32) for s in scratch]
        + [pltpu.SemaphoreType.DMA((n_in,)), pltpu.SemaphoreType.DMA((sends,))],
        compiler_params=PARAMS,
    )(*smem, *loaded_args, *aliased)


def edges_kernel(ins, outs):
    cot_ref, bottom_ref = [x.get() for x in ins]
    rows_ref, cols_ref, corner_ref = [x.ref for x in outs]
    cot = cot_ref[...]
    bottom = bottom_ref[...].astype(F32)
    rows_ref[0:8] = cot[8:16]
    rows_ref[8:16] = bottom[8:16]
    cols_ref[0:16] = cot[:, 128:256]
    cols_ref[16:32] = bottom[:, 128:256]
    corner_ref[0:8] = cot[8:16, 128:256]
    corner_ref[8:16] = bottom[8:16, 128:256]
    for out in outs:
        out.send()


def merge_rows(a, b, step):
    shape = a[0].shape
    first = (iota(shape, 0) & step) == 0

    def part(x, y):
        mixed = jnp.where(first, y, x)
        if step == 4:
            other = pltpu.roll(mixed, 4, 0)
        else:
            other = jnp.where(first, pltpu.roll(mixed, 8 - step, 0), pltpu.roll(mixed, step, 0))
        return jnp.where(first, x, y), other

    kept_high, other_high = part(a[0], b[0])
    kept_low, other_low = part(a[1], b[1])
    return df_add((kept_high, kept_low), (other_high, other_low))


def krylov_kernel(ins, outs, place_ref):
    cot_ref, bottom_ref, rows_ref, cols_ref, corner_ref = [x.get() for x in ins]
    up_out, left_out, sums_out, own_out, diag_out = outs
    sums_ref, own_ref, up_ref, left_ref, diag_ref = [
        x.ref for x in (sums_out, own_out, up_out, left_out, diag_out)
    ]
    r = place_ref[0]
    c = place_ref[1]
    shape = (24, 384)
    row = iota(shape, 0)
    lane = iota(shape, 1)

    def window(main, at):
        top = jnp.concatenate([corner_ref[8 * at : 8 * at + 8], rows_ref[8 * at : 8 * at + 8]], axis=1)
        rest = jnp.concatenate([cols_ref[16 * at : 16 * at + 16], main], axis=1)
        return jnp.concatenate([top, rest], axis=0)

    inside = ((row >= 8) | (r > 0)) & ((lane >= 128) | (c > 0))
    start = jnp.where(inside, window(cot_ref[...], 0), 0.0)
    bottom = window(bottom_ref[...].astype(F32), 1)
    shifted = (4.2 + bottom / 25.0) - CENTRE

    def apply_shifted(v):
        below = jnp.where(row == 23, 0.0, pltpu.roll(v, 23, 0))
        right = jnp.where(lane == 383, 0.0, pltpu.roll(v, 383, 1))
        beside = below + pltpu.roll(v, 1, 0) + right + pltpu.roll(v, 1, 1)
        return jnp.where(inside, shifted * v - beside, 0.0)

    vectors = [start]
    images = []
    for step in range(KRYLOV):
        moved = apply_shifted(vectors[-1])
        images.append(moved + CENTRE * vectors[-1])
        if step == 0:
            vectors.append(moved * 0.25)
        elif step + 1 < KRYLOV:
            vectors.append(moved * 0.5 - vectors[-2])

    for k, v in enumerate(vectors):
        own_ref[24 * k : 24 * k + 24] = v
        near = pltpu.roll(v[0:16], 12, 0)[0:8]
        up_ref[8 * k : 8 * k + 8] = near[:, 128:384]
        up_ref[32 + 8 * (k // 2) : 40 + 8 * (k // 2), 128 * (k % 2) : 128 * (k % 2) + 128] = near[:, 0:128]
        beside = pltpu.roll(v[:, 0:256], 192, 1)[:, 0:128]
        for n in range(3):
            at = 3 * k + n
            left_ref[at // 2, 8 * (at % 2) : 8 * (at % 2) + 8] = beside[8 * n : 8 * n + 8]
        diag_ref[8 * k : 8 * k + 8] = pltpu.roll(near[:, 0:256], 192, 1)[:, 0:128]
    for out in (up_out, left_out, diag_out, own_out):
        out.send()

    domain = (
        (row >= 4)
        & (row < jnp.where(r == 15, 24, 20))
        & (lane >= 124)
        & (lane < jnp.where(c == 15, 384, 380))
    )
    cut = [jnp.where(domain, v, 0.0) for v in vectors]
    cut_parts = [halves(v) for v in cut]
    image_parts = [halves(w) for w in images]

    def tile(x, at):
        i, j = divmod(at, 3)
        return x[8 * i : 8 * i + 8, 128 * j : 128 * j + 128]

    def dot(x, x_parts, y, y_parts):
        total = None
        for at in range(9):
            p, e = two_prod(
                tile(x, at),
                tile(y, at),
                [tile(h, at) for h in x_parts],
                [tile(h, at) for h in y_parts],
            )
            if total is None:
                total = (p, e)
            else:
                s, f = two_sum(total[0], p)
                total = (s, total[1] + (e + f))
        return total

    dots = [dot(cut[i], cut_parts[i], images[j], image_parts[j]) for i, j in PAIRS]
    start_parts = halves(start)
    dots += [dot(cut[i], cut_parts[i], start, start_parts) for i in range(KRYLOV)]
    zero = jnp.zeros((8, 128), F32)
    dots += [(zero, zero)] * (16 - len(dots))
    packed = []
    for base in (0, 8):
        group = dots[base : base + 8]
        for step in (4, 2, 1):
            group = [merge_rows(group[i], group[i + step], step) for i in range(step)]
        total = group[0]
        for step in (64, 32, 16, 8, 4, 2, 1):
            total = df_add(total, (pltpu.roll(total[0], step, 1), pltpu.roll(total[1], step, 1)))
        packed.append(total)
    small_row = iota((8, 128), 0)
    small_lane = iota((8, 128), 1)
    spread = zero
    for part in (0, 1):
        for base in (0, 1):
            chosen = jnp.zeros((8, 128), jnp.bool_)
            for i in range(KRYLOV):
                for j in range(KRYLOV + 1):
                    index = len(PAIRS) + i if j == KRYLOV else PAIRS.index((min(i, j), max(i, j)))
                    if index // 8 == base:
                        chosen = chosen | (
                            (small_row == index % 8) & (small_lane == 32 * part + 8 * i + j)
                        )
            spread = spread + jnp.where(chosen, packed[base][part], 0.0)
    line = jnp.sum(spread, axis=0, keepdims=True)
    sums_ref[...] = jnp.broadcast_to(line, (256, 128))

    sums_out.send()


ROW_TURNS = (0, 4, 2, 6)
FIELDS = 6


def packed_rows(parts, from_above):
    row = iota((8, 256), 0)
    order = (2, 1, 3, 0) if from_above else (0, 2, 1, 3)
    turned = [pltpu.roll(p, t, 0) if t else p for p, t in zip(parts, ROW_TURNS)]
    out = turned[order[3]]
    for n in (2, 1, 0):
        out = jnp.where(row < 2 * n + 2, turned[order[n]], out)
    return out


def packed_cols(parts):
    group = (iota((16, 128), 1) + 2) & 127
    out = pltpu.roll(parts[-1], 4 * (len(parts) - 1), 1)
    for f in range(len(parts) - 2, -1, -1):
        out = jnp.where(group < 4 * f + 4, pltpu.roll(parts[f], 4 * f, 1) if f else parts[f], out)
    return out


def columns_kernel(ins, outs):
    depth = ins[0].ref.shape[0]
    land_in, kappa_in, bottom_in, tcot_in, scot_in, theta_in, salt_in, ux_in, uy_in = ins
    a_out, c_out, w_out, inv_out, ratio_out, down_out, up_out, right_out, left_out = outs
    a_ref, c_ref, w_ref, inv_ref, ratio_ref, down_ref, up_ref, right_ref, left_ref = [x.ref for x in outs]
    bottom = bottom_in.get()[...]
    land_ref = land_in.get()
    kappa_ref = kappa_in.get()
    tcot_ref = tcot_in.get()
    scot_ref = scot_in.get()

    def wet_at(k):
        return jnp.where(k < bottom, land_ref[k].astype(F32), 0.0)

    wet = wet_at(0)
    ratio = None
    couple_last = None
    state = None
    for k in range(depth):
        diagonal = jnp.ones((16, 256), F32)
        if k > 0:
            diagonal = diagonal + couple_last - couple_last * ratio
        if k < depth - 1:
            wet_next = wet_at(k + 1)
            couple = kappa_ref[k] * wet * wet_next
            diagonal = diagonal + couple
        inverse = 1.0 / diagonal
        rhs = (tcot_ref[k], scot_ref[k], wet)
        if k == 0:
            state = tuple(x * inverse for x in rhs)
        else:
            state = tuple((x + couple_last * s) * inverse for x, s in zip(rhs, state))
        a_ref[k], c_ref[k], w_ref[k] = state
        inv_ref[k] = inverse
        if k < depth - 1:
            ratio = couple * inverse
            ratio_ref[k] = ratio
            couple_last = couple
            wet = wet_next
    inv_out.send()
    ratio_out.send()
    theta_ref = theta_in.get()
    salt_ref = salt_in.get()
    ux_ref = ux_in.get()
    uy_ref = uy_in.get()
    row8 = iota((8, 256), 0)
    lane = iota((16, 128), 1)
    tails = {}
    for k in range(depth - 1, -1, -1):
        wet = wet_at(k)
        if k < depth - 1:
            ratio = ratio_ref[k]
            state = tuple(x + ratio * s for x, s in zip((a_ref[k], c_ref[k], w_ref[k]), state))
            a_ref[k], c_ref[k], w_ref[k] = state
        fields = (theta_ref[k] * wet, salt_ref[k] * wet) + state
        down_ref[8 * k : 8 * k + 8] = packed_rows([f[8:16] for f in fields[:4]], True)
        up_ref[8 * k : 8 * k + 8] = packed_rows([f[0:8] for f in fields[:4]], False)
        flow = ux_ref[k] * wet
        open_low = flow[8:16] * pltpu.roll(wet[8:16], 7, 0)
        open_high = flow[0:8] * pltpu.roll(wet[0:8], 7, 0)
        face_low = jnp.where(row8 == 6, open_low, flow[8:16])
        face_high = jnp.where(row8 == 0, open_high, pltpu.roll(wet[0:8], 1, 0))
        tails[k] = ((state[2][8:16], face_low), (state[2][0:8], face_high))
        if k % 2 == 0:
            later = tails.pop(k + 1, tails[k])
            this = tails.pop(k)
            at = 8 * depth + 4 * k
            down_ref[at : at + 8] = packed_rows(this[0] + later[0], True)
            up_ref[at : at + 8] = packed_rows(this[1] + later[1], False)
        flow = uy_ref[k] * wet
        open_last = flow[:, 128:256] * pltpu.roll(wet[:, 128:256], 127, 1)
        open_first = flow[:, 0:128] * pltpu.roll(wet[:, 0:128], 127, 1)
        last = [f[:, 128:256] for f in fields] + [jnp.where(lane == 126, open_last, flow[:, 128:256])]
        first = [f[:, 0:128] for f in fields] + [
            jnp.where(lane == 0, open_first, pltpu.roll(wet[:, 0:128], 1, 1))
        ]
        right_ref[k] = packed_cols(last)
        left_ref[k] = packed_cols(first)
    for out in (down_out, right_out, up_out, left_out, a_out, c_out, w_out):
        out.send()


def final_kernel(ins, outs, place_ref, theta_sweep_ref, salt_sweep_ref, x_open_ref, y_open_ref):
    (
        sums_in,
        own_in,
        corner_in,
        land_in,
        bottom_in,
        above_in,
        below_in,
        west_in,
        east_in,
        ux_in,
        uy_in,
        theta_in,
        salt_in,
        forcing_in,
        kappa_in,
        inv_in,
        ratio_in,
        w_in,
        a_in,
        c_in,
    ) = ins
    theta_out, salt_out, kappa_out, forcing_out = outs
    theta_grad_ref, salt_grad_ref, kappa_grad_ref, forcing_grad_ref = [x.ref for x in outs]
    depth = theta_in.ref.shape[0]
    lines = 8 * depth + 8 * ((depth + 1) // 2)
    r = place_ref[0]
    c = place_ref[1]
    has_up = jnp.where(r > 0, 1.0, 0.0)
    has_down = jnp.where(r < 15, 1.0, 0.0)
    has_left = jnp.where(c > 0, 1.0, 0.0)
    has_right = jnp.where(c < 15, 1.0, 0.0)
    row8 = iota((8, 256), 0)
    lane16 = iota((16, 128), 1)
    bottom = bottom_in.get()[...]
    land_ref = land_in.get()
    sums_ref, own_ref, from_corner_ref, above_ref, below_ref, west_ref, east_ref = [
        x.get() for x in (sums_in, own_in, corner_in, above_in, below_in, west_in, east_in)
    ]
    from_right_ref = [east_ref[depth + n] for n in range(6)]

    def near_of(k):
        at = lines + 8 * k
        side = lines + 32 + 8 * (k // 2)
        start = 128 * (k % 2)
        return jnp.concatenate([below_ref[side : side + 8, start : start + 128], below_ref[at : at + 8]], axis=1)

    from_right = jnp.concatenate(from_right_ref, axis=0)

    small = (8, 128)
    small_row = iota(small, 0)
    total = (sums_ref[0:8], jnp.zeros(small, F32))
    for at in range(1, 32):
        s, e = two_sum(total[0], sums_ref[8 * at : 8 * at + 8])
        total = (s, total[1] + e)
    for step in (4, 2, 1):
        s, e = two_sum(total[0], pltpu.roll(total[0], step, 0))
        total = (s, (total[1] + pltpu.roll(total[1], step, 0)) + e)
    low = total[1] + pltpu.roll(total[0] + total[1], 96, 1)
    total = quick_two_sum(total[0], low)

    def as_rows(x):
        out = x
        for i in range(1, KRYLOV):
            out = jnp.where(small_row == i, pltpu.roll(x, 128 - 8 * i, 1), out)
        return out

    system = (as_rows(total[0]), as_rows(total[1]))

    def row_of(x, k):
        return jnp.broadcast_to(x[k : k + 1, :], small)

    def lane_of(x, k):
        return jnp.broadcast_to(x[:, k : k + 1], small)

    keep = []
    weights = []
    scales = [lane_of(row_of(system[0], k), k) for k in range(KRYLOV)]
    for k in range(KRYLOV):
        across = (row_of(system[0], k), row_of(system[1], k))
        pivot = (lane_of(across[0], k), lane_of(across[1], k))
        fine = pivot[0] > 1e-13 * scales[k]
        keep.append(fine)
        pivot = (jnp.where(fine, pivot[0], 1.0), jnp.where(fine, pivot[1], 0.0))
        factor = df_div((lane_of(system[0], k), lane_of(system[1], k)), pivot)
        used = fine & (small_row != k)
        factor = (jnp.where(used, factor[0], 0.0), jnp.where(used, factor[1], 0.0))
        product = df_mul(factor, across)
        system = df_add(system, (-product[0], -product[1]))
    for k in range(KRYLOV):
        pivot = lane_of(row_of(system[0], k), k)
        value = lane_of(row_of(system[0], k), KRYLOV)
        value = jnp.where(keep[k], value / jnp.where(keep[k], pivot, 1.0), 0.0)
        weights.append(value[0:1, 0:1])

    def combined(ref, rows):
        out = weights[0] * ref[0:rows]
        for k in range(1, KRYLOV):
            out = out + weights[k] * ref[rows * k : rows * k + rows]
        return out

    def rows_joined(upper, lower):
        turned = pltpu.roll(lower, 4, 0)
        row8 = iota(turned.shape, 0)
        middle = jnp.where((row8 >= 5) & (r < 15), turned, upper[16:24])
        return jnp.concatenate([upper[0:16], middle, turned * has_down], axis=0)

    near = weights[0] * near_of(0)
    for k in range(1, KRYLOV):
        near = near + weights[k] * near_of(k)
    joined = rows_joined(combined(own_ref, 24), near)
    beside = pltpu.roll(rows_joined(combined(from_right, 24), combined(from_corner_ref, 8)), 64, 1)
    lane_wide = iota((32, 128), 1)
    ending = jnp.where((lane_wide >= 125) & (c < 15), beside, joined[:, 256:384])
    surface = jnp.concatenate([joined[:, 128:256], ending], axis=1)
    zeta = surface[8:24]

    zeta_rows = jnp.where(row8 < 4, surface[24:32], surface[0:8])
    zeta_cols = jnp.where(lane16 < 64, beside[8:24], joined[8:24, 0:128])

    def wet_at(k):
        return jnp.where(k < bottom, land_ref[k].astype(F32), 0.0)

    above_rows = (row8 & 2) != 0
    row_flag = jnp.where(above_rows, has_up, has_down)
    row_flag_turned = jnp.where(above_rows, has_down, has_up)
    west_lanes = (lane16 & 2) != 0
    lane_flag = jnp.where(west_lanes, has_left, has_right)

    def row_pair(at, second):
        above = above_ref[at : at + 8]
        below = below_ref[at : at + 8]
        if second:
            return jnp.where(above_rows, below, above) * row_flag_turned
        return jnp.where(above_rows, above, below) * row_flag

    def turned_rows(pair, f):
        turn = (8 - ROW_TURNS[f]) % 8
        return pltpu.roll(pair, turn, 0) if turn else pair

    def tail_pair(k):
        return row_pair(8 * depth + 8 * (k // 2), k % 2 == 1)

    def tail_rows(k, f):
        return turned_rows(tail_pair(k), f + 2 * (k % 2))

    def col_pair(k):
        return jnp.where(west_lanes, west_ref[k], east_ref[k]) * lane_flag

    def turned_cols(pair, f):
        return pltpu.roll(pair, 128 - 4 * f, 1) if f else pair

    def next_of(x, axis):
        return pltpu.roll(x, x.shape[axis] - 1, axis)

    def last_of(x, axis):
        return pltpu.roll(x, 1, axis)

    def main_of(x):
        return x[0:16, 0:256]

    def spread_of(q, edge, faces, axis):
        wide = jnp.concatenate([q, edge], axis=axis)
        pair = wide + next_of(wide, axis)
        flux = faces * (8.0 * pair - last_of(pair, axis) - next_of(pair, axis))
        return main_of(flux - last_of(flux, axis))

    def gathered(m, edge, faces, axis):
        wide = jnp.concatenate([m, edge], axis=axis)
        h = faces * (wide - next_of(wide, axis))
        pair = h + last_of(h, axis)
        return main_of(8.0 * pair - last_of(pair, axis) - next_of(pair, axis))

    scale = 1.0 / 12.0
    ux_ref, uy_ref, theta_ref, salt_ref, forcing_ref, kappa_ref, inv_ref = [
        x.get() for x in (ux_in, uy_in, theta_in, salt_in, forcing_in, kappa_in, inv_in)
    ]
    couple_last = None
    state = None
    wet = wet_at(0)
    for k in range(depth):
        faces = tail_rows(k, 1)
        wide = jnp.concatenate([wet, pltpu.roll(faces, 7, 0)], axis=0)
        later = next_of(wide, 0)
        x_open = jnp.concatenate(
            [ux_ref[k] * wet * later[0:16], jnp.where(row8 == 7, faces * later[16:24], faces)], axis=0
        )
        x_open = x_open * scale
        columns = col_pair(k)
        faces = turned_cols(columns, 5)
        wide = jnp.concatenate([wet, pltpu.roll(faces, 127, 1)], axis=1)
        later = next_of(wide, 1)
        y_open = jnp.concatenate(
            [uy_ref[k] * wet * later[:, 0:256], jnp.where(lane16 == 127, faces * later[:, 256:384], faces)], axis=1
        )
        y_open = y_open * scale
        x_open_ref[k] = x_open
        y_open_ref[k] = y_open
        rows = row_pair(8 * k, False)
        advected = []
        for f, ref in ((0, theta_ref), (1, salt_ref)):
            q = ref[k]
            masked = q * wet
            along_rows = spread_of(masked, turned_rows(rows, f), x_open, 0)
            along_cols = spread_of(masked, turned_cols(columns, f), y_open, 1)
            advected.append(q - along_rows - along_cols)
        if k == 0:
            advected[0] = advected[0] + forcing_ref[...] * wet
        inverse = inv_ref[k]
        if k == 0:
            state = tuple(x * inverse for x in advected)
        else:
            state = tuple((x + couple_last * s) * inverse for x, s in zip(advected, state))
        theta_sweep_ref[k], salt_sweep_ref[k] = state
        if k < depth - 1:
            wet_next = wet_at(k + 1)
            couple_last = kappa_ref[k] * wet * wet_next
            wet = wet_next

    ratio_ref, w_ref, a_ref, c_ref = [x.get() for x in (ratio_in, w_in, a_in, c_in)]
    share = (0.2, -0.15)
    mu_later = None
    wet_later = None
    for k in range(depth - 1, -1, -1):
        wet = wet_at(k)
        rise = zeta * w_ref[k]
        mu = (a_ref[k] + share[0] * rise, c_ref[k] + share[1] * rise)
        if k < depth - 1:
            ratio = ratio_ref[k]
            new = (theta_sweep_ref[k] + ratio * state[0], salt_sweep_ref[k] + ratio * state[1])
            kappa_grad_ref[k] = -(wet * wet_later) * (
                (mu[0] - mu_later[0]) * (new[0] - state[0]) + (mu[1] - mu_later[1]) * (new[1] - state[1])
            )
            state = new
        rows = row_pair(8 * k, True)
        columns = col_pair(k)
        row_rise = zeta_rows * tail_rows(k, 0)
        col_rise = zeta_cols * turned_cols(columns, 4)
        x_open = x_open_ref[k]
        y_open = y_open_ref[k]
        for n, ref in ((0, theta_grad_ref), (1, salt_grad_ref)):
            row_edge = turned_rows(rows, 2 + n) + share[n] * row_rise
            col_edge = turned_cols(columns, 2 + n) + share[n] * col_rise
            total = gathered(mu[n], row_edge, x_open, 0) + gathered(mu[n], col_edge, y_open, 1)
            ref[k] = mu[n] - wet * total
        if k == 0:
            forcing_grad_ref[...] = zeta + wet * mu[0]
        mu_later = mu
        wet_later = wet
        if k % 5 == 0:
            theta_out.send(k, 5)
            salt_out.send(k, 5)
            kappa_out.send(k, min(5, depth - 1 - k))
    forcing_out.send()


def around(count, step):
    return [(i, (i + step) % count) for i in range(count)]


def across(step):
    return [
        (16 * i + j, 16 * ((i + step) % 16) + (j + step) % 16) for i in range(16) for j in range(16)
    ]


def shards(
    theta,
    salt,
    velocity_x,
    velocity_y,
    land_mask,
    kappa,
    forcing,
    bottom,
    theta_cot,
    salt_cot,
    surface_cot,
):
    depth = theta.shape[0]
    whole = theta.shape
    place = jnp.stack([lax.axis_index(TROW), lax.axis_index(TCOL)]).astype(jnp.int32)
    rows, cols, corner = staged(edges_kernel, (surface_cot, bottom), [(16, 256), (32, 128), (16, 128)])
    rows = lax.ppermute(rows, TROW, around(16, 1))
    cols = lax.ppermute(cols, TCOL, around(16, 1))
    corner = lax.ppermute(corner, ALL, across(1))
    lines = 8 * depth + 8 * ((depth + 1) // 2)
    columns = (depth, 16, 128)
    extra_lines, extra_cols = 48, 6
    a, c, w, inv, ratio, down, up, right, left = staged(
        columns_kernel,
        (land_mask, kappa, bottom, theta_cot, salt_cot, theta, salt, velocity_x, velocity_y),
        [whole] * 4 + [kappa.shape, (lines, 256), (lines + extra_lines, 256), columns, (depth + extra_cols, 16, 128)],
        views={6: (0, lines), 8: (0, depth)},
    )
    above = lax.ppermute(down, TROW, around(16, 1))
    west = lax.ppermute(right, TCOL, around(16, 1))
    up, left, sums, own, tip = staged(
        krylov_kernel,
        (surface_cot, bottom, rows, cols, corner, up, left),
        [up.shape, left.shape, (256, 128), (96, 384), (32, 128)],
        place=place,
        aliases={5: 0, 6: 1},
        views={0: (lines, extra_lines), 1: (depth, extra_cols)},
    )
    below = lax.ppermute(up, TROW, around(16, -1))
    east = lax.ppermute(left, TCOL, around(16, -1))
    tip = lax.ppermute(tip, ALL, across(-1))
    sums = lax.all_to_all(sums, ALL, 0, 0, tiled=True)
    return tuple(
        staged(
            final_kernel,
            (sums, own, tip, land_mask, bottom, above, below, west, east, velocity_x, velocity_y, theta, salt)
            + (forcing, kappa, inv, ratio, w, a, c),
            [whole, whole, kappa.shape, forcing.shape],
            place=place,
            scratch=[whole, whole, (depth, 24, 256), (depth, 16, 384)],
            sends=16,
        )
    )


def solution(mesh):
    split = Mesh(mesh.devices.reshape(4, 2, 2, 2, 8), ALL)
    block = P(None, TROW, TCOL)
    flat = P(TROW, TCOL)
    return jax.shard_map(
        shards,
        mesh=split,
        in_specs=(block,) * 6 + (flat, flat, block, block, flat),
        out_specs=(block, block, block, flat),
        check_vma=False,
    )
```

```python
import math

import jax
import jax.numpy as jnp
import numpy as np
from jax import lax
from jax.experimental import pallas as pl
from jax.experimental.pallas import tpu as pltpu
from jax.sharding import Mesh
from jax.sharding import PartitionSpec as P

TROW = ("trow_0", "trow_1", "trow_2")
TCOL = ("tcol_0", "tcol_1")
ALL = TROW + TCOL
CENTRE = 4.75
KRYLOV = 4
PAIRS = [(i, j) for i in range(KRYLOV) for j in range(i, KRYLOV)]
F32 = jnp.float32
VM = pl.BlockSpec(memory_space=pltpu.VMEM)
SM = pl.BlockSpec(memory_space=pltpu.SMEM)
HB = pl.BlockSpec(memory_space=pltpu.HBM)
PARAMS = pltpu.CompilerParams(vmem_limit_bytes=58 * 1024 * 1024)


def iota(shape, dim):
    return lax.broadcasted_iota(jnp.int32, shape, dim)


def two_sum(a, b):
    s = a + b
    t = s - a
    return s, (a - (s - t)) + (b - t)


def quick_two_sum(a, b):
    s = a + b
    return s, b - (s - a)


def halves(a):
    t = a * 4097.0
    high = t - (t - a)
    return high, a - high


def two_prod(a, b, a_parts, b_parts):
    p = a * b
    ah, al = a_parts
    bh, bl = b_parts
    return p, ((ah * bh - p) + ah * bl + al * bh) + al * bl


def df_add(a, b):
    s, e = two_sum(a[0], b[0])
    return quick_two_sum(s, e + (a[1] + b[1]))


def df_mul(a, b):
    p, e = two_prod(a[0], b[0], halves(a[0]), halves(b[0]))
    return quick_two_sum(p, e + (a[0] * b[1] + a[1] * b[0]))


def df_div(a, b):
    inverse = 1.0 / b[0]
    q1 = a[0] * inverse
    back = df_mul((q1, jnp.zeros_like(q1)), b)
    rest = df_add(a, (-back[0], -back[1]))
    return quick_two_sum(q1, rest[0] * inverse)


class Loaded:
    def __init__(self, source, ref, sem):
        self.ref = ref
        self.copy = pltpu.make_async_copy(source, ref, sem)
        self.copy.start()
        self.waited = False

    def get(self):
        if not self.waited:
            self.copy.wait()
            self.waited = True
        return self.ref


class Stored:
    def __init__(self, target, ref, take_sem, pending):
        self.target, self.ref, self.take_sem, self.pending = target, ref, take_sem, pending

    def send(self, start=None, count=None):
        source, target = self.ref, self.target
        if start is not None:
            source, target = source.at[pl.ds(start, count)], target.at[pl.ds(start, count)]
        copy = pltpu.make_async_copy(source, target, self.take_sem())
        copy.start()
        self.pending.append(copy)


def staged(kernel, args, outs, place=None, scratch=(), sends=None, after=(), flops=0):
    smem = [] if place is None else [place]
    cuts = [a[1:] if isinstance(a, tuple) else None for a in args]
    args = [a[0] if isinstance(a, tuple) else a for a in args]
    n_in, n_out = len(args), len(outs)
    sends = sends or n_out
    staging = [pltpu.VMEM(a.shape if cut is None else (cut[1],) + a.shape[1:], a.dtype) for a, cut in zip(args, cuts)]
    staging += [pltpu.VMEM(s, F32) for s in outs]

    def body(*refs):
        refs = list(refs)
        places = [refs.pop(0) for _ in smem]
        sources = [refs.pop(0) for _ in range(n_in)]
        sources = [s if cut is None else s.at[pl.ds(*cut)] for s, cut in zip(sources, cuts)]
        for _ in after:
            refs.pop(0)
        targets = [refs.pop(0) for _ in range(n_out)]
        buffers = [refs.pop(0) for _ in range(n_in)]
        holds = [refs.pop(0) for _ in range(n_out)]
        in_sems, out_sems = refs.pop(-2), refs.pop(-1)
        ins = [Loaded(s, b, in_sems.at[n]) for n, (s, b) in enumerate(zip(sources, buffers))]
        pending = []
        given = []
        for n in range(n_out):
            given.append(Stored(targets[n], holds[n], lambda: out_sems.at[len(pending)], pending))
        kernel(ins, given, *places, *refs)
        for x in ins:
            x.get()
        for copy in pending:
            copy.wait()

    return pl.pallas_call(
        body,
        out_shape=[jax.ShapeDtypeStruct(s, F32) for s in outs],
        in_specs=[SM] * len(smem) + [HB] * (n_in + len(after)),
        out_specs=[HB] * n_out,
        scratch_shapes=staging
        + [pltpu.VMEM(s, t) for s, t in scratch]
        + [pltpu.SemaphoreType.DMA((n_in,)), pltpu.SemaphoreType.DMA((sends,))],
        cost_estimate=pl.CostEstimate(
            flops=flops, bytes_accessed=4 * (sum(a.size for a in args) + sum(map(math.prod, outs))), transcendentals=0
        ),
        compiler_params=PARAMS,
    )(*smem, *args, *after)


def merge_rows(a, b, step):
    shape = a[0].shape
    first = (iota(shape, 0) & step) == 0

    def part(x, y):
        mixed = jnp.where(first, y, x)
        if step == 4:
            other = pltpu.roll(mixed, 4, 0)
        else:
            other = jnp.where(first, pltpu.roll(mixed, 8 - step, 0), pltpu.roll(mixed, step, 0))
        return jnp.where(first, x, y), other

    kept_high, other_high = part(a[0], b[0])
    kept_low, other_low = part(a[1], b[1])
    return df_add((kept_high, kept_low), (other_high, other_low))


def krylov_kernel(ins, outs, place_ref):
    cot_ref, bottom_ref, rows_ref, cols_ref, corner_ref = [x.get() for x in ins]
    up_out, left_out, own_out, diag_out = outs
    own_ref, up_ref, left_ref, diag_ref = [x.ref for x in (own_out, up_out, left_out, diag_out)]
    r = place_ref[0]
    c = place_ref[1]
    shape = (24, 384)
    row = iota(shape, 0)
    lane = iota(shape, 1)

    def window(main, at):
        top = jnp.concatenate([corner_ref[8 * at : 8 * at + 8], rows_ref[8 * at : 8 * at + 8]], axis=1)
        rest = jnp.concatenate([cols_ref[at], main], axis=1)
        return jnp.concatenate([top, rest], axis=0)

    inside = ((row >= 8) | (r > 0)) & ((lane >= 128) | (c > 0))
    start = jnp.where(inside, window(cot_ref[...], 0), 0.0)
    bottom = window(bottom_ref[...].astype(F32), 1)
    shifted = (4.2 + bottom / 25.0) - CENTRE

    def apply_shifted(v):
        below = jnp.where(row == 23, 0.0, pltpu.roll(v, 23, 0))
        right = jnp.where(lane == 383, 0.0, pltpu.roll(v, 383, 1))
        beside = below + pltpu.roll(v, 1, 0) + right + pltpu.roll(v, 1, 1)
        return jnp.where(inside, shifted * v - beside, 0.0)

    vectors = [start]
    images = []
    for step in range(KRYLOV):
        moved = apply_shifted(vectors[-1])
        images.append(moved + CENTRE * vectors[-1])
        if step == 0:
            vectors.append(moved * 0.25)
        elif step + 1 < KRYLOV:
            vectors.append(moved * 0.5 - vectors[-2])

    for k, v in enumerate(vectors):
        own_ref[24 * k : 24 * k + 24] = v
        own_ref[24 * (KRYLOV + k) : 24 * (KRYLOV + k) + 24] = images[k]
        near = pltpu.roll(v[0:16], 12, 0)[0:8]
        up_ref[8 * k : 8 * k + 8] = near
        left_ref[24 * k : 24 * k + 24] = pltpu.roll(v[:, 0:256], 192, 1)[:, 0:128]
        diag_ref[8 * k : 8 * k + 8] = pltpu.roll(near[:, 0:256], 192, 1)[:, 0:128]
    for out in (up_out, left_out, diag_out, own_out):
        out.send()


def products_kernel(ins, outs, place_ref):
    own_ref = ins[0].get()
    sums_out = outs[0]
    sums_ref = sums_out.ref
    r = place_ref[0]
    c = place_ref[1]
    shape = (24, 384)
    row = iota(shape, 0)
    lane = iota(shape, 1)
    vectors = [own_ref[24 * k : 24 * k + 24] for k in range(KRYLOV)]
    images = [own_ref[24 * k : 24 * k + 24] for k in range(KRYLOV, 2 * KRYLOV)]
    start = vectors[0]
    domain = (
        (row >= 4)
        & (row < jnp.where(r == 15, 24, 20))
        & (lane >= 124)
        & (lane < jnp.where(c == 15, 384, 380))
    )
    cut = [jnp.where(domain, v, 0.0) for v in vectors]
    cut_parts = [halves(v) for v in cut]
    image_parts = [halves(w) for w in images]

    def tile(x, at):
        i, j = divmod(at, 3)
        return x[8 * i : 8 * i + 8, 128 * j : 128 * j + 128]

    def dot(x, x_parts, y, y_parts):
        total = None
        for at in range(9):
            p, e = two_prod(
                tile(x, at),
                tile(y, at),
                [tile(h, at) for h in x_parts],
                [tile(h, at) for h in y_parts],
            )
            if total is None:
                total = (p, e)
            else:
                s, f = two_sum(total[0], p)
                total = (s, total[1] + (e + f))
        return total

    dots = [dot(cut[i], cut_parts[i], images[j], image_parts[j]) for i, j in PAIRS]
    start_parts = halves(start)
    dots += [dot(cut[i], cut_parts[i], start, start_parts) for i in range(KRYLOV)]
    zero = jnp.zeros((8, 128), F32)
    dots += [(zero, zero)] * (16 - len(dots))
    packed = []
    for base in (0, 8):
        group = dots[base : base + 8]
        for step in (4, 2, 1):
            group = [merge_rows(group[i], group[i + step], step) for i in range(step)]
        total = group[0]
        for step in (64, 32, 16, 8, 4, 2, 1):
            total = df_add(total, (pltpu.roll(total[0], step, 1), pltpu.roll(total[1], step, 1)))
        packed.append(total)
    small_row = iota((8, 128), 0)
    small_lane = iota((8, 128), 1)
    spread = zero
    for part in (0, 1):
        for base in (0, 1):
            chosen = jnp.zeros((8, 128), jnp.bool_)
            for i in range(KRYLOV):
                for j in range(KRYLOV + 1):
                    index = len(PAIRS) + i if j == KRYLOV else PAIRS.index((min(i, j), max(i, j)))
                    if index // 8 == base:
                        chosen = chosen | (
                            (small_row == index % 8) & (small_lane == 32 * part + 8 * i + j)
                        )
            spread = spread + jnp.where(chosen, packed[base][part], 0.0)
    line = jnp.sum(spread, axis=0, keepdims=True)
    sums_ref[...] = jnp.broadcast_to(line, (256, 128))

    sums_out.send()


ROW_TURNS = (0, 4, 2, 6)
FIELDS = 6


def packed_rows(parts, from_above):
    row = iota((8, 256), 0)
    order = (2, 1, 3, 0) if from_above else (0, 2, 1, 3)
    turned = [pltpu.roll(p, t, 0) if t else p for p, t in zip(parts, ROW_TURNS)]
    out = turned[order[3]]
    for n in (2, 1, 0):
        out = jnp.where(row < 2 * n + 2, turned[order[n]], out)
    return out


def packed_cols(parts):
    group = (iota((16, 128), 1) + 2) & 127
    out = pltpu.roll(parts[-1], 4 * (len(parts) - 1), 1)
    for f in range(len(parts) - 2, -1, -1):
        out = jnp.where(group < 4 * f + 4, pltpu.roll(parts[f], 4 * f, 1) if f else parts[f], out)
    return out


def columns_kernel(ins, outs):
    depth = ins[0].ref.shape[0]
    land_in, kappa_in, bottom_in, tcot_in, scot_in, theta_in, salt_in, ux_in, uy_in, surface_in = ins
    a_out, c_out, w_out, inv_out, ratio_out, down_out, up_out, right_out, left_out, corner_out = outs
    a_ref, c_ref, w_ref, inv_ref, ratio_ref, down_ref, up_ref, right_ref, left_ref, corner_ref = [x.ref for x in outs]
    bottom = bottom_in.get()[...]
    lines = 8 * depth + 8 * ((depth + 1) // 2)
    for n, field in enumerate((surface_in.get()[...], bottom.astype(F32))):
        down_ref[lines + 8 * n : lines + 8 * n + 8] = field[8:16]
        right_ref[depth + n] = field[:, 128:256]
        corner_ref[8 * n : 8 * n + 8] = field[8:16, 128:256]
    corner_out.send()
    land_ref = land_in.get()
    kappa_ref = kappa_in.get()
    tcot_ref = tcot_in.get()
    scot_ref = scot_in.get()

    def wet_at(k):
        return jnp.where(k < bottom, land_ref[k].astype(F32), 0.0)

    wet = wet_at(0)
    ratio = None
    couple_last = None
    state = None
    for k in range(depth):
        diagonal = jnp.ones((16, 256), F32)
        if k > 0:
            diagonal = diagonal + couple_last - couple_last * ratio
        if k < depth - 1:
            wet_next = wet_at(k + 1)
            couple = kappa_ref[k] * wet * wet_next
            diagonal = diagonal + couple
        inverse = 1.0 / diagonal
        rhs = (tcot_ref[k], scot_ref[k], wet)
        if k == 0:
            state = tuple(x * inverse for x in rhs)
        else:
            state = tuple((x + couple_last * s) * inverse for x, s in zip(rhs, state))
        a_ref[k], c_ref[k], w_ref[k] = state
        inv_ref[k] = inverse
        if k < depth - 1:
            ratio = couple * inverse
            ratio_ref[k] = ratio
            couple_last = couple
            wet = wet_next
    inv_out.send()
    ratio_out.send()
    theta_ref = theta_in.get()
    salt_ref = salt_in.get()
    ux_ref = ux_in.get()
    uy_ref = uy_in.get()
    row8 = iota((8, 256), 0)
    lane = iota((16, 128), 1)
    tails = {}
    for k in range(depth - 1, -1, -1):
        wet = wet_at(k)
        if k < depth - 1:
            ratio = ratio_ref[k]
            state = tuple(x + ratio * s for x, s in zip((a_ref[k], c_ref[k], w_ref[k]), state))
            a_ref[k], c_ref[k], w_ref[k] = state
        fields = (theta_ref[k] * wet, salt_ref[k] * wet) + state
        down_ref[8 * k : 8 * k + 8] = packed_rows([f[8:16] for f in fields[:4]], True)
        up_ref[8 * k : 8 * k + 8] = packed_rows([f[0:8] for f in fields[:4]], False)
        flow = ux_ref[k] * wet
        open_low = flow[8:16] * pltpu.roll(wet[8:16], 7, 0)
        open_high = flow[0:8] * pltpu.roll(wet[0:8], 7, 0)
        face_low = jnp.where(row8 == 6, open_low, flow[8:16])
        face_high = jnp.where(row8 == 0, open_high, pltpu.roll(wet[0:8], 1, 0))
        tails[k] = ((state[2][8:16], face_low), (state[2][0:8], face_high))
        if k % 2 == 0:
            later = tails.pop(k + 1, tails[k])
            this = tails.pop(k)
            at = 8 * depth + 4 * k
            down_ref[at : at + 8] = packed_rows(this[0] + later[0], True)
            up_ref[at : at + 8] = packed_rows(this[1] + later[1], False)
        flow = uy_ref[k] * wet
        open_last = flow[:, 128:256] * pltpu.roll(wet[:, 128:256], 127, 1)
        open_first = flow[:, 0:128] * pltpu.roll(wet[:, 0:128], 127, 1)
        last = [f[:, 128:256] for f in fields] + [jnp.where(lane == 126, open_last, flow[:, 128:256])]
        first = [f[:, 0:128] for f in fields] + [
            jnp.where(lane == 0, open_first, pltpu.roll(wet[:, 0:128], 1, 1))
        ]
        right_ref[k] = packed_cols(last)
        left_ref[k] = packed_cols(first)
    for out in (down_out, right_out, up_out, left_out, a_out, c_out, w_out):
        out.send()


SCALE = 1.0 / 12.0
BF16 = jnp.bfloat16


class Edges:
    def __init__(self, place_ref, depth, above, below, west, east):
        r = place_ref[0]
        c = place_ref[1]
        self.depth, self.above, self.below, self.west, self.east = depth, above, below, west, east
        self.row8 = iota((8, 256), 0)
        self.lane16 = iota((16, 128), 1)
        has_up = jnp.where(r > 0, 1.0, 0.0)
        has_down = jnp.where(r < 15, 1.0, 0.0)
        has_left = jnp.where(c > 0, 1.0, 0.0)
        has_right = jnp.where(c < 15, 1.0, 0.0)
        self.above_rows = (self.row8 & 2) != 0
        self.row_flags = (
            jnp.where(self.above_rows, has_up, has_down),
            jnp.where(self.above_rows, has_down, has_up),
        )
        self.west_lanes = (self.lane16 & 2) != 0
        self.lane_flag = jnp.where(self.west_lanes, has_left, has_right)

    def row_pair(self, at, second):
        above = self.above[at : at + 8]
        below = self.below[at : at + 8]
        if second:
            return jnp.where(self.above_rows, below, above) * self.row_flags[1]
        return jnp.where(self.above_rows, above, below) * self.row_flags[0]

    def turned_rows(self, pair, f):
        turn = (8 - ROW_TURNS[f]) % 8
        return pltpu.roll(pair, turn, 0) if turn else pair

    def tail_rows(self, k, f):
        pair = self.row_pair(8 * self.depth + 8 * (k // 2), k % 2 == 1)
        return self.turned_rows(pair, f + 2 * (k % 2))

    def col_pair(self, k):
        return jnp.where(self.west_lanes, self.west[k], self.east[k]) * self.lane_flag

    def turned_cols(self, pair, f):
        return pltpu.roll(pair, 128 - 4 * f, 1) if f else pair


def next_of(x, axis):
    return pltpu.roll(x, x.shape[axis] - 1, axis)


def last_of(x, axis):
    return pltpu.roll(x, 1, axis)


def two_parts(x):
    high = x.astype(BF16)
    return jnp.concatenate([high, (x - high.astype(F32)).astype(BF16)], axis=1)


def stencil(offsets, columns):
    out = np.zeros((384, columns), np.float32)
    for j in range(columns):
        for offset, value in offsets:
            out[(j + offset) % 384, j] += value
    return jnp.asarray(np.concatenate([out, out]), BF16)


def forward_kernel(ins, outs, place_ref, parts_ref, filtered_ref, theta_sweep_ref, salt_sweep_ref):
    (
        land_in,
        bottom_in,
        above_in,
        below_in,
        west_in,
        east_in,
        ux_in,
        uy_in,
        theta_in,
        salt_in,
        filter_in,
        forcing_in,
        kappa_in,
        inv_in,
        ratio_in,
    ) = ins
    x_out, y_out, theta_out, salt_out = outs
    x_open_ref, y_open_ref, theta_drop_ref, salt_drop_ref = [x.ref for x in outs]
    depth = theta_in.ref.shape[0]
    bottom = bottom_in.get()[...]
    land_ref = land_in.get()
    edges = Edges(place_ref, depth, *[x.get() for x in (above_in, below_in, west_in, east_in)])
    row8, lane16 = edges.row8, edges.lane16
    ux_ref, uy_ref, theta_ref, salt_ref = [x.get() for x in (ux_in, uy_in, theta_in, salt_in)]

    def wet_at(k):
        return jnp.where(k < bottom, land_ref[k].astype(F32), 0.0)

    for k in range(depth):
        wet = wet_at(k)
        faces = edges.tail_rows(k, 1)
        wide = jnp.concatenate([wet, pltpu.roll(faces, 7, 0)], axis=0)
        later = next_of(wide, 0)
        x_open = jnp.concatenate(
            [ux_ref[k] * wet * later[0:16], jnp.where(row8 == 7, faces * later[16:24], faces)], axis=0
        )
        x_open_ref[k] = x_open * SCALE
        columns = edges.col_pair(k)
        faces = edges.turned_cols(columns, 5)
        wide = jnp.concatenate([wet, pltpu.roll(faces, 127, 1)], axis=1)
        later = next_of(wide, 1)
        y_open = jnp.concatenate(
            [uy_ref[k] * wet * later[:, 0:256], jnp.where(lane16 == 127, faces * later[:, 256:384], faces)], axis=1
        )
        y_open_ref[k] = y_open * SCALE
        for f, ref in ((0, theta_ref), (1, salt_ref)):
            wide = jnp.concatenate([ref[k] * wet, edges.turned_cols(columns, f)], axis=1)
            at = 16 * (depth * f + k)
            parts_ref[at : at + 16] = two_parts(wide)
    x_out.send()
    y_out.send()
    filtered_ref[...] = jnp.dot(parts_ref[...], filter_in.get()[...], preferred_element_type=F32)
    forcing_ref, kappa_ref, inv_ref, ratio_ref = [x.get() for x in (forcing_in, kappa_in, inv_in, ratio_in)]

    couple_last = None
    state = None
    wet = wet_at(0)
    for k in range(depth):
        rows = edges.row_pair(8 * k, False)
        x_open = x_open_ref[k]
        y_open = y_open_ref[k]
        advected = []
        for f, ref in ((0, theta_ref), (1, salt_ref)):
            q = ref[k]
            wide = jnp.concatenate([q * wet, edges.turned_rows(rows, f)], axis=0)
            pair = wide + next_of(wide, 0)
            flux = x_open * (8.0 * pair - last_of(pair, 0) - next_of(pair, 0))
            change = (flux - last_of(flux, 0))[0:16]
            at = 16 * (depth * f + k)
            flux = y_open * filtered_ref[at : at + 16]
            change = change + (flux - last_of(flux, 1))[:, 0:256]
            advected.append(q - change)
        if k == 0:
            advected[0] = advected[0] + forcing_ref[...] * wet
        inverse = inv_ref[k]
        if k == 0:
            state = tuple(x * inverse for x in advected)
        else:
            state = tuple((x + couple_last * s) * inverse for x, s in zip(advected, state))
        theta_sweep_ref[k], salt_sweep_ref[k] = state
        if k < depth - 1:
            wet_next = wet_at(k + 1)
            couple_last = kappa_ref[k] * wet * wet_next
            wet = wet_next
    wet_later = wet
    for k in range(depth - 2, -1, -1):
        wet = wet_at(k)
        ratio = ratio_ref[k]
        new = (theta_sweep_ref[k] + ratio * state[0], salt_sweep_ref[k] + ratio * state[1])
        opened = wet * wet_later
        theta_drop_ref[k] = opened * (state[0] - new[0])
        salt_drop_ref[k] = opened * (state[1] - new[1])
        state = new
        wet_later = wet
    theta_out.send()
    salt_out.send()


def backward_kernel(ins, outs, place_ref, parts_ref, filtered_ref):
    (
        sums_in,
        own_in,
        near_in,
        side_in,
        corner_in,
        land_in,
        bottom_in,
        above_in,
        below_in,
        west_in,
        east_in,
        w_in,
        a_in,
        c_in,
        theta_drop_in,
        salt_drop_in,
        x_open_in,
        y_open_in,
        filter_in,
    ) = ins
    theta_out, salt_out, kappa_out, forcing_out = outs
    theta_grad_ref, salt_grad_ref, kappa_grad_ref, forcing_grad_ref = [x.ref for x in outs]
    depth = w_in.ref.shape[0]
    r = place_ref[0]
    c = place_ref[1]
    has_down = jnp.where(r < 15, 1.0, 0.0)
    sums_ref, own_ref, from_below_ref, from_right_ref, from_corner_ref = [
        x.get() for x in (sums_in, own_in, near_in, side_in, corner_in)
    ]

    small = (8, 128)
    small_row = iota(small, 0)
    total = (sums_ref[0:8], jnp.zeros(small, F32))
    for at in range(1, 32):
        s, e = two_sum(total[0], sums_ref[8 * at : 8 * at + 8])
        total = (s, total[1] + e)
    for step in (4, 2, 1):
        s, e = two_sum(total[0], pltpu.roll(total[0], step, 0))
        total = (s, (total[1] + pltpu.roll(total[1], step, 0)) + e)
    low = total[1] + pltpu.roll(total[0] + total[1], 96, 1)
    total = quick_two_sum(total[0], low)

    def as_rows(x):
        out = x
        for i in range(1, KRYLOV):
            out = jnp.where(small_row == i, pltpu.roll(x, 128 - 8 * i, 1), out)
        return out

    system = (as_rows(total[0]), as_rows(total[1]))

    def row_of(x, k):
        return jnp.broadcast_to(x[k : k + 1, :], small)

    def lane_of(x, k):
        return jnp.broadcast_to(x[:, k : k + 1], small)

    keep = []
    weights = []
    scales = [lane_of(row_of(system[0], k), k) for k in range(KRYLOV)]
    for k in range(KRYLOV):
        across = (row_of(system[0], k), row_of(system[1], k))
        pivot = (lane_of(across[0], k), lane_of(across[1], k))
        fine = pivot[0] > 1e-13 * scales[k]
        keep.append(fine)
        pivot = (jnp.where(fine, pivot[0], 1.0), jnp.where(fine, pivot[1], 0.0))
        factor = df_div((lane_of(system[0], k), lane_of(system[1], k)), pivot)
        used = fine & (small_row != k)
        factor = (jnp.where(used, factor[0], 0.0), jnp.where(used, factor[1], 0.0))
        product = df_mul(factor, across)
        system = df_add(system, (-product[0], -product[1]))
    for k in range(KRYLOV):
        pivot = lane_of(row_of(system[0], k), k)
        value = lane_of(row_of(system[0], k), KRYLOV)
        value = jnp.where(keep[k], value / jnp.where(keep[k], pivot, 1.0), 0.0)
        weights.append(value[0:1, 0:1])

    def combined(ref, rows):
        out = weights[0] * ref[0:rows]
        for k in range(1, KRYLOV):
            out = out + weights[k] * ref[rows * k : rows * k + rows]
        return out

    def rows_joined(upper, lower):
        turned = pltpu.roll(lower, 4, 0)
        row8 = iota(turned.shape, 0)
        middle = jnp.where((row8 >= 5) & (r < 15), turned, upper[16:24])
        return jnp.concatenate([upper[0:16], middle, turned * has_down], axis=0)

    joined = rows_joined(combined(own_ref, 24), combined(from_below_ref, 8))
    beside = pltpu.roll(rows_joined(combined(from_right_ref, 24), combined(from_corner_ref, 8)), 64, 1)
    lane_wide = iota((32, 128), 1)
    ending = jnp.where((lane_wide >= 125) & (c < 15), beside, joined[:, 256:384])
    surface = jnp.concatenate([joined[:, 128:256], ending], axis=1)
    zeta = surface[8:24]

    bottom = bottom_in.get()[...]
    land_ref = land_in.get()
    edges = Edges(place_ref, depth, *[x.get() for x in (above_in, below_in, west_in, east_in)])
    zeta_rows = jnp.where(edges.row8 < 4, surface[24:32], surface[0:8])
    zeta_cols = jnp.where(edges.lane16 < 64, beside[8:24], joined[8:24, 0:128])

    def wet_at(k):
        return jnp.where(k < bottom, land_ref[k].astype(F32), 0.0)

    w_ref, a_ref, c_ref, theta_drop_ref, salt_drop_ref, x_open_ref, y_open_ref = [
        x.get() for x in (w_in, a_in, c_in, theta_drop_in, salt_drop_in, x_open_in, y_open_in)
    ]
    share = (0.2, -0.15)
    mu_later = None
    for k in range(depth - 1, -1, -1):
        wet = wet_at(k)
        rise = zeta * w_ref[k]
        mu = (a_ref[k] + share[0] * rise, c_ref[k] + share[1] * rise)
        if k < depth - 1:
            kappa_grad_ref[k] = theta_drop_ref[k] * (mu[0] - mu_later[0]) + salt_drop_ref[k] * (mu[1] - mu_later[1])
        rows = edges.row_pair(8 * k, True)
        columns = edges.col_pair(k)
        row_rise = zeta_rows * edges.tail_rows(k, 0)
        col_rise = zeta_cols * edges.turned_cols(columns, 4)
        x_open = x_open_ref[k]
        y_open = y_open_ref[k]
        for n, ref in ((0, theta_grad_ref), (1, salt_grad_ref)):
            wide = jnp.concatenate([mu[n], edges.turned_cols(columns, 2 + n) + share[n] * col_rise], axis=1)
            at = 16 * (depth * n + k)
            parts_ref[at : at + 16] = two_parts(y_open * (wide - next_of(wide, 1)))
            wide = jnp.concatenate([mu[n], edges.turned_rows(rows, 2 + n) + share[n] * row_rise], axis=0)
            h = x_open * (wide - next_of(wide, 0))
            pair = h + last_of(h, 0)
            change = (8.0 * pair - last_of(pair, 0) - next_of(pair, 0))[0:16]
            ref[k] = mu[n] - wet * change
        if k == 0:
            forcing_grad_ref[...] = zeta + wet * mu[0]
        mu_later = mu
    kappa_out.send()
    forcing_out.send()
    filtered_ref[...] = jnp.dot(parts_ref[...], filter_in.get()[...], preferred_element_type=F32)
    for n, ref, out in ((0, theta_grad_ref, theta_out), (1, salt_grad_ref, salt_out)):
        for k in range(depth):
            at = 16 * (depth * n + k)
            ref[k] = ref[k] - wet_at(k) * filtered_ref[at : at + 16]
            if k % 5 == 4:
                out.send(k - 4, 5)


def around(count, step):
    return [(i, (i + step) % count) for i in range(count)]


def across(step):
    return [
        (16 * i + j, 16 * ((i + step) % 16) + (j + step) % 16) for i in range(16) for j in range(16)
    ]


def shards(
    theta,
    salt,
    velocity_x,
    velocity_y,
    land_mask,
    kappa,
    forcing,
    bottom,
    theta_cot,
    salt_cot,
    surface_cot,
):
    depth = theta.shape[0]
    whole = theta.shape
    place = jnp.stack([lax.axis_index(TROW), lax.axis_index(TCOL)]).astype(jnp.int32)
    lines = 8 * depth + 8 * ((depth + 1) // 2)
    columns = (depth, 16, 128)
    a, c, w, inv, ratio, down, up, right, left, corner = staged(
        columns_kernel,
        (land_mask, kappa, bottom, theta_cot, salt_cot, theta, salt, velocity_x, velocity_y, surface_cot),
        [whole] * 4
        + [kappa.shape, (lines + 16, 256), (lines, 256), (depth + 2, 16, 128), columns, (16, 128)],
        flops=100 * theta.size,
    )
    above = lax.ppermute(down, TROW, around(16, 1))
    west = lax.ppermute(right, TCOL, around(16, 1))
    corner = lax.ppermute(corner, ALL, across(1))
    below = lax.ppermute(up, TROW, around(16, -1))
    east = lax.ppermute(left, TCOL, around(16, -1))
    near, side, own, tip = staged(
        krylov_kernel,
        (surface_cot, bottom, (above, lines, 16), (west, depth, 2), corner),
        [(32, 384), (96, 128), (192, 384), (32, 128)],
        place=place,
    )
    near = lax.ppermute(near, TROW, around(16, -1))
    side = lax.ppermute(side, TCOL, around(16, -1))
    tip = lax.ppermute(tip, ALL, across(-1))
    x_open, y_open, theta_drop, salt_drop = staged(
        forward_kernel,
        (land_mask, bottom, above, below, west, east, velocity_x, velocity_y, theta, salt)
        + (stencil(((-1, -1), (0, 7), (1, 7), (2, -1)), 384), forcing, kappa, inv, ratio),
        [(depth, 24, 256), (depth, 16, 384), kappa.shape, kappa.shape],
        place=place,
        after=(own,),
        flops=200 * theta.size,
        scratch=[((32 * depth, 768), BF16), ((32 * depth, 384), F32), (whole, F32), (whole, F32)],
    )
    (sums,) = staged(products_kernel, (own,), [(256, 128)], place=place, after=(theta_drop, near, side, tip))
    sums = lax.all_to_all(sums, ALL, 0, 0, tiled=True)
    return tuple(
        staged(
            backward_kernel,
            (sums, own, near, side, tip, land_mask, bottom, above, below, west, east, w, a, c)
            + (theta_drop, salt_drop, x_open, y_open, stencil(((-2, -1), (-1, 7), (0, 7), (1, -1)), 256)),
            [whole, whole, kappa.shape, forcing.shape],
            place=place,
            scratch=[((32 * depth, 768), BF16), ((32 * depth, 256), F32)],
            sends=12,
        )
    )


def solution(mesh):
    split = Mesh(mesh.devices.reshape(4, 2, 2, 2, 8), ALL)
    block = P(None, TROW, TCOL)
    flat = P(TROW, TCOL)
    return jax.shard_map(
        shards,
        mesh=split,
        in_specs=(block,) * 6 + (flat, flat, block, block, flat),
        out_specs=(block, block, block, flat),
        check_vma=False,
    )
```

```python
import math

import jax
import jax.numpy as jnp
import numpy as np
from jax import lax
from jax.experimental import pallas as pl
from jax.experimental.pallas import tpu as pltpu
from jax.sharding import Mesh
from jax.sharding import PartitionSpec as P

TROW = ("trow_0", "trow_1", "trow_2")
TCOL = ("tcol_0", "tcol_1")
ALL = TROW + TCOL
CENTRE = 4.75
KRYLOV = 4
PAIRS = [(i, j) for i in range(KRYLOV) for j in range(i, KRYLOV)]
F32 = jnp.float32
VM = pl.BlockSpec(memory_space=pltpu.VMEM)
SM = pl.BlockSpec(memory_space=pltpu.SMEM)
HB = pl.BlockSpec(memory_space=pltpu.HBM)
PARAMS = pltpu.CompilerParams(vmem_limit_bytes=58 * 1024 * 1024)


def iota(shape, dim):
    return lax.broadcasted_iota(jnp.int32, shape, dim)


def two_sum(a, b):
    s = a + b
    t = s - a
    return s, (a - (s - t)) + (b - t)


def quick_two_sum(a, b):
    s = a + b
    return s, b - (s - a)


def halves(a):
    t = a * 4097.0
    high = t - (t - a)
    return high, a - high


def two_prod(a, b, a_parts, b_parts):
    p = a * b
    ah, al = a_parts
    bh, bl = b_parts
    return p, ((ah * bh - p) + ah * bl + al * bh) + al * bl


def df_add(a, b):
    s, e = two_sum(a[0], b[0])
    return quick_two_sum(s, e + (a[1] + b[1]))


def df_mul(a, b):
    p, e = two_prod(a[0], b[0], halves(a[0]), halves(b[0]))
    return quick_two_sum(p, e + (a[0] * b[1] + a[1] * b[0]))


def df_div(a, b):
    inverse = 1.0 / b[0]
    q1 = a[0] * inverse
    back = df_mul((q1, jnp.zeros_like(q1)), b)
    rest = df_add(a, (-back[0], -back[1]))
    return quick_two_sum(q1, rest[0] * inverse)


class Loaded:
    def __init__(self, source, ref, sem):
        self.ref = ref
        self.copy = pltpu.make_async_copy(source, ref, sem)
        self.copy.start()
        self.waited = False

    def get(self):
        if not self.waited:
            self.copy.wait()
            self.waited = True
        return self.ref


class Stored:
    def __init__(self, target, ref, take_sem, pending):
        self.target, self.ref, self.take_sem, self.pending = target, ref, take_sem, pending

    def send(self, start=None, count=None):
        source, target = self.ref, self.target
        if start is not None:
            source, target = source.at[pl.ds(start, count)], target.at[pl.ds(start, count)]
        copy = pltpu.make_async_copy(source, target, self.take_sem())
        copy.start()
        self.pending.append(copy)


def staged(kernel, args, outs, place=None, scratch=(), sends=None, after=(), flops=0):
    smem = [] if place is None else [place]
    cuts = [a[1:] if isinstance(a, tuple) else None for a in args]
    args = [a[0] if isinstance(a, tuple) else a for a in args]
    n_in, n_out = len(args), len(outs)
    sends = sends or n_out
    staging = [pltpu.VMEM(a.shape if cut is None else (cut[1],) + a.shape[1:], a.dtype) for a, cut in zip(args, cuts)]
    staging += [pltpu.VMEM(s, F32) for s in outs]

    def body(*refs):
        refs = list(refs)
        places = [refs.pop(0) for _ in smem]
        sources = [refs.pop(0) for _ in range(n_in)]
        sources = [s if cut is None else s.at[pl.ds(*cut)] for s, cut in zip(sources, cuts)]
        for _ in after:
            refs.pop(0)
        targets = [refs.pop(0) for _ in range(n_out)]
        buffers = [refs.pop(0) for _ in range(n_in)]
        holds = [refs.pop(0) for _ in range(n_out)]
        in_sems, out_sems = refs.pop(-2), refs.pop(-1)
        ins = [Loaded(s, b, in_sems.at[n]) for n, (s, b) in enumerate(zip(sources, buffers))]
        pending = []
        given = []
        for n in range(n_out):
            given.append(Stored(targets[n], holds[n], lambda: out_sems.at[len(pending)], pending))
        kernel(ins, given, *places, *refs)
        for x in ins:
            x.get()
        for copy in pending:
            copy.wait()

    return pl.pallas_call(
        body,
        out_shape=[jax.ShapeDtypeStruct(s, F32) for s in outs],
        in_specs=[SM] * len(smem) + [HB] * (n_in + len(after)),
        out_specs=[HB] * n_out,
        scratch_shapes=staging
        + [pltpu.VMEM(s, t) for s, t in scratch]
        + [pltpu.SemaphoreType.DMA((n_in,)), pltpu.SemaphoreType.DMA((sends,))],
        cost_estimate=pl.CostEstimate(
            flops=flops, bytes_accessed=4 * (sum(a.size for a in args) + sum(map(math.prod, outs))), transcendentals=0
        ),
        compiler_params=PARAMS,
    )(*smem, *args, *after)


def merge_rows(a, b, step):
    shape = a[0].shape
    first = (iota(shape, 0) & step) == 0

    def part(x, y):
        mixed = jnp.where(first, y, x)
        if step == 4:
            other = pltpu.roll(mixed, 4, 0)
        else:
            other = jnp.where(first, pltpu.roll(mixed, 8 - step, 0), pltpu.roll(mixed, step, 0))
        return jnp.where(first, x, y), other

    kept_high, other_high = part(a[0], b[0])
    kept_low, other_low = part(a[1], b[1])
    return df_add((kept_high, kept_low), (other_high, other_low))


def krylov_kernel(ins, outs, place_ref):
    cot_ref, bottom_ref, rows_ref, cols_ref, corner_ref = [x.get() for x in ins]
    up_out, left_out, own_out, diag_out, sums_out = outs
    up_ref, left_ref, own_ref, diag_ref, sums_ref = [x.ref for x in outs]
    r = place_ref[0]
    c = place_ref[1]
    shape = (24, 384)
    row = iota(shape, 0)
    lane = iota(shape, 1)

    def window(main, at):
        top = jnp.concatenate([corner_ref[8 * at : 8 * at + 8], rows_ref[8 * at : 8 * at + 8]], axis=1)
        side = jnp.where(iota((16, 128), 1) >= 120, pltpu.roll(cols_ref[at], 2, 1), 0.0)
        rest = jnp.concatenate([side, main], axis=1)
        return jnp.concatenate([top, rest], axis=0)

    inside = ((row >= 8) | (r > 0)) & ((lane >= 128) | (c > 0))
    start = jnp.where(inside, window(cot_ref[...], 0), 0.0)
    bottom = window(bottom_ref[...].astype(F32), 1)
    shifted = (4.2 + bottom / 25.0) - CENTRE

    def apply_shifted(v):
        below = jnp.where(row == 23, 0.0, pltpu.roll(v, 23, 0))
        right = jnp.where(lane == 383, 0.0, pltpu.roll(v, 383, 1))
        beside = below + pltpu.roll(v, 1, 0) + right + pltpu.roll(v, 1, 1)
        return jnp.where(inside, shifted * v - beside, 0.0)

    vectors = [start]
    images = []
    for step in range(KRYLOV):
        moved = apply_shifted(vectors[-1])
        images.append(moved + CENTRE * vectors[-1])
        if step == 0:
            vectors.append(moved * 0.25)
        elif step + 1 < KRYLOV:
            vectors.append(moved * 0.5 - vectors[-2])

    for k, v in enumerate(vectors):
        own_ref[24 * k : 24 * k + 24] = v
        near = pltpu.roll(v[0:16], 12, 0)[0:8]
        up_ref[8 * k : 8 * k + 8] = near
        left_ref[24 * k : 24 * k + 24] = pltpu.roll(v[:, 0:256], 192, 1)[:, 0:128]
        diag_ref[8 * k : 8 * k + 8] = pltpu.roll(near[:, 0:256], 192, 1)[:, 0:128]
    for out in (up_out, left_out, diag_out, own_out):
        out.send()

    domain = (
        (row >= 4)
        & (row < jnp.where(r == 15, 24, 20))
        & (lane >= 124)
        & (lane < jnp.where(c == 15, 384, 380))
    )
    cut = [jnp.where(domain, v, 0.0) for v in vectors]
    cut_parts = [halves(v) for v in cut]
    image_parts = [halves(w) for w in images]

    def tile(x, at):
        i, j = divmod(at, 3)
        return x[8 * i : 8 * i + 8, 128 * j : 128 * j + 128]

    def dot(x, x_parts, y, y_parts):
        total = None
        for at in range(9):
            p, e = two_prod(
                tile(x, at),
                tile(y, at),
                [tile(h, at) for h in x_parts],
                [tile(h, at) for h in y_parts],
            )
            if total is None:
                total = (p, e)
            else:
                s, f = two_sum(total[0], p)
                total = (s, total[1] + (e + f))
        return total

    dots = [dot(cut[i], cut_parts[i], images[j], image_parts[j]) for i, j in PAIRS]
    start_parts = halves(start)
    dots += [dot(cut[i], cut_parts[i], start, start_parts) for i in range(KRYLOV)]
    zero = jnp.zeros((8, 128), F32)
    dots += [(zero, zero)] * (16 - len(dots))
    packed = []
    for base in (0, 8):
        group = dots[base : base + 8]
        for step in (4, 2, 1):
            group = [merge_rows(group[i], group[i + step], step) for i in range(step)]
        total = group[0]
        for step in (64, 32, 16, 8, 4, 2, 1):
            total = df_add(total, (pltpu.roll(total[0], step, 1), pltpu.roll(total[1], step, 1)))
        packed.append(total)
    small_row = iota((8, 128), 0)
    small_lane = iota((8, 128), 1)
    spread = zero
    for part in (0, 1):
        for base in (0, 1):
            chosen = jnp.zeros((8, 128), jnp.bool_)
            for i in range(KRYLOV):
                for j in range(KRYLOV + 1):
                    index = len(PAIRS) + i if j == KRYLOV else PAIRS.index((min(i, j), max(i, j)))
                    if index // 8 == base:
                        chosen = chosen | (
                            (small_row == index % 8) & (small_lane == 32 * part + 8 * i + j)
                        )
            spread = spread + jnp.where(chosen, packed[base][part], 0.0)
    line = jnp.sum(spread, axis=0, keepdims=True)
    sums_ref[...] = jnp.broadcast_to(line, (256, 128))

    sums_out.send()


ROW_TURNS = (0, 4, 2, 6)
FIELDS = 6
LEVELS = 5


def packed_rows(parts, from_above):
    row = iota((8, 256), 0)
    order = (2, 1, 3, 0) if from_above else (0, 2, 1, 3)
    turned = [pltpu.roll(p, t, 0) if t else p for p, t in zip(parts, ROW_TURNS)]
    out = turned[order[3]]
    for n in (2, 1, 0):
        out = jnp.where(row < 2 * n + 2, turned[order[n]], out)
    return out


def packed_cols(parts, spare):
    group = (iota((16, 128), 1) + 2) & 127
    out = spare
    for m in range(len(parts) - 1, -1, -1):
        out = jnp.where(group < 4 * m + 4, pltpu.roll(parts[m], 4 * m, 1) if m else parts[m], out)
    return out


def columns_kernel(ins, outs):
    depth = ins[0].ref.shape[0]
    land_in, kappa_in, bottom_in, tcot_in, scot_in, theta_in, salt_in, ux_in, uy_in, surface_in = ins
    a_out, c_out, w_out, inv_out, ratio_out, down_out, up_out, right_out, left_out, corner_out = outs
    a_ref, c_ref, w_ref, inv_ref, ratio_ref, down_ref, up_ref, right_ref, left_ref, corner_ref = [x.ref for x in outs]
    bottom = bottom_in.get()[...]
    lines = 8 * depth + 8 * ((depth + 1) // 2)
    spare = []
    for n, field in enumerate((surface_in.get()[...], bottom.astype(F32))):
        down_ref[lines + 8 * n : lines + 8 * n + 8] = field[8:16]
        spare.append(pltpu.roll(field[:, 128:256], 126, 1))
        corner_ref[8 * n : 8 * n + 8] = field[8:16, 128:256]
    corner_out.send()
    land_ref = land_in.get()
    kappa_ref = kappa_in.get()
    tcot_ref = tcot_in.get()
    scot_ref = scot_in.get()

    def wet_at(k):
        return jnp.where(k < bottom, land_ref[k].astype(F32), 0.0)

    wet = wet_at(0)
    ratio = None
    couple_last = None
    state = None
    for k in range(depth):
        diagonal = jnp.ones((16, 256), F32)
        if k > 0:
            diagonal = diagonal + couple_last - couple_last * ratio
        if k < depth - 1:
            wet_next = wet_at(k + 1)
            couple = kappa_ref[k] * wet * wet_next
            diagonal = diagonal + couple
        inverse = 1.0 / diagonal
        rhs = (tcot_ref[k], scot_ref[k], wet)
        if k == 0:
            state = tuple(x * inverse for x in rhs)
        else:
            state = tuple((x + couple_last * s) * inverse for x, s in zip(rhs, state))
        a_ref[k], c_ref[k], w_ref[k] = state
        inv_ref[k] = inverse
        if k < depth - 1:
            ratio = couple * inverse
            ratio_ref[k] = ratio
            couple_last = couple
            wet = wet_next
    inv_out.send()
    ratio_out.send()
    theta_ref = theta_in.get()
    salt_ref = salt_in.get()
    ux_ref = ux_in.get()
    uy_ref = uy_in.get()
    row8 = iota((8, 256), 0)
    lane = iota((16, 128), 1)
    tails = {}
    last_parts, first_parts = [], []
    for k in range(depth - 1, -1, -1):
        wet = wet_at(k)
        if k < depth - 1:
            ratio = ratio_ref[k]
            state = tuple(x + ratio * s for x, s in zip((a_ref[k], c_ref[k], w_ref[k]), state))
            a_ref[k], c_ref[k], w_ref[k] = state
        fields = (theta_ref[k] * wet, salt_ref[k] * wet) + state
        down_ref[8 * k : 8 * k + 8] = packed_rows([f[8:16] for f in fields[:4]], True)
        up_ref[8 * k : 8 * k + 8] = packed_rows([f[0:8] for f in fields[:4]], False)
        flow = ux_ref[k] * wet
        open_low = flow[8:16] * pltpu.roll(wet[8:16], 7, 0)
        open_high = flow[0:8] * pltpu.roll(wet[0:8], 7, 0)
        face_low = jnp.where(row8 == 6, open_low, flow[8:16])
        face_high = jnp.where(row8 == 0, open_high, pltpu.roll(wet[0:8], 1, 0))
        tails[k] = ((state[2][8:16], face_low), (state[2][0:8], face_high))
        if k % 2 == 0:
            later = tails.pop(k + 1, tails[k])
            this = tails.pop(k)
            at = 8 * depth + 4 * k
            down_ref[at : at + 8] = packed_rows(this[0] + later[0], True)
            up_ref[at : at + 8] = packed_rows(this[1] + later[1], False)
        flow = uy_ref[k] * wet
        open_last = flow[:, 128:256] * pltpu.roll(wet[:, 128:256], 127, 1)
        open_first = flow[:, 0:128] * pltpu.roll(wet[:, 0:128], 127, 1)
        last = [f[:, 128:256] for f in fields] + [jnp.where(lane == 126, open_last, flow[:, 128:256])]
        first = [f[:, 0:128] for f in fields] + [
            jnp.where(lane == 0, open_first, pltpu.roll(wet[:, 0:128], 1, 1))
        ]
        last_parts = last + last_parts
        first_parts = first + first_parts
        if k % LEVELS == 0:
            g = k // LEVELS
            filler = spare[g % 2]
            right_ref[g] = packed_cols(last_parts, filler)
            left_ref[g] = packed_cols(first_parts, filler)
            last_parts, first_parts = [], []
    for out in (down_out, right_out, up_out, left_out, a_out, c_out, w_out):
        out.send()


SCALE = 1.0 / 12.0
BF16 = jnp.bfloat16


class Edges:
    def __init__(self, place_ref, depth, above, below, west, east):
        r = place_ref[0]
        c = place_ref[1]
        self.depth, self.above, self.below, self.west, self.east = depth, above, below, west, east
        self.row8 = iota((8, 256), 0)
        self.lane16 = iota((16, 128), 1)
        has_up = jnp.where(r > 0, 1.0, 0.0)
        has_down = jnp.where(r < 15, 1.0, 0.0)
        has_left = jnp.where(c > 0, 1.0, 0.0)
        has_right = jnp.where(c < 15, 1.0, 0.0)
        self.above_rows = (self.row8 & 2) != 0
        self.row_flags = (
            jnp.where(self.above_rows, has_up, has_down),
            jnp.where(self.above_rows, has_down, has_up),
        )
        self.west_lanes = (self.lane16 & 2) != 0
        self.lane_flag = jnp.where(self.west_lanes, has_left, has_right)

    def row_pair(self, at, second):
        above = self.above[at : at + 8]
        below = self.below[at : at + 8]
        if second:
            return jnp.where(self.above_rows, below, above) * self.row_flags[1]
        return jnp.where(self.above_rows, above, below) * self.row_flags[0]

    def turned_rows(self, pair, f):
        turn = (8 - ROW_TURNS[f]) % 8
        return pltpu.roll(pair, turn, 0) if turn else pair

    def tail_rows(self, k, f):
        pair = self.row_pair(8 * self.depth + 8 * (k // 2), k % 2 == 1)
        return self.turned_rows(pair, f + 2 * (k % 2))

    def cols(self, k, f):
        g = k // LEVELS
        pair = jnp.where(self.west_lanes, self.west[g], self.east[g]) * self.lane_flag
        turn = 4 * (FIELDS * (k % LEVELS) + f)
        return pltpu.roll(pair, 128 - turn, 1) if turn else pair


def next_of(x, axis):
    return pltpu.roll(x, x.shape[axis] - 1, axis)


def last_of(x, axis):
    return pltpu.roll(x, 1, axis)


def two_parts(x):
    high = x.astype(BF16)
    return jnp.concatenate([high, (x - high.astype(F32)).astype(BF16)], axis=1)


def stencil(offsets, columns):
    out = np.zeros((384, columns), np.float32)
    for j in range(columns):
        for offset, value in offsets:
            out[(j + offset) % 384, j] += value
    return jnp.asarray(np.concatenate([out, out]), BF16)


def forward_kernel(ins, outs, place_ref, parts_ref, filtered_ref, theta_sweep_ref, salt_sweep_ref):
    (
        land_in,
        bottom_in,
        above_in,
        below_in,
        west_in,
        east_in,
        ux_in,
        uy_in,
        theta_in,
        salt_in,
        filter_in,
        forcing_in,
        kappa_in,
        inv_in,
        ratio_in,
    ) = ins
    x_out, y_out, theta_out, salt_out = outs
    x_open_ref, y_open_ref, theta_drop_ref, salt_drop_ref = [x.ref for x in outs]
    depth = theta_in.ref.shape[0]
    bottom = bottom_in.get()[...]
    land_ref = land_in.get()
    edges = Edges(place_ref, depth, *[x.get() for x in (above_in, below_in, west_in, east_in)])
    row8, lane16 = edges.row8, edges.lane16
    ux_ref, uy_ref, theta_ref, salt_ref = [x.get() for x in (ux_in, uy_in, theta_in, salt_in)]

    def wet_at(k):
        return jnp.where(k < bottom, land_ref[k].astype(F32), 0.0)

    for k in range(depth):
        wet = wet_at(k)
        faces = edges.tail_rows(k, 1)
        wide = jnp.concatenate([wet, pltpu.roll(faces, 7, 0)], axis=0)
        later = next_of(wide, 0)
        x_open = jnp.concatenate(
            [ux_ref[k] * wet * later[0:16], jnp.where(row8 == 7, faces * later[16:24], faces)], axis=0
        )
        x_open_ref[k] = x_open * SCALE
        faces = edges.cols(k, 5)
        wide = jnp.concatenate([wet, pltpu.roll(faces, 127, 1)], axis=1)
        later = next_of(wide, 1)
        y_open = jnp.concatenate(
            [uy_ref[k] * wet * later[:, 0:256], jnp.where(lane16 == 127, faces * later[:, 256:384], faces)], axis=1
        )
        y_open_ref[k] = y_open * SCALE
        for f, ref in ((0, theta_ref), (1, salt_ref)):
            wide = jnp.concatenate([ref[k] * wet, edges.cols(k, f)], axis=1)
            at = 16 * (depth * f + k)
            parts_ref[at : at + 16] = two_parts(wide)
    x_out.send()
    y_out.send()
    filtered_ref[...] = jnp.dot(parts_ref[...], filter_in.get()[...], preferred_element_type=F32)
    forcing_ref, kappa_ref, inv_ref, ratio_ref = [x.get() for x in (forcing_in, kappa_in, inv_in, ratio_in)]

    couple_last = None
    state = None
    wet = wet_at(0)
    for k in range(depth):
        rows = edges.row_pair(8 * k, False)
        x_open = x_open_ref[k]
        y_open = y_open_ref[k]
        advected = []
        for f, ref in ((0, theta_ref), (1, salt_ref)):
            q = ref[k]
            wide = jnp.concatenate([q * wet, edges.turned_rows(rows, f)], axis=0)
            pair = wide + next_of(wide, 0)
            flux = x_open * (8.0 * pair - last_of(pair, 0) - next_of(pair, 0))
            change = (flux - last_of(flux, 0))[0:16]
            at = 16 * (depth * f + k)
            flux = y_open * filtered_ref[at : at + 16]
            change = change + (flux - last_of(flux, 1))[:, 0:256]
            advected.append(q - change)
        if k == 0:
            advected[0] = advected[0] + forcing_ref[...] * wet
        inverse = inv_ref[k]
        if k == 0:
            state = tuple(x * inverse for x in advected)
        else:
            state = tuple((x + couple_last * s) * inverse for x, s in zip(advected, state))
        theta_sweep_ref[k], salt_sweep_ref[k] = state
        if k < depth - 1:
            wet_next = wet_at(k + 1)
            couple_last = kappa_ref[k] * wet * wet_next
            wet = wet_next
    wet_later = wet
    for k in range(depth - 2, -1, -1):
        wet = wet_at(k)
        ratio = ratio_ref[k]
        new = (theta_sweep_ref[k] + ratio * state[0], salt_sweep_ref[k] + ratio * state[1])
        opened = wet * wet_later
        theta_drop_ref[k] = opened * (state[0] - new[0])
        salt_drop_ref[k] = opened * (state[1] - new[1])
        state = new
        wet_later = wet
    theta_out.send()
    salt_out.send()


def backward_kernel(ins, outs, place_ref, parts_ref, filtered_ref):
    (
        sums_in,
        own_in,
        near_in,
        side_in,
        corner_in,
        land_in,
        bottom_in,
        above_in,
        below_in,
        west_in,
        east_in,
        w_in,
        a_in,
        c_in,
        theta_drop_in,
        salt_drop_in,
        x_open_in,
        y_open_in,
        filter_in,
    ) = ins
    theta_out, salt_out, kappa_out, forcing_out = outs
    theta_grad_ref, salt_grad_ref, kappa_grad_ref, forcing_grad_ref = [x.ref for x in outs]
    depth = w_in.ref.shape[0]
    r = place_ref[0]
    c = place_ref[1]
    has_down = jnp.where(r < 15, 1.0, 0.0)
    sums_ref, own_ref, from_below_ref, from_right_ref, from_corner_ref = [
        x.get() for x in (sums_in, own_in, near_in, side_in, corner_in)
    ]

    small = (8, 128)
    small_row = iota(small, 0)
    total = (sums_ref[0:8], jnp.zeros(small, F32))
    for at in range(1, 32):
        s, e = two_sum(total[0], sums_ref[8 * at : 8 * at + 8])
        total = (s, total[1] + e)
    for step in (4, 2, 1):
        s, e = two_sum(total[0], pltpu.roll(total[0], step, 0))
        total = (s, (total[1] + pltpu.roll(total[1], step, 0)) + e)
    low = total[1] + pltpu.roll(total[0] + total[1], 96, 1)
    total = quick_two_sum(total[0], low)

    def as_rows(x):
        out = x
        for i in range(1, KRYLOV):
            out = jnp.where(small_row == i, pltpu.roll(x, 128 - 8 * i, 1), out)
        return out

    system = (as_rows(total[0]), as_rows(total[1]))

    def row_of(x, k):
        return jnp.broadcast_to(x[k : k + 1, :], small)

    def lane_of(x, k):
        return jnp.broadcast_to(x[:, k : k + 1], small)

    keep = []
    weights = []
    scales = [lane_of(row_of(system[0], k), k) for k in range(KRYLOV)]
    for k in range(KRYLOV):
        across = (row_of(system[0], k), row_of(system[1], k))
        pivot = (lane_of(across[0], k), lane_of(across[1], k))
        fine = pivot[0] > 1e-13 * scales[k]
        keep.append(fine)
        pivot = (jnp.where(fine, pivot[0], 1.0), jnp.where(fine, pivot[1], 0.0))
        factor = df_div((lane_of(system[0], k), lane_of(system[1], k)), pivot)
        used = fine & (small_row != k)
        factor = (jnp.where(used, factor[0], 0.0), jnp.where(used, factor[1], 0.0))
        product = df_mul(factor, across)
        system = df_add(system, (-product[0], -product[1]))
    for k in range(KRYLOV):
        pivot = lane_of(row_of(system[0], k), k)
        value = lane_of(row_of(system[0], k), KRYLOV)
        value = jnp.where(keep[k], value / jnp.where(keep[k], pivot, 1.0), 0.0)
        weights.append(value[0:1, 0:1])

    def combined(ref, rows):
        out = weights[0] * ref[0:rows]
        for k in range(1, KRYLOV):
            out = out + weights[k] * ref[rows * k : rows * k + rows]
        return out

    def rows_joined(upper, lower):
        turned = pltpu.roll(lower, 4, 0)
        row8 = iota(turned.shape, 0)
        middle = jnp.where((row8 >= 5) & (r < 15), turned, upper[16:24])
        return jnp.concatenate([upper[0:16], middle, turned * has_down], axis=0)

    joined = rows_joined(combined(own_ref, 24), combined(from_below_ref, 8))
    beside = pltpu.roll(rows_joined(combined(from_right_ref, 24), combined(from_corner_ref, 8)), 64, 1)
    lane_wide = iota((32, 128), 1)
    ending = jnp.where((lane_wide >= 125) & (c < 15), beside, joined[:, 256:384])
    surface = jnp.concatenate([joined[:, 128:256], ending], axis=1)
    zeta = surface[8:24]

    bottom = bottom_in.get()[...]
    land_ref = land_in.get()
    edges = Edges(place_ref, depth, *[x.get() for x in (above_in, below_in, west_in, east_in)])
    zeta_rows = jnp.where(edges.row8 < 4, surface[24:32], surface[0:8])
    zeta_cols = jnp.where(edges.lane16 < 64, beside[8:24], joined[8:24, 0:128])

    def wet_at(k):
        return jnp.where(k < bottom, land_ref[k].astype(F32), 0.0)

    w_ref, a_ref, c_ref, theta_drop_ref, salt_drop_ref, x_open_ref, y_open_ref = [
        x.get() for x in (w_in, a_in, c_in, theta_drop_in, salt_drop_in, x_open_in, y_open_in)
    ]
    share = (0.2, -0.15)
    mu_later = None
    for k in range(depth - 1, -1, -1):
        wet = wet_at(k)
        rise = zeta * w_ref[k]
        mu = (a_ref[k] + share[0] * rise, c_ref[k] + share[1] * rise)
        if k < depth - 1:
            kappa_grad_ref[k] = theta_drop_ref[k] * (mu[0] - mu_later[0]) + salt_drop_ref[k] * (mu[1] - mu_later[1])
        rows = edges.row_pair(8 * k, True)
        row_rise = zeta_rows * edges.tail_rows(k, 0)
        col_rise = zeta_cols * edges.cols(k, 4)
        x_open = x_open_ref[k]
        y_open = y_open_ref[k]
        for n, ref in ((0, theta_grad_ref), (1, salt_grad_ref)):
            wide = jnp.concatenate([mu[n], edges.cols(k, 2 + n) + share[n] * col_rise], axis=1)
            at = 16 * (depth * n + k)
            parts_ref[at : at + 16] = two_parts(y_open * (wide - next_of(wide, 1)))
            wide = jnp.concatenate([mu[n], edges.turned_rows(rows, 2 + n) + share[n] * row_rise], axis=0)
            h = x_open * (wide - next_of(wide, 0))
            pair = h + last_of(h, 0)
            change = (8.0 * pair - last_of(pair, 0) - next_of(pair, 0))[0:16]
            ref[k] = mu[n] - wet * change
        if k == 0:
            forcing_grad_ref[...] = zeta + wet * mu[0]
        mu_later = mu
    kappa_out.send()
    forcing_out.send()
    filtered_ref[...] = jnp.dot(parts_ref[...], filter_in.get()[...], preferred_element_type=F32)
    for n, ref, out in ((0, theta_grad_ref, theta_out), (1, salt_grad_ref, salt_out)):
        for k in range(depth):
            at = 16 * (depth * n + k)
            ref[k] = ref[k] - wet_at(k) * filtered_ref[at : at + 16]
            if k % 5 == 4:
                out.send(k - 4, 5)


def around(count, step):
    return [(i, (i + step) % count) for i in range(count)]


def across(step):
    return [
        (16 * i + j, 16 * ((i + step) % 16) + (j + step) % 16) for i in range(16) for j in range(16)
    ]


def shards(
    theta,
    salt,
    velocity_x,
    velocity_y,
    land_mask,
    kappa,
    forcing,
    bottom,
    theta_cot,
    salt_cot,
    surface_cot,
):
    depth = theta.shape[0]
    whole = theta.shape
    place = jnp.stack([lax.axis_index(TROW), lax.axis_index(TCOL)]).astype(jnp.int32)
    lines = 8 * depth + 8 * ((depth + 1) // 2)
    columns = (depth // LEVELS, 16, 128)
    a, c, w, inv, ratio, down, up, right, left, corner = staged(
        columns_kernel,
        (land_mask, kappa, bottom, theta_cot, salt_cot, theta, salt, velocity_x, velocity_y, surface_cot),
        [whole] * 4
        + [kappa.shape, (lines + 16, 256), (lines, 256), columns, columns, (16, 128)],
        flops=100 * theta.size,
    )
    above = lax.ppermute(down, TROW, around(16, 1))
    west = lax.ppermute(right, TCOL, around(16, 1))
    corner = lax.ppermute(corner, ALL, across(1))
    below = lax.ppermute(up, TROW, around(16, -1))
    east = lax.ppermute(left, TCOL, around(16, -1))
    near, side, own, tip, sums = staged(
        krylov_kernel,
        (surface_cot, bottom, (above, lines, 16), (west, 0, 2), corner),
        [(32, 384), (96, 128), (96, 384), (32, 128), (256, 128)],
        place=place,
    )
    near = lax.ppermute(near, TROW, around(16, -1))
    side = lax.ppermute(side, TCOL, around(16, -1))
    tip = lax.ppermute(tip, ALL, across(-1))
    x_open, y_open, theta_drop, salt_drop = staged(
        forward_kernel,
        (land_mask, bottom, above, below, west, east, velocity_x, velocity_y, theta, salt)
        + (stencil(((-1, -1), (0, 7), (1, 7), (2, -1)), 384), forcing, kappa, inv, ratio),
        [(depth, 24, 256), (depth, 16, 384), kappa.shape, kappa.shape],
        place=place,
        flops=200 * theta.size,
        scratch=[((32 * depth, 768), BF16), ((32 * depth, 384), F32), (whole, F32), (whole, F32)],
    )
    sums = lax.all_to_all(sums, ALL, 0, 0, tiled=True)
    return tuple(
        staged(
            backward_kernel,
            (sums, own, near, side, tip, land_mask, bottom, above, below, west, east, w, a, c)
            + (theta_drop, salt_drop, x_open, y_open, stencil(((-2, -1), (-1, 7), (0, 7), (1, -1)), 256)),
            [whole, whole, kappa.shape, forcing.shape],
            place=place,
            scratch=[((32 * depth, 768), BF16), ((32 * depth, 256), F32)],
            sends=12,
        )
    )


def solution(mesh):
    split = Mesh(mesh.devices.reshape(4, 2, 2, 2, 8), ALL)
    block = P(None, TROW, TCOL)
    flat = P(TROW, TCOL)
    return jax.shard_map(
        shards,
        mesh=split,
        in_specs=(block,) * 6 + (flat, flat, block, block, flat),
        out_specs=(block, block, block, flat),
        check_vma=False,
    )
```

```python
import math

import jax
import jax.numpy as jnp
import numpy as np
from jax import lax
from jax.experimental import pallas as pl
from jax.experimental.pallas import tpu as pltpu
from jax.sharding import Mesh
from jax.sharding import PartitionSpec as P

TROW = ("trow_0", "trow_1", "trow_2")
TCOL = ("tcol_0", "tcol_1")
ALL = TROW + TCOL
CENTRE = 4.75
KRYLOV = 4
PAIRS = [(i, j) for i in range(KRYLOV) for j in range(i, KRYLOV)]
F32 = jnp.float32
VM = pl.BlockSpec(memory_space=pltpu.VMEM)
SM = pl.BlockSpec(memory_space=pltpu.SMEM)
HB = pl.BlockSpec(memory_space=pltpu.HBM)
PARAMS = pltpu.CompilerParams(vmem_limit_bytes=58 * 1024 * 1024)


def iota(shape, dim):
    return lax.broadcasted_iota(jnp.int32, shape, dim)


def two_sum(a, b):
    s = a + b
    t = s - a
    return s, (a - (s - t)) + (b - t)


def quick_two_sum(a, b):
    s = a + b
    return s, b - (s - a)


def halves(a):
    t = a * 4097.0
    high = t - (t - a)
    return high, a - high


def two_prod(a, b, a_parts, b_parts):
    p = a * b
    ah, al = a_parts
    bh, bl = b_parts
    return p, ((ah * bh - p) + ah * bl + al * bh) + al * bl


def df_add(a, b):
    s, e = two_sum(a[0], b[0])
    return quick_two_sum(s, e + (a[1] + b[1]))


def df_mul(a, b):
    p, e = two_prod(a[0], b[0], halves(a[0]), halves(b[0]))
    return quick_two_sum(p, e + (a[0] * b[1] + a[1] * b[0]))


def df_div(a, b):
    inverse = 1.0 / b[0]
    q1 = a[0] * inverse
    back = df_mul((q1, jnp.zeros_like(q1)), b)
    rest = df_add(a, (-back[0], -back[1]))
    return quick_two_sum(q1, rest[0] * inverse)


class Loaded:
    def __init__(self, source, ref, parts, take_sem):
        self.ref = ref
        self.copies = []
        for part in parts:
            if part is None:
                self.copies.append(pltpu.make_async_copy(source, ref, take_sem()))
            else:
                self.copies.append(pltpu.make_async_copy(source.at[pl.ds(*part)], ref.at[pl.ds(*part)], take_sem()))

    def start(self, n):
        if n < len(self.copies):
            self.copies[n].start()
            self.waiting = list(self.copies)

    def first(self):
        if len(self.waiting) == len(self.copies):
            self.waiting.pop(0).wait()
        return self.ref

    def get(self):
        while self.waiting:
            self.waiting.pop(0).wait()
        return self.ref


class Stored:
    def __init__(self, target, ref, take_sem, pending):
        self.target, self.ref, self.take_sem, self.pending = target, ref, take_sem, pending

    def send(self, start=None, count=None):
        source, target = self.ref, self.target
        if start is not None:
            source, target = source.at[pl.ds(start, count)], target.at[pl.ds(start, count)]
        copy = pltpu.make_async_copy(source, target, self.take_sem())
        copy.start()
        self.pending.append(copy)


def staged(kernel, args, outs, place=None, scratch=(), sends=None, after=(), flops=0, lead=None):
    smem = [] if place is None else [place]

    def parts_of(shape):
        if lead is None or len(shape) < 3 or shape[0] < 24:
            return [None]
        start, stop = lead[0], min(lead[0] + lead[1], shape[0])
        return [(start, stop - start), (0, start) if start else (stop, shape[0] - stop)]

    cuts = [a[1:] if isinstance(a, tuple) else None for a in args]
    args = [a[0] if isinstance(a, tuple) else a for a in args]
    n_in, n_out = len(args), len(outs)
    sends = sends or n_out
    staging = [pltpu.VMEM(a.shape if cut is None else (cut[1],) + a.shape[1:], a.dtype) for a, cut in zip(args, cuts)]
    staging += [pltpu.VMEM(s, F32) for s in outs]

    def body(*refs):
        refs = list(refs)
        places = [refs.pop(0) for _ in smem]
        sources = [refs.pop(0) for _ in range(n_in)]
        sources = [s if cut is None else s.at[pl.ds(*cut)] for s, cut in zip(sources, cuts)]
        for _ in after:
            refs.pop(0)
        targets = [refs.pop(0) for _ in range(n_out)]
        buffers = [refs.pop(0) for _ in range(n_in)]
        holds = [refs.pop(0) for _ in range(n_out)]
        in_sems, out_sems = refs.pop(-2), refs.pop(-1)
        numbers = iter(range(2 * n_in))
        ins = [Loaded(s, b, parts_of(b.shape), lambda: in_sems.at[next(numbers)]) for s, b in zip(sources, buffers)]
        for n in (0, 1):
            for x in ins:
                x.start(n)
        pending = []
        given = []
        for n in range(n_out):
            given.append(Stored(targets[n], holds[n], lambda: out_sems.at[len(pending)], pending))
        kernel(ins, given, *places, *refs)
        for x in ins:
            x.get()
        for copy in pending:
            copy.wait()

    return pl.pallas_call(
        body,
        out_shape=[jax.ShapeDtypeStruct(s, F32) for s in outs],
        in_specs=[SM] * len(smem) + [HB] * (n_in + len(after)),
        out_specs=[HB] * n_out,
        scratch_shapes=staging
        + [pltpu.VMEM(s, t) for s, t in scratch]
        + [pltpu.SemaphoreType.DMA((2 * n_in,)), pltpu.SemaphoreType.DMA((sends,))],
        cost_estimate=pl.CostEstimate(
            flops=flops, bytes_accessed=4 * (sum(a.size for a in args) + sum(map(math.prod, outs))), transcendentals=0
        ),
        compiler_params=PARAMS,
    )(*smem, *args, *after)


def merge_rows(a, b, step):
    shape = a[0].shape
    first = (iota(shape, 0) & step) == 0

    def part(x, y):
        mixed = jnp.where(first, y, x)
        if step == 4:
            other = pltpu.roll(mixed, 4, 0)
        else:
            other = jnp.where(first, pltpu.roll(mixed, 8 - step, 0), pltpu.roll(mixed, step, 0))
        return jnp.where(first, x, y), other

    kept_high, other_high = part(a[0], b[0])
    kept_low, other_low = part(a[1], b[1])
    return df_add((kept_high, kept_low), (other_high, other_low))


def krylov_kernel(ins, outs, place_ref):
    cot_ref, bottom_ref, rows_ref, cols_ref, corner_ref = [x.get() for x in ins]
    up_out, left_out, own_out, diag_out, sums_out = outs
    up_ref, left_ref, own_ref, diag_ref, sums_ref = [x.ref for x in outs]
    r = place_ref[0]
    c = place_ref[1]
    shape = (24, 384)
    row = iota(shape, 0)
    lane = iota(shape, 1)

    def window(main, at):
        top = jnp.concatenate([corner_ref[8 * at : 8 * at + 8], rows_ref[8 * at : 8 * at + 8]], axis=1)
        side = jnp.where(iota((16, 128), 1) >= 120, pltpu.roll(cols_ref[at], 2, 1), 0.0)
        rest = jnp.concatenate([side, main], axis=1)
        return jnp.concatenate([top, rest], axis=0)

    inside = ((row >= 8) | (r > 0)) & ((lane >= 128) | (c > 0))
    start = jnp.where(inside, window(cot_ref[...], 0), 0.0)
    bottom = window(bottom_ref[...].astype(F32), 1)
    shifted = (4.2 + bottom / 25.0) - CENTRE

    def apply_shifted(v):
        below = jnp.where(row == 23, 0.0, pltpu.roll(v, 23, 0))
        right = jnp.where(lane == 383, 0.0, pltpu.roll(v, 383, 1))
        beside = below + pltpu.roll(v, 1, 0) + right + pltpu.roll(v, 1, 1)
        return jnp.where(inside, shifted * v - beside, 0.0)

    vectors = [start]
    images = []
    for step in range(KRYLOV):
        moved = apply_shifted(vectors[-1])
        images.append(moved + CENTRE * vectors[-1])
        if step == 0:
            vectors.append(moved * 0.25)
        elif step + 1 < KRYLOV:
            vectors.append(moved * 0.5 - vectors[-2])

    for k, v in enumerate(vectors):
        own_ref[24 * k : 24 * k + 24] = v
        near = pltpu.roll(v[0:16], 12, 0)[0:8]
        up_ref[8 * k : 8 * k + 8] = near
        left_ref[24 * k : 24 * k + 24] = pltpu.roll(v[:, 0:256], 192, 1)[:, 0:128]
        diag_ref[8 * k : 8 * k + 8] = pltpu.roll(near[:, 0:256], 192, 1)[:, 0:128]
    for out in (up_out, left_out, diag_out, own_out):
        out.send()

    domain = (
        (row >= 4)
        & (row < jnp.where(r == 15, 24, 20))
        & (lane >= 124)
        & (lane < jnp.where(c == 15, 384, 380))
    )
    cut = [jnp.where(domain, v, 0.0) for v in vectors]
    cut_parts = [halves(v) for v in cut]
    image_parts = [halves(w) for w in images]

    def tile(x, at):
        i, j = divmod(at, 3)
        return x[8 * i : 8 * i + 8, 128 * j : 128 * j + 128]

    def dot(x, x_parts, y, y_parts):
        total = None
        for at in range(9):
            p, e = two_prod(
                tile(x, at),
                tile(y, at),
                [tile(h, at) for h in x_parts],
                [tile(h, at) for h in y_parts],
            )
            if total is None:
                total = (p, e)
            else:
                s, f = two_sum(total[0], p)
                total = (s, total[1] + (e + f))
        return total

    dots = [dot(cut[i], cut_parts[i], images[j], image_parts[j]) for i, j in PAIRS]
    start_parts = halves(start)
    dots += [dot(cut[i], cut_parts[i], start, start_parts) for i in range(KRYLOV)]
    zero = jnp.zeros((8, 128), F32)
    dots += [(zero, zero)] * (16 - len(dots))
    packed = []
    for base in (0, 8):
        group = dots[base : base + 8]
        for step in (4, 2, 1):
            group = [merge_rows(group[i], group[i + step], step) for i in range(step)]
        total = group[0]
        for step in (64, 32, 16, 8, 4, 2, 1):
            total = df_add(total, (pltpu.roll(total[0], step, 1), pltpu.roll(total[1], step, 1)))
        packed.append(total)
    small_row = iota((8, 128), 0)
    small_lane = iota((8, 128), 1)
    spread = zero
    for part in (0, 1):
        for base in (0, 1):
            chosen = jnp.zeros((8, 128), jnp.bool_)
            for i in range(KRYLOV):
                for j in range(KRYLOV + 1):
                    index = len(PAIRS) + i if j == KRYLOV else PAIRS.index((min(i, j), max(i, j)))
                    if index // 8 == base:
                        chosen = chosen | (
                            (small_row == index % 8) & (small_lane == 32 * part + 8 * i + j)
                        )
            spread = spread + jnp.where(chosen, packed[base][part], 0.0)
    line = jnp.sum(spread, axis=0, keepdims=True)
    sums_ref[...] = jnp.broadcast_to(line, (256, 128))

    sums_out.send()


ROW_TURNS = (0, 4, 2, 6)
FIELDS = 6
LEVELS = 5


def packed_rows(parts, from_above):
    row = iota((8, 256), 0)
    order = (2, 1, 3, 0) if from_above else (0, 2, 1, 3)
    turned = [pltpu.roll(p, t, 0) if t else p for p, t in zip(parts, ROW_TURNS)]
    out = turned[order[3]]
    for n in (2, 1, 0):
        out = jnp.where(row < 2 * n + 2, turned[order[n]], out)
    return out


def packed_cols(parts, spare):
    group = (iota((16, 128), 1) + 2) & 127
    out = spare
    for m in range(len(parts) - 1, -1, -1):
        out = jnp.where(group < 4 * m + 4, pltpu.roll(parts[m], 4 * m, 1) if m else parts[m], out)
    return out


def columns_kernel(ins, outs):
    depth = ins[0].ref.shape[0]
    land_in, kappa_in, bottom_in, tcot_in, scot_in, theta_in, salt_in, ux_in, uy_in, surface_in = ins
    a_out, c_out, w_out, inv_out, ratio_out, down_out, up_out, right_out, left_out, corner_out = outs
    a_ref, c_ref, w_ref, inv_ref, ratio_ref, down_ref, up_ref, right_ref, left_ref, corner_ref = [x.ref for x in outs]
    bottom = bottom_in.get()[...]
    lines = 8 * depth + 8 * ((depth + 1) // 2)
    spare = []
    for n, field in enumerate((surface_in.get()[...], bottom.astype(F32))):
        down_ref[lines + 8 * n : lines + 8 * n + 8] = field[8:16]
        spare.append(pltpu.roll(field[:, 128:256], 126, 1))
        corner_ref[8 * n : 8 * n + 8] = field[8:16, 128:256]
    corner_out.send()
    early = (land_in, kappa_in, tcot_in, scot_in)
    land_ref, kappa_ref, tcot_ref, scot_ref = [x.first() for x in early]

    def wet_at(k):
        return jnp.where(k < bottom, land_ref[k].astype(F32), 0.0)

    wet = wet_at(0)
    ratio = None
    couple_last = None
    state = None
    for k in range(depth):
        if k == LEVELS - 1:
            for x in early:
                x.get()
        diagonal = jnp.ones((16, 256), F32)
        if k > 0:
            diagonal = diagonal + couple_last - couple_last * ratio
        if k < depth - 1:
            wet_next = wet_at(k + 1)
            couple = kappa_ref[k] * wet * wet_next
            diagonal = diagonal + couple
        inverse = 1.0 / diagonal
        rhs = (tcot_ref[k], scot_ref[k], wet)
        if k == 0:
            state = tuple(x * inverse for x in rhs)
        else:
            state = tuple((x + couple_last * s) * inverse for x, s in zip(rhs, state))
        a_ref[k], c_ref[k], w_ref[k] = state
        inv_ref[k] = inverse
        if k < depth - 1:
            ratio = couple * inverse
            ratio_ref[k] = ratio
            couple_last = couple
            wet = wet_next
    inv_out.send()
    ratio_out.send()
    theta_ref = theta_in.get()
    salt_ref = salt_in.get()
    ux_ref = ux_in.get()
    uy_ref = uy_in.get()
    row8 = iota((8, 256), 0)
    lane = iota((16, 128), 1)
    tails = {}
    last_parts, first_parts = [], []
    for k in range(depth - 1, -1, -1):
        wet = wet_at(k)
        if k < depth - 1:
            ratio = ratio_ref[k]
            state = tuple(x + ratio * s for x, s in zip((a_ref[k], c_ref[k], w_ref[k]), state))
            a_ref[k], c_ref[k], w_ref[k] = state
        fields = (theta_ref[k] * wet, salt_ref[k] * wet) + state
        down_ref[8 * k : 8 * k + 8] = packed_rows([f[8:16] for f in fields[:4]], True)
        up_ref[8 * k : 8 * k + 8] = packed_rows([f[0:8] for f in fields[:4]], False)
        flow = ux_ref[k] * wet
        open_low = flow[8:16] * pltpu.roll(wet[8:16], 7, 0)
        open_high = flow[0:8] * pltpu.roll(wet[0:8], 7, 0)
        face_low = jnp.where(row8 == 6, open_low, flow[8:16])
        face_high = jnp.where(row8 == 0, open_high, pltpu.roll(wet[0:8], 1, 0))
        tails[k] = ((state[2][8:16], face_low), (state[2][0:8], face_high))
        if k % 2 == 0:
            later = tails.pop(k + 1, tails[k])
            this = tails.pop(k)
            at = 8 * depth + 4 * k
            down_ref[at : at + 8] = packed_rows(this[0] + later[0], True)
            up_ref[at : at + 8] = packed_rows(this[1] + later[1], False)
        flow = uy_ref[k] * wet
        open_last = flow[:, 128:256] * pltpu.roll(wet[:, 128:256], 127, 1)
        open_first = flow[:, 0:128] * pltpu.roll(wet[:, 0:128], 127, 1)
        last = [f[:, 128:256] for f in fields] + [jnp.where(lane == 126, open_last, flow[:, 128:256])]
        first = [f[:, 0:128] for f in fields] + [
            jnp.where(lane == 0, open_first, pltpu.roll(wet[:, 0:128], 1, 1))
        ]
        last_parts = last + last_parts
        first_parts = first + first_parts
        if k % LEVELS == 0:
            g = k // LEVELS
            filler = spare[g % 2]
            right_ref[g] = packed_cols(last_parts, filler)
            left_ref[g] = packed_cols(first_parts, filler)
            last_parts, first_parts = [], []
            for out in (a_out, c_out, w_out):
                out.send(k, LEVELS)
    for out in (down_out, right_out, up_out, left_out):
        out.send()


SCALE = 1.0 / 12.0
BF16 = jnp.bfloat16


class Edges:
    def __init__(self, place_ref, depth, above, below, west, east):
        r = place_ref[0]
        c = place_ref[1]
        self.depth, self.above, self.below, self.west, self.east = depth, above, below, west, east
        self.row8 = iota((8, 256), 0)
        self.lane16 = iota((16, 128), 1)
        has_up = jnp.where(r > 0, 1.0, 0.0)
        has_down = jnp.where(r < 15, 1.0, 0.0)
        has_left = jnp.where(c > 0, 1.0, 0.0)
        has_right = jnp.where(c < 15, 1.0, 0.0)
        self.above_rows = (self.row8 & 2) != 0
        self.row_flags = (
            jnp.where(self.above_rows, has_up, has_down),
            jnp.where(self.above_rows, has_down, has_up),
        )
        self.west_lanes = (self.lane16 & 2) != 0
        self.lane_flag = jnp.where(self.west_lanes, has_left, has_right)

    def row_pair(self, at, second):
        above = self.above[at : at + 8]
        below = self.below[at : at + 8]
        if second:
            return jnp.where(self.above_rows, below, above) * self.row_flags[1]
        return jnp.where(self.above_rows, above, below) * self.row_flags[0]

    def turned_rows(self, pair, f):
        turn = (8 - ROW_TURNS[f]) % 8
        return pltpu.roll(pair, turn, 0) if turn else pair

    def tail_rows(self, k, f):
        pair = self.row_pair(8 * self.depth + 8 * (k // 2), k % 2 == 1)
        return self.turned_rows(pair, f + 2 * (k % 2))

    def cols(self, k, f):
        g = k // LEVELS
        pair = jnp.where(self.west_lanes, self.west[g], self.east[g]) * self.lane_flag
        turn = 4 * (FIELDS * (k % LEVELS) + f)
        return pltpu.roll(pair, 128 - turn, 1) if turn else pair


def next_of(x, axis):
    return pltpu.roll(x, x.shape[axis] - 1, axis)


def last_of(x, axis):
    return pltpu.roll(x, 1, axis)


def two_parts(x):
    high = x.astype(BF16)
    return jnp.concatenate([high, (x - high.astype(F32)).astype(BF16)], axis=1)


def stencil(offsets, columns):
    out = np.zeros((384, columns), np.float32)
    for j in range(columns):
        for offset, value in offsets:
            out[(j + offset) % 384, j] += value
    return jnp.asarray(np.concatenate([out, out]), BF16)


def forward_kernel(ins, outs, place_ref, parts_ref, filtered_ref, theta_sweep_ref, salt_sweep_ref):
    (
        land_in,
        bottom_in,
        above_in,
        below_in,
        west_in,
        east_in,
        ux_in,
        uy_in,
        theta_in,
        salt_in,
        filter_in,
        forcing_in,
        kappa_in,
        inv_in,
        ratio_in,
    ) = ins
    x_out, y_out, theta_out, salt_out = outs
    x_open_ref, y_open_ref, theta_drop_ref, salt_drop_ref = [x.ref for x in outs]
    depth = theta_in.ref.shape[0]
    bottom = bottom_in.get()[...]
    land_ref = land_in.first()
    edges = Edges(place_ref, depth, *[x.get() for x in (above_in, below_in, west_in, east_in)])
    row8, lane16 = edges.row8, edges.lane16
    early = (ux_in, uy_in, theta_in, salt_in, land_in)
    ux_ref, uy_ref, theta_ref, salt_ref, _ = [x.first() for x in early]

    def wet_at(k):
        return jnp.where(k < bottom, land_ref[k].astype(F32), 0.0)

    for k in range(depth):
        if k == LEVELS:
            for x in early:
                x.get()
        wet = wet_at(k)
        faces = edges.tail_rows(k, 1)
        wide = jnp.concatenate([wet, pltpu.roll(faces, 7, 0)], axis=0)
        later = next_of(wide, 0)
        x_open = jnp.concatenate(
            [ux_ref[k] * wet * later[0:16], jnp.where(row8 == 7, faces * later[16:24], faces)], axis=0
        )
        x_open_ref[k] = x_open * SCALE
        faces = edges.cols(k, 5)
        wide = jnp.concatenate([wet, pltpu.roll(faces, 127, 1)], axis=1)
        later = next_of(wide, 1)
        y_open = jnp.concatenate(
            [uy_ref[k] * wet * later[:, 0:256], jnp.where(lane16 == 127, faces * later[:, 256:384], faces)], axis=1
        )
        y_open_ref[k] = y_open * SCALE
        for f, ref in ((0, theta_ref), (1, salt_ref)):
            wide = jnp.concatenate([ref[k] * wet, edges.cols(k, f)], axis=1)
            at = 16 * (depth * f + k)
            parts_ref[at : at + 16] = two_parts(wide)
    x_out.send()
    y_out.send()
    filtered_ref[...] = jnp.dot(parts_ref[...], filter_in.get()[...], preferred_element_type=F32)
    forcing_ref, kappa_ref, inv_ref, ratio_ref = [x.get() for x in (forcing_in, kappa_in, inv_in, ratio_in)]

    couple_last = None
    state = None
    wet = wet_at(0)
    for k in range(depth):
        rows = edges.row_pair(8 * k, False)
        x_open = x_open_ref[k]
        y_open = y_open_ref[k]
        advected = []
        for f, ref in ((0, theta_ref), (1, salt_ref)):
            q = ref[k]
            wide = jnp.concatenate([q * wet, edges.turned_rows(rows, f)], axis=0)
            pair = wide + next_of(wide, 0)
            flux = x_open * (8.0 * pair - last_of(pair, 0) - next_of(pair, 0))
            change = (flux - last_of(flux, 0))[0:16]
            at = 16 * (depth * f + k)
            flux = y_open * filtered_ref[at : at + 16]
            change = change + (flux - last_of(flux, 1))[:, 0:256]
            advected.append(q - change)
        if k == 0:
            advected[0] = advected[0] + forcing_ref[...] * wet
        inverse = inv_ref[k]
        if k == 0:
            state = tuple(x * inverse for x in advected)
        else:
            state = tuple((x + couple_last * s) * inverse for x, s in zip(advected, state))
        theta_sweep_ref[k], salt_sweep_ref[k] = state
        if k < depth - 1:
            wet_next = wet_at(k + 1)
            couple_last = kappa_ref[k] * wet * wet_next
            wet = wet_next
    wet_later = wet
    for k in range(depth - 2, -1, -1):
        wet = wet_at(k)
        ratio = ratio_ref[k]
        new = (theta_sweep_ref[k] + ratio * state[0], salt_sweep_ref[k] + ratio * state[1])
        opened = wet * wet_later
        theta_drop_ref[k] = opened * (state[0] - new[0])
        salt_drop_ref[k] = opened * (state[1] - new[1])
        state = new
        wet_later = wet
        if k % LEVELS == 0:
            theta_out.send(k, min(LEVELS, depth - 1 - k))
            salt_out.send(k, min(LEVELS, depth - 1 - k))


def backward_kernel(ins, outs, place_ref, parts_ref, filtered_ref):
    (
        sums_in,
        own_in,
        near_in,
        side_in,
        corner_in,
        land_in,
        bottom_in,
        above_in,
        below_in,
        west_in,
        east_in,
        w_in,
        a_in,
        c_in,
        theta_drop_in,
        salt_drop_in,
        x_open_in,
        y_open_in,
        filter_in,
    ) = ins
    theta_out, salt_out, kappa_out, forcing_out = outs
    theta_grad_ref, salt_grad_ref, kappa_grad_ref, forcing_grad_ref = [x.ref for x in outs]
    depth = w_in.ref.shape[0]
    r = place_ref[0]
    c = place_ref[1]
    has_down = jnp.where(r < 15, 1.0, 0.0)
    sums_ref, own_ref, from_below_ref, from_right_ref, from_corner_ref = [
        x.get() for x in (sums_in, own_in, near_in, side_in, corner_in)
    ]

    small = (8, 128)
    small_row = iota(small, 0)
    total = (sums_ref[0:8], jnp.zeros(small, F32))
    for at in range(1, 32):
        s, e = two_sum(total[0], sums_ref[8 * at : 8 * at + 8])
        total = (s, total[1] + e)
    for step in (4, 2, 1):
        s, e = two_sum(total[0], pltpu.roll(total[0], step, 0))
        total = (s, (total[1] + pltpu.roll(total[1], step, 0)) + e)
    low = total[1] + pltpu.roll(total[0] + total[1], 96, 1)
    total = quick_two_sum(total[0], low)

    def as_rows(x):
        out = x
        for i in range(1, KRYLOV):
            out = jnp.where(small_row == i, pltpu.roll(x, 128 - 8 * i, 1), out)
        return out

    system = (as_rows(total[0]), as_rows(total[1]))

    def row_of(x, k):
        return jnp.broadcast_to(x[k : k + 1, :], small)

    def lane_of(x, k):
        return jnp.broadcast_to(x[:, k : k + 1], small)

    keep = []
    weights = []
    scales = [lane_of(row_of(system[0], k), k) for k in range(KRYLOV)]
    for k in range(KRYLOV):
        across = (row_of(system[0], k), row_of(system[1], k))
        pivot = (lane_of(across[0], k), lane_of(across[1], k))
        fine = pivot[0] > 1e-13 * scales[k]
        keep.append(fine)
        pivot = (jnp.where(fine, pivot[0], 1.0), jnp.where(fine, pivot[1], 0.0))
        factor = df_div((lane_of(system[0], k), lane_of(system[1], k)), pivot)
        used = fine & (small_row != k)
        factor = (jnp.where(used, factor[0], 0.0), jnp.where(used, factor[1], 0.0))
        product = df_mul(factor, across)
        system = df_add(system, (-product[0], -product[1]))
    for k in range(KRYLOV):
        pivot = lane_of(row_of(system[0], k), k)
        value = lane_of(row_of(system[0], k), KRYLOV)
        value = jnp.where(keep[k], value / jnp.where(keep[k], pivot, 1.0), 0.0)
        weights.append(value[0:1, 0:1])

    def combined(ref, rows):
        out = weights[0] * ref[0:rows]
        for k in range(1, KRYLOV):
            out = out + weights[k] * ref[rows * k : rows * k + rows]
        return out

    def rows_joined(upper, lower):
        turned = pltpu.roll(lower, 4, 0)
        row8 = iota(turned.shape, 0)
        middle = jnp.where((row8 >= 5) & (r < 15), turned, upper[16:24])
        return jnp.concatenate([upper[0:16], middle, turned * has_down], axis=0)

    joined = rows_joined(combined(own_ref, 24), combined(from_below_ref, 8))
    beside = pltpu.roll(rows_joined(combined(from_right_ref, 24), combined(from_corner_ref, 8)), 64, 1)
    lane_wide = iota((32, 128), 1)
    ending = jnp.where((lane_wide >= 125) & (c < 15), beside, joined[:, 256:384])
    surface = jnp.concatenate([joined[:, 128:256], ending], axis=1)
    zeta = surface[8:24]

    bottom = bottom_in.get()[...]
    land_ref = land_in.first()
    edges = Edges(place_ref, depth, *[x.get() for x in (above_in, below_in, west_in, east_in)])
    zeta_rows = jnp.where(edges.row8 < 4, surface[24:32], surface[0:8])
    zeta_cols = jnp.where(edges.lane16 < 64, beside[8:24], joined[8:24, 0:128])

    def wet_at(k):
        return jnp.where(k < bottom, land_ref[k].astype(F32), 0.0)

    early = (w_in, a_in, c_in, theta_drop_in, salt_drop_in, x_open_in, y_open_in, land_in)
    w_ref, a_ref, c_ref, theta_drop_ref, salt_drop_ref, x_open_ref, y_open_ref, _ = [x.first() for x in early]
    share = (0.2, -0.15)
    mu_later = None
    for k in range(depth - 1, -1, -1):
        if k == depth - LEVELS - 1:
            for x in early:
                x.get()
        wet = wet_at(k)
        rise = zeta * w_ref[k]
        mu = (a_ref[k] + share[0] * rise, c_ref[k] + share[1] * rise)
        if k < depth - 1:
            kappa_grad_ref[k] = theta_drop_ref[k] * (mu[0] - mu_later[0]) + salt_drop_ref[k] * (mu[1] - mu_later[1])
        rows = edges.row_pair(8 * k, True)
        row_rise = zeta_rows * edges.tail_rows(k, 0)
        col_rise = zeta_cols * edges.cols(k, 4)
        x_open = x_open_ref[k]
        y_open = y_open_ref[k]
        for n, ref in ((0, theta_grad_ref), (1, salt_grad_ref)):
            wide = jnp.concatenate([mu[n], edges.cols(k, 2 + n) + share[n] * col_rise], axis=1)
            at = 16 * (depth * n + k)
            parts_ref[at : at + 16] = two_parts(y_open * (wide - next_of(wide, 1)))
            wide = jnp.concatenate([mu[n], edges.turned_rows(rows, 2 + n) + share[n] * row_rise], axis=0)
            h = x_open * (wide - next_of(wide, 0))
            pair = h + last_of(h, 0)
            change = (8.0 * pair - last_of(pair, 0) - next_of(pair, 0))[0:16]
            ref[k] = mu[n] - wet * change
        if k == 0:
            forcing_grad_ref[...] = zeta + wet * mu[0]
        mu_later = mu
    kappa_out.send()
    forcing_out.send()
    filtered_ref[...] = jnp.dot(parts_ref[...], filter_in.get()[...], preferred_element_type=F32)
    for n, ref, out in ((0, theta_grad_ref, theta_out), (1, salt_grad_ref, salt_out)):
        for k in range(depth):
            at = 16 * (depth * n + k)
            ref[k] = ref[k] - wet_at(k) * filtered_ref[at : at + 16]
            if k % 5 == 4:
                out.send(k - 4, 5)


def around(count, step):
    return [(i, (i + step) % count) for i in range(count)]


def across(step):
    return [
        (16 * i + j, 16 * ((i + step) % 16) + (j + step) % 16) for i in range(16) for j in range(16)
    ]


def shards(
    theta,
    salt,
    velocity_x,
    velocity_y,
    land_mask,
    kappa,
    forcing,
    bottom,
    theta_cot,
    salt_cot,
    surface_cot,
):
    depth = theta.shape[0]
    whole = theta.shape
    place = jnp.stack([lax.axis_index(TROW), lax.axis_index(TCOL)]).astype(jnp.int32)
    lines = 8 * depth + 8 * ((depth + 1) // 2)
    columns = (depth // LEVELS, 16, 128)
    a, c, w, inv, ratio, down, up, right, left, corner = staged(
        columns_kernel,
        (land_mask, kappa, bottom, theta_cot, salt_cot, theta, salt, velocity_x, velocity_y, surface_cot),
        [whole] * 4
        + [kappa.shape, (lines + 16, 256), (lines, 256), columns, columns, (16, 128)],
        flops=100 * theta.size,
        lead=(0, LEVELS),
        sends=32,
    )
    above = lax.ppermute(down, TROW, around(16, 1))
    west = lax.ppermute(right, TCOL, around(16, 1))
    corner = lax.ppermute(corner, ALL, across(1))
    below = lax.ppermute(up, TROW, around(16, -1))
    east = lax.ppermute(left, TCOL, around(16, -1))
    near, side, own, tip, sums = staged(
        krylov_kernel,
        (surface_cot, bottom, (above, lines, 16), (west, 0, 2), corner),
        [(32, 384), (96, 128), (96, 384), (32, 128), (256, 128)],
        place=place,
        after=(below, east),
    )
    near = lax.ppermute(near, TROW, around(16, -1))
    side = lax.ppermute(side, TCOL, around(16, -1))
    tip = lax.ppermute(tip, ALL, across(-1))
    x_open, y_open, theta_drop, salt_drop = staged(
        forward_kernel,
        (land_mask, bottom, above, below, west, east, velocity_x, velocity_y, theta, salt)
        + (stencil(((-1, -1), (0, 7), (1, 7), (2, -1)), 384), forcing, kappa, inv, ratio),
        [(depth, 24, 256), (depth, 16, 384), kappa.shape, kappa.shape],
        place=place,
        flops=200 * theta.size,
        lead=(0, LEVELS),
        sends=16,
        scratch=[((32 * depth, 768), BF16), ((32 * depth, 384), F32), (whole, F32), (whole, F32)],
    )
    sums = lax.all_to_all(sums, ALL, 0, 0, tiled=True)
    return tuple(
        staged(
            backward_kernel,
            (sums, own, near, side, tip, land_mask, bottom, above, below, west, east, w, a, c)
            + (theta_drop, salt_drop, x_open, y_open, stencil(((-2, -1), (-1, 7), (0, 7), (1, -1)), 256)),
            [whole, whole, kappa.shape, forcing.shape],
            place=place,
            scratch=[((32 * depth, 768), BF16), ((32 * depth, 256), F32)],
            sends=12,
            lead=(depth - LEVELS, LEVELS),
        )
    )


def solution(mesh):
    split = Mesh(mesh.devices.reshape(4, 2, 2, 2, 8), ALL)
    block = P(None, TROW, TCOL)
    flat = P(TROW, TCOL)
    return jax.shard_map(
        shards,
        mesh=split,
        in_specs=(block,) * 6 + (flat, flat, block, block, flat),
        out_specs=(block, block, block, flat),
        check_vma=False,
    )
```

```python
import math

import jax
import jax.numpy as jnp
import numpy as np
from jax import lax
from jax.experimental import pallas as pl
from jax.experimental.pallas import tpu as pltpu
from jax.sharding import Mesh
from jax.sharding import PartitionSpec as P

TROW = ("trow_0", "trow_1", "trow_2")
TCOL = ("tcol_0", "tcol_1")
ALL = TROW + TCOL
CENTRE = 4.75
KRYLOV = 4
PAIRS = [(i, j) for i in range(KRYLOV) for j in range(i, KRYLOV)]
F32 = jnp.float32
VM = pl.BlockSpec(memory_space=pltpu.VMEM)
SM = pl.BlockSpec(memory_space=pltpu.SMEM)
HB = pl.BlockSpec(memory_space=pltpu.HBM)
PARAMS = pltpu.CompilerParams(vmem_limit_bytes=58 * 1024 * 1024)


def iota(shape, dim):
    return lax.broadcasted_iota(jnp.int32, shape, dim)


def two_sum(a, b):
    s = a + b
    t = s - a
    return s, (a - (s - t)) + (b - t)


def quick_two_sum(a, b):
    s = a + b
    return s, b - (s - a)


def halves(a):
    t = a * 4097.0
    high = t - (t - a)
    return high, a - high


def two_prod(a, b, a_parts, b_parts):
    p = a * b
    ah, al = a_parts
    bh, bl = b_parts
    return p, ((ah * bh - p) + ah * bl + al * bh) + al * bl


def df_add(a, b):
    s, e = two_sum(a[0], b[0])
    return quick_two_sum(s, e + (a[1] + b[1]))


def df_mul(a, b):
    p, e = two_prod(a[0], b[0], halves(a[0]), halves(b[0]))
    return quick_two_sum(p, e + (a[0] * b[1] + a[1] * b[0]))


def df_div(a, b):
    inverse = 1.0 / b[0]
    q1 = a[0] * inverse
    back = df_mul((q1, jnp.zeros_like(q1)), b)
    rest = df_add(a, (-back[0], -back[1]))
    return quick_two_sum(q1, rest[0] * inverse)


class Loaded:
    def __init__(self, source, ref, parts, take_sem):
        self.ref = ref
        self.copies = []
        for part in parts:
            if part is None:
                self.copies.append(pltpu.make_async_copy(source, ref, take_sem()))
            else:
                self.copies.append(pltpu.make_async_copy(source.at[pl.ds(*part)], ref.at[pl.ds(*part)], take_sem()))

    def start(self, n):
        if n < len(self.copies):
            self.copies[n].start()
            self.waiting = list(self.copies)

    def first(self):
        if len(self.waiting) == len(self.copies):
            self.waiting.pop(0).wait()
        return self.ref

    def get(self):
        while self.waiting:
            self.waiting.pop(0).wait()
        return self.ref


class Stored:
    def __init__(self, target, ref, take_sem, pending):
        self.target, self.ref, self.take_sem, self.pending = target, ref, take_sem, pending

    def send(self, start=None, count=None):
        source, target = self.ref, self.target
        if start is not None:
            source, target = source.at[pl.ds(start, count)], target.at[pl.ds(start, count)]
        copy = pltpu.make_async_copy(source, target, self.take_sem())
        copy.start()
        self.pending.append(copy)


def staged(kernel, args, outs, place=None, scratch=(), sends=None, after=(), flops=0, lead=None):
    smem = [] if place is None else [place]

    def parts_of(shape):
        if lead is None or len(shape) < 3 or shape[0] < 24:
            return [None]
        start, stop = lead[0], min(lead[0] + lead[1], shape[0])
        return [(start, stop - start), (0, start) if start else (stop, shape[0] - stop)]

    cuts = [a[1:] if isinstance(a, tuple) else None for a in args]
    args = [a[0] if isinstance(a, tuple) else a for a in args]
    n_in, n_out = len(args), len(outs)
    sends = sends or n_out
    staging = [pltpu.VMEM(a.shape if cut is None else (cut[1],) + a.shape[1:], a.dtype) for a, cut in zip(args, cuts)]
    staging += [pltpu.VMEM(s, F32) for s in outs]

    def body(*refs):
        refs = list(refs)
        places = [refs.pop(0) for _ in smem]
        sources = [refs.pop(0) for _ in range(n_in)]
        sources = [s if cut is None else s.at[pl.ds(*cut)] for s, cut in zip(sources, cuts)]
        for _ in after:
            refs.pop(0)
        targets = [refs.pop(0) for _ in range(n_out)]
        buffers = [refs.pop(0) for _ in range(n_in)]
        holds = [refs.pop(0) for _ in range(n_out)]
        in_sems, out_sems = refs.pop(-2), refs.pop(-1)
        numbers = iter(range(2 * n_in))
        ins = [Loaded(s, b, parts_of(b.shape), lambda: in_sems.at[next(numbers)]) for s, b in zip(sources, buffers)]
        for n in (0, 1):
            for x in ins:
                x.start(n)
        pending = []
        given = []
        for n in range(n_out):
            given.append(Stored(targets[n], holds[n], lambda: out_sems.at[len(pending)], pending))
        kernel(ins, given, *places, *refs)
        for x in ins:
            x.get()
        for copy in pending:
            copy.wait()

    return pl.pallas_call(
        body,
        out_shape=[jax.ShapeDtypeStruct(s, F32) for s in outs],
        in_specs=[SM] * len(smem) + [HB] * (n_in + len(after)),
        out_specs=[HB] * n_out,
        scratch_shapes=staging
        + [pltpu.VMEM(s, t) for s, t in scratch]
        + [pltpu.SemaphoreType.DMA((2 * n_in,)), pltpu.SemaphoreType.DMA((sends,))],
        cost_estimate=pl.CostEstimate(
            flops=flops, bytes_accessed=4 * (sum(a.size for a in args) + sum(map(math.prod, outs))), transcendentals=0
        ),
        compiler_params=PARAMS,
    )(*smem, *args, *after)


def corners_kernel(ins, outs, place_ref):
    fields = (ins[0].get()[...], ins[1].get()[...].astype(F32))
    main_a, main_b, cross_a, cross_b = [x.ref for x in outs]
    odd_row = (place_ref[0] & 1) == 1
    for n, field in enumerate(fields):
        at = slice(8 * n, 8 * n + 8)
        top_left, top_right = field[0:8, 0:128], field[0:8, 128:256]
        bottom_left, bottom_right = field[8:16, 0:128], field[8:16, 128:256]
        main_a[at] = jnp.where(odd_row, top_left, bottom_right)
        main_b[at] = jnp.where(odd_row, bottom_right, top_left)
        cross_a[at] = jnp.where(odd_row, top_right, bottom_left)
        cross_b[at] = jnp.where(odd_row, bottom_left, top_right)
    for out in outs:
        out.send()


def merge_rows(a, b, step):
    shape = a[0].shape
    first = (iota(shape, 0) & step) == 0

    def part(x, y):
        mixed = jnp.where(first, y, x)
        if step == 4:
            other = pltpu.roll(mixed, 4, 0)
        else:
            other = jnp.where(first, pltpu.roll(mixed, 8 - step, 0), pltpu.roll(mixed, step, 0))
        return jnp.where(first, x, y), other

    kept_high, other_high = part(a[0], b[0])
    kept_low, other_low = part(a[1], b[1])
    return df_add((kept_high, kept_low), (other_high, other_low))


def krylov_kernel(ins, outs, place_ref):
    cot_in, bottom_in, rows_a_in, rows_b_in, cols_a_in, cols_b_in = ins[:6]
    own_out, sums_out = outs
    own_ref, sums_ref = own_out.ref, sums_out.ref
    r = place_ref[0]
    c = place_ref[1]
    odd_row = (r & 1) == 1
    odd_col = (c & 1) == 1
    shape = (32, 384)
    row = iota(shape, 0)
    lane = iota(shape, 1)
    edge = iota((16, 128), 1)
    inside = ((row >= 8) | (r > 0)) & ((row < 24) | (r < 15))
    inside = inside & ((lane < 256) | ((lane < 264) & (c < 15)) | ((lane >= 376) & (c > 0)))
    rows_a, rows_b, cols_a, cols_b = [x.get() for x in (rows_a_in, rows_b_in, cols_a_in, cols_b_in)]
    main_a, main_b, cross_a, cross_b = [x.get() for x in ins[6:]]

    def window(main, n):
        at = slice(8 * n, 8 * n + 8)
        above = jnp.where(odd_row, rows_a[at], rows_b[at])
        below = jnp.where(odd_row, rows_b[at], rows_a[at])
        west = jnp.where(odd_col, cols_a[n], cols_b[n])
        east = jnp.where(odd_col, cols_b[n], cols_a[n])
        up_left = jnp.where(odd_row, main_a[at], main_b[at])
        down_right = jnp.where(odd_row, main_b[at], main_a[at])
        up_right = jnp.where(odd_row, cross_a[at], cross_b[at])
        down_left = jnp.where(odd_row, cross_b[at], cross_a[at])
        sides = jnp.where(edge < 64, pltpu.roll(east, 10, 1), pltpu.roll(west, 2, 1))
        return jnp.concatenate(
            [
                jnp.concatenate([above, jnp.where(edge[0:8] < 64, up_right, up_left)], axis=1),
                jnp.concatenate([main, sides], axis=1),
                jnp.concatenate([below, jnp.where(edge[0:8] < 64, down_right, down_left)], axis=1),
            ],
            axis=0,
        )

    start = jnp.where(inside, window(cot_in.get()[...], 0), 0.0)
    bottom = window(bottom_in.get()[...].astype(F32), 1)
    shifted = (4.2 + bottom / 25.0) - CENTRE

    def apply_shifted(v):
        beside = pltpu.roll(v, 31, 0) + pltpu.roll(v, 1, 0) + pltpu.roll(v, 383, 1) + pltpu.roll(v, 1, 1)
        return jnp.where(inside, shifted * v - beside, 0.0)

    vectors = [start]
    images = []
    for step in range(KRYLOV):
        moved = apply_shifted(vectors[-1])
        images.append(moved + CENTRE * vectors[-1])
        if step == 0:
            vectors.append(moved * 0.25)
        elif step + 1 < KRYLOV:
            vectors.append(moved * 0.5 - vectors[-2])

    for k, v in enumerate(vectors):
        own_ref[32 * k : 32 * k + 32] = v
    own_out.send()

    cut = [v[8:24, 0:256] for v in vectors]
    images = [w[8:24, 0:256] for w in images]
    cut_parts = [halves(v) for v in cut]
    image_parts = [halves(w) for w in images]

    def tile(x, at):
        i, j = divmod(at, 2)
        return x[8 * i : 8 * i + 8, 128 * j : 128 * j + 128]

    def dot(x, x_parts, y, y_parts):
        total = None
        for at in range(4):
            p, e = two_prod(
                tile(x, at),
                tile(y, at),
                [tile(h, at) for h in x_parts],
                [tile(h, at) for h in y_parts],
            )
            if total is None:
                total = (p, e)
            else:
                s, f = two_sum(total[0], p)
                total = (s, total[1] + (e + f))
        return total

    dots = [dot(cut[i], cut_parts[i], images[j], image_parts[j]) for i, j in PAIRS]
    dots += [dot(cut[i], cut_parts[i], cut[0], cut_parts[0]) for i in range(KRYLOV)]
    zero = jnp.zeros((8, 128), F32)
    dots += [(zero, zero)] * (16 - len(dots))
    packed = []
    for base in (0, 8):
        group = dots[base : base + 8]
        for step in (4, 2, 1):
            group = [merge_rows(group[i], group[i + step], step) for i in range(step)]
        total = group[0]
        for step in (64, 32, 16, 8, 4, 2, 1):
            total = df_add(total, (pltpu.roll(total[0], step, 1), pltpu.roll(total[1], step, 1)))
        packed.append(total)
    small_row = iota((8, 128), 0)
    small_lane = iota((8, 128), 1)
    spread = zero
    for part in (0, 1):
        for base in (0, 1):
            chosen = jnp.zeros((8, 128), jnp.bool_)
            for i in range(KRYLOV):
                for j in range(KRYLOV + 1):
                    index = len(PAIRS) + i if j == KRYLOV else PAIRS.index((min(i, j), max(i, j)))
                    if index // 8 == base:
                        chosen = chosen | (
                            (small_row == index % 8) & (small_lane == 32 * part + 8 * i + j)
                        )
            spread = spread + jnp.where(chosen, packed[base][part], 0.0)
    line = jnp.sum(spread, axis=0, keepdims=True)
    sums_ref[...] = jnp.broadcast_to(line, (256, 128))

    sums_out.send()


ROW_TURNS = (0, 4, 2, 6)
FIELDS = 6
LEVELS = 5


def packed_rows(parts, from_above):
    row = iota((8, 256), 0)
    order = (2, 1, 3, 0) if from_above else (0, 2, 1, 3)
    turned = [pltpu.roll(p, t, 0) if t else p for p, t in zip(parts, ROW_TURNS)]
    out = turned[order[3]]
    for n in (2, 1, 0):
        out = jnp.where(row < 2 * n + 2, turned[order[n]], out)
    return out


def packed_cols(parts, spare):
    group = (iota((16, 128), 1) + 2) & 127
    out = spare
    for m in range(len(parts) - 1, -1, -1):
        out = jnp.where(group < 4 * m + 4, pltpu.roll(parts[m], 4 * m, 1) if m else parts[m], out)
    return out


def columns_kernel(ins, outs, place_ref):
    depth = ins[0].ref.shape[0]
    land_in, kappa_in, bottom_in, tcot_in, scot_in, theta_in, salt_in, ux_in, uy_in, surface_in = ins
    a_out, c_out, w_out, inv_out, ratio_out, rows_a_out, rows_b_out, cols_a_out, cols_b_out = outs
    a_ref, c_ref, w_ref, inv_ref, ratio_ref, rows_a_ref, rows_b_ref, cols_a_ref, cols_b_ref = [x.ref for x in outs]
    odd_row = (place_ref[0] & 1) == 1
    odd_col = (place_ref[1] & 1) == 1

    def put_rows(at, down, up):
        rows_a_ref[at : at + 8] = jnp.where(odd_row, up, down)
        rows_b_ref[at : at + 8] = jnp.where(odd_row, down, up)

    def put_cols(g, right, left):
        cols_a_ref[g] = jnp.where(odd_col, left, right)
        cols_b_ref[g] = jnp.where(odd_col, right, left)

    bottom = bottom_in.get()[...]
    lines = 8 * depth + 8 * ((depth + 1) // 2)
    spare = []
    for n, field in enumerate((surface_in.get()[...], bottom.astype(F32))):
        put_rows(lines + 8 * n, field[8:16], field[0:8])
        spare.append((pltpu.roll(field[:, 128:256], 126, 1), pltpu.roll(field[:, 0:128], 118, 1)))
    early = (land_in, kappa_in, tcot_in, scot_in)
    land_ref, kappa_ref, tcot_ref, scot_ref = [x.first() for x in early]

    def wet_at(k):
        return jnp.where(k < bottom, land_ref[k].astype(F32), 0.0)

    wet = wet_at(0)
    ratio = None
    couple_last = None
    state = None
    for k in range(depth):
        if k == LEVELS - 1:
            for x in early:
                x.get()
        diagonal = jnp.ones((16, 256), F32)
        if k > 0:
            diagonal = diagonal + couple_last - couple_last * ratio
        if k < depth - 1:
            wet_next = wet_at(k + 1)
            couple = kappa_ref[k] * wet * wet_next
            diagonal = diagonal + couple
        inverse = 1.0 / diagonal
        rhs = (tcot_ref[k], scot_ref[k], wet)
        if k == 0:
            state = tuple(x * inverse for x in rhs)
        else:
            state = tuple((x + couple_last * s) * inverse for x, s in zip(rhs, state))
        a_ref[k], c_ref[k], w_ref[k] = state
        inv_ref[k] = inverse
        if k < depth - 1:
            ratio = couple * inverse
            ratio_ref[k] = ratio
            couple_last = couple
            wet = wet_next
    inv_out.send()
    ratio_out.send()
    theta_ref = theta_in.get()
    salt_ref = salt_in.get()
    ux_ref = ux_in.get()
    uy_ref = uy_in.get()
    row8 = iota((8, 256), 0)
    lane = iota((16, 128), 1)
    tails = {}
    last_parts, first_parts = [], []
    for k in range(depth - 1, -1, -1):
        wet = wet_at(k)
        if k < depth - 1:
            ratio = ratio_ref[k]
            state = tuple(x + ratio * s for x, s in zip((a_ref[k], c_ref[k], w_ref[k]), state))
            a_ref[k], c_ref[k], w_ref[k] = state
        fields = (theta_ref[k] * wet, salt_ref[k] * wet) + state
        put_rows(
            8 * k,
            packed_rows([f[8:16] for f in fields[:4]], True),
            packed_rows([f[0:8] for f in fields[:4]], False),
        )
        flow = ux_ref[k] * wet
        open_low = flow[8:16] * pltpu.roll(wet[8:16], 7, 0)
        open_high = flow[0:8] * pltpu.roll(wet[0:8], 7, 0)
        face_low = jnp.where(row8 == 6, open_low, flow[8:16])
        face_high = jnp.where(row8 == 0, open_high, pltpu.roll(wet[0:8], 1, 0))
        tails[k] = ((state[2][8:16], face_low), (state[2][0:8], face_high))
        if k % 2 == 0:
            later = tails.pop(k + 1, tails[k])
            this = tails.pop(k)
            put_rows(8 * depth + 4 * k, packed_rows(this[0] + later[0], True), packed_rows(this[1] + later[1], False))
        flow = uy_ref[k] * wet
        open_last = flow[:, 128:256] * pltpu.roll(wet[:, 128:256], 127, 1)
        open_first = flow[:, 0:128] * pltpu.roll(wet[:, 0:128], 127, 1)
        last = [f[:, 128:256] for f in fields] + [jnp.where(lane == 126, open_last, flow[:, 128:256])]
        first = [f[:, 0:128] for f in fields] + [
            jnp.where(lane == 0, open_first, pltpu.roll(wet[:, 0:128], 1, 1))
        ]
        last_parts = last + last_parts
        first_parts = first + first_parts
        if k % LEVELS == 0:
            g = k // LEVELS
            put_cols(g, packed_cols(last_parts, spare[g % 2][0]), packed_cols(first_parts, spare[g % 2][1]))
            last_parts, first_parts = [], []
            for out in (a_out, c_out, w_out):
                out.send(k, LEVELS)
    for out in (rows_a_out, rows_b_out, cols_a_out, cols_b_out):
        out.send()


SCALE = 1.0 / 12.0
BF16 = jnp.bfloat16


class Edges:
    def __init__(self, place_ref, depth, rows_a, rows_b, cols_a, cols_b):
        r = place_ref[0]
        c = place_ref[1]
        self.depth, self.rows_a, self.rows_b, self.cols_a, self.cols_b = depth, rows_a, rows_b, cols_a, cols_b
        self.row8 = iota((8, 256), 0)
        self.lane16 = iota((16, 128), 1)
        has_up = jnp.where(r > 0, 1.0, 0.0)
        has_down = jnp.where(r < 15, 1.0, 0.0)
        has_left = jnp.where(c > 0, 1.0, 0.0)
        has_right = jnp.where(c < 15, 1.0, 0.0)
        above_rows = (self.row8 >> 1) & 1
        self.row_flags = (
            jnp.where(above_rows == 1, has_up, has_down),
            jnp.where(above_rows == 1, has_down, has_up),
        )
        self.rows_from_a = (above_rows == (r & 1), above_rows != (r & 1))
        west_lanes = (self.lane16 >> 1) & 1
        self.lane_flag = jnp.where(west_lanes == 1, has_left, has_right)
        self.cols_from_a = west_lanes == (c & 1)

    def row_pair(self, at, second):
        n = 1 if second else 0
        pair = jnp.where(self.rows_from_a[n], self.rows_a[at : at + 8], self.rows_b[at : at + 8])
        return pair * self.row_flags[n]

    def turned_rows(self, pair, f):
        turn = (8 - ROW_TURNS[f]) % 8
        return pltpu.roll(pair, turn, 0) if turn else pair

    def tail_rows(self, k, f):
        pair = self.row_pair(8 * self.depth + 8 * (k // 2), k % 2 == 1)
        return self.turned_rows(pair, f + 2 * (k % 2))

    def cols(self, k, f):
        g = k // LEVELS
        pair = jnp.where(self.cols_from_a, self.cols_a[g], self.cols_b[g]) * self.lane_flag
        turn = 4 * (FIELDS * (k % LEVELS) + f)
        return pltpu.roll(pair, 128 - turn, 1) if turn else pair


def next_of(x, axis):
    return pltpu.roll(x, x.shape[axis] - 1, axis)


def last_of(x, axis):
    return pltpu.roll(x, 1, axis)


def two_parts(x):
    high = x.astype(BF16)
    return jnp.concatenate([high, (x - high.astype(F32)).astype(BF16)], axis=1)


def stencil(offsets, columns):
    out = np.zeros((384, columns), np.float32)
    for j in range(columns):
        for offset, value in offsets:
            out[(j + offset) % 384, j] += value
    return jnp.asarray(np.concatenate([out, out]), BF16)


def forward_kernel(ins, outs, place_ref, parts_ref, filtered_ref, theta_sweep_ref, salt_sweep_ref):
    (
        land_in,
        bottom_in,
        rows_a_in,
        rows_b_in,
        cols_a_in,
        cols_b_in,
        ux_in,
        uy_in,
        theta_in,
        salt_in,
        filter_in,
        forcing_in,
        kappa_in,
        inv_in,
        ratio_in,
    ) = ins
    x_out, y_out, theta_out, salt_out = outs
    x_open_ref, y_open_ref, theta_drop_ref, salt_drop_ref = [x.ref for x in outs]
    depth = theta_in.ref.shape[0]
    bottom = bottom_in.get()[...]
    land_ref = land_in.first()
    edges = Edges(place_ref, depth, *[x.get() for x in (rows_a_in, rows_b_in, cols_a_in, cols_b_in)])
    row8, lane16 = edges.row8, edges.lane16
    early = (ux_in, uy_in, theta_in, salt_in, land_in)
    ux_ref, uy_ref, theta_ref, salt_ref, _ = [x.first() for x in early]

    def wet_at(k):
        return jnp.where(k < bottom, land_ref[k].astype(F32), 0.0)

    for k in range(depth):
        if k == LEVELS:
            for x in early:
                x.get()
        wet = wet_at(k)
        faces = edges.tail_rows(k, 1)
        wide = jnp.concatenate([wet, pltpu.roll(faces, 7, 0)], axis=0)
        later = next_of(wide, 0)
        x_open = jnp.concatenate(
            [ux_ref[k] * wet * later[0:16], jnp.where(row8 == 7, faces * later[16:24], faces)], axis=0
        )
        x_open_ref[k] = x_open * SCALE
        faces = edges.cols(k, 5)
        wide = jnp.concatenate([wet, pltpu.roll(faces, 127, 1)], axis=1)
        later = next_of(wide, 1)
        y_open = jnp.concatenate(
            [uy_ref[k] * wet * later[:, 0:256], jnp.where(lane16 == 127, faces * later[:, 256:384], faces)], axis=1
        )
        y_open_ref[k] = y_open * SCALE
        for f, ref in ((0, theta_ref), (1, salt_ref)):
            wide = jnp.concatenate([ref[k] * wet, edges.cols(k, f)], axis=1)
            at = 16 * (depth * f + k)
            parts_ref[at : at + 16] = two_parts(wide)
    x_out.send()
    y_out.send()
    filtered_ref[...] = jnp.dot(parts_ref[...], filter_in.get()[...], preferred_element_type=F32)
    forcing_ref, kappa_ref, inv_ref, ratio_ref = [x.get() for x in (forcing_in, kappa_in, inv_in, ratio_in)]

    couple_last = None
    state = None
    wet = wet_at(0)
    for k in range(depth):
        rows = edges.row_pair(8 * k, False)
        x_open = x_open_ref[k]
        y_open = y_open_ref[k]
        advected = []
        for f, ref in ((0, theta_ref), (1, salt_ref)):
            q = ref[k]
            wide = jnp.concatenate([q * wet, edges.turned_rows(rows, f)], axis=0)
            pair = wide + next_of(wide, 0)
            flux = x_open * (8.0 * pair - last_of(pair, 0) - next_of(pair, 0))
            change = (flux - last_of(flux, 0))[0:16]
            at = 16 * (depth * f + k)
            flux = y_open * filtered_ref[at : at + 16]
            change = change + (flux - last_of(flux, 1))[:, 0:256]
            advected.append(q - change)
        if k == 0:
            advected[0] = advected[0] + forcing_ref[...] * wet
        inverse = inv_ref[k]
        if k == 0:
            state = tuple(x * inverse for x in advected)
        else:
            state = tuple((x + couple_last * s) * inverse for x, s in zip(advected, state))
        theta_sweep_ref[k], salt_sweep_ref[k] = state
        if k < depth - 1:
            wet_next = wet_at(k + 1)
            couple_last = kappa_ref[k] * wet * wet_next
            wet = wet_next
    wet_later = wet
    for k in range(depth - 2, -1, -1):
        wet = wet_at(k)
        ratio = ratio_ref[k]
        new = (theta_sweep_ref[k] + ratio * state[0], salt_sweep_ref[k] + ratio * state[1])
        opened = wet * wet_later
        theta_drop_ref[k] = opened * (state[0] - new[0])
        salt_drop_ref[k] = opened * (state[1] - new[1])
        state = new
        wet_later = wet
        if k % LEVELS == 0:
            theta_out.send(k, min(LEVELS, depth - 1 - k))
            salt_out.send(k, min(LEVELS, depth - 1 - k))


def backward_kernel(ins, outs, place_ref, parts_ref, filtered_ref):
    (
        sums_in,
        own_in,
        land_in,
        bottom_in,
        rows_a_in,
        rows_b_in,
        cols_a_in,
        cols_b_in,
        w_in,
        a_in,
        c_in,
        theta_drop_in,
        salt_drop_in,
        x_open_in,
        y_open_in,
        filter_in,
    ) = ins
    theta_out, salt_out, kappa_out, forcing_out = outs
    theta_grad_ref, salt_grad_ref, kappa_grad_ref, forcing_grad_ref = [x.ref for x in outs]
    depth = w_in.ref.shape[0]
    sums_ref = sums_in.get()
    own_ref = own_in.get()

    small = (8, 128)
    small_row = iota(small, 0)
    total = (sums_ref[0:8], jnp.zeros(small, F32))
    for at in range(1, 32):
        s, e = two_sum(total[0], sums_ref[8 * at : 8 * at + 8])
        total = (s, total[1] + e)
    for step in (4, 2, 1):
        s, e = two_sum(total[0], pltpu.roll(total[0], step, 0))
        total = (s, (total[1] + pltpu.roll(total[1], step, 0)) + e)
    low = total[1] + pltpu.roll(total[0] + total[1], 96, 1)
    total = quick_two_sum(total[0], low)

    def as_rows(x):
        out = x
        for i in range(1, KRYLOV):
            out = jnp.where(small_row == i, pltpu.roll(x, 128 - 8 * i, 1), out)
        return out

    system = (as_rows(total[0]), as_rows(total[1]))

    def row_of(x, k):
        return jnp.broadcast_to(x[k : k + 1, :], small)

    def lane_of(x, k):
        return jnp.broadcast_to(x[:, k : k + 1], small)

    keep = []
    weights = []
    scales = [lane_of(row_of(system[0], k), k) for k in range(KRYLOV)]
    for k in range(KRYLOV):
        across = (row_of(system[0], k), row_of(system[1], k))
        pivot = (lane_of(across[0], k), lane_of(across[1], k))
        fine = pivot[0] > 1e-13 * scales[k]
        keep.append(fine)
        pivot = (jnp.where(fine, pivot[0], 1.0), jnp.where(fine, pivot[1], 0.0))
        factor = df_div((lane_of(system[0], k), lane_of(system[1], k)), pivot)
        used = fine & (small_row != k)
        factor = (jnp.where(used, factor[0], 0.0), jnp.where(used, factor[1], 0.0))
        product = df_mul(factor, across)
        system = df_add(system, (-product[0], -product[1]))
    for k in range(KRYLOV):
        pivot = lane_of(row_of(system[0], k), k)
        value = lane_of(row_of(system[0], k), KRYLOV)
        value = jnp.where(keep[k], value / jnp.where(keep[k], pivot, 1.0), 0.0)
        weights.append(value[0:1, 0:1])

    def combined(ref, rows):
        out = weights[0] * ref[0:rows]
        for k in range(1, KRYLOV):
            out = out + weights[k] * ref[rows * k : rows * k + rows]
        return out

    surface = combined(own_ref, 32)
    zeta = surface[8:24, 0:256]
    bottom = bottom_in.get()[...]
    land_ref = land_in.first()
    edges = Edges(place_ref, depth, *[x.get() for x in (rows_a_in, rows_b_in, cols_a_in, cols_b_in)])
    zeta_rows = jnp.where(edges.row8 < 4, surface[24:32, 0:256], surface[0:8, 0:256])
    zeta_cols = surface[8:24, 256:384]

    def wet_at(k):
        return jnp.where(k < bottom, land_ref[k].astype(F32), 0.0)

    early = (w_in, a_in, c_in, theta_drop_in, salt_drop_in, x_open_in, y_open_in, land_in)
    w_ref, a_ref, c_ref, theta_drop_ref, salt_drop_ref, x_open_ref, y_open_ref, _ = [x.first() for x in early]
    share = (0.2, -0.15)
    mu_later = None
    for k in range(depth - 1, -1, -1):
        if k == depth - LEVELS - 1:
            for x in early:
                x.get()
        wet = wet_at(k)
        rise = zeta * w_ref[k]
        mu = (a_ref[k] + share[0] * rise, c_ref[k] + share[1] * rise)
        if k < depth - 1:
            kappa_grad_ref[k] = theta_drop_ref[k] * (mu[0] - mu_later[0]) + salt_drop_ref[k] * (mu[1] - mu_later[1])
        rows = edges.row_pair(8 * k, True)
        row_rise = zeta_rows * edges.tail_rows(k, 0)
        col_rise = zeta_cols * edges.cols(k, 4)
        x_open = x_open_ref[k]
        y_open = y_open_ref[k]
        for n, ref in ((0, theta_grad_ref), (1, salt_grad_ref)):
            wide = jnp.concatenate([mu[n], edges.cols(k, 2 + n) + share[n] * col_rise], axis=1)
            at = 16 * (depth * n + k)
            parts_ref[at : at + 16] = two_parts(y_open * (wide - next_of(wide, 1)))
            wide = jnp.concatenate([mu[n], edges.turned_rows(rows, 2 + n) + share[n] * row_rise], axis=0)
            h = x_open * (wide - next_of(wide, 0))
            pair = h + last_of(h, 0)
            change = (8.0 * pair - last_of(pair, 0) - next_of(pair, 0))[0:16]
            ref[k] = mu[n] - wet * change
        if k == 0:
            forcing_grad_ref[...] = zeta + wet * mu[0]
        mu_later = mu
    kappa_out.send()
    forcing_out.send()
    filtered_ref[...] = jnp.dot(parts_ref[...], filter_in.get()[...], preferred_element_type=F32)
    for n, ref, out in ((0, theta_grad_ref, theta_out), (1, salt_grad_ref, salt_out)):
        for k in range(depth):
            at = 16 * (depth * n + k)
            ref[k] = ref[k] - wet_at(k) * filtered_ref[at : at + 16]
            if k % 5 == 4:
                out.send(k - 4, 5)


def swaps(first):
    out = []
    for i in range(16):
        j = i + 1 if (i - first) % 2 == 0 else i - 1
        out.append((i, j if 0 <= j < 16 else i))
    return out


def corner_swaps(first, side):
    out = []
    for i in range(16):
        for j in range(16):
            step = 1 if (i - first) % 2 == 0 else -1
            row, col = i + step, j + side * step
            there = 0 <= row < 16 and 0 <= col < 16
            out.append((16 * i + j, 16 * row + col if there else 16 * i + j))
    return out


def shards(
    theta,
    salt,
    velocity_x,
    velocity_y,
    land_mask,
    kappa,
    forcing,
    bottom,
    theta_cot,
    salt_cot,
    surface_cot,
):
    depth = theta.shape[0]
    whole = theta.shape
    place = jnp.stack([lax.axis_index(TROW), lax.axis_index(TCOL)]).astype(jnp.int32)
    lines = 8 * depth + 8 * ((depth + 1) // 2)
    columns = (depth // LEVELS, 16, 128)
    corners = staged(corners_kernel, (surface_cot, bottom), [(16, 128)] * 4, place=place)
    corners = [
        lax.ppermute(x, ALL, corner_swaps(first, side))
        for x, (first, side) in zip(corners, ((0, 1), (1, 1), (0, -1), (1, -1)))
    ]
    a, c, w, inv, ratio, rows_a, rows_b, cols_a, cols_b = staged(
        columns_kernel,
        (land_mask, kappa, bottom, theta_cot, salt_cot, theta, salt, velocity_x, velocity_y, surface_cot),
        [whole] * 4 + [kappa.shape, (lines + 16, 256), (lines + 16, 256), columns, columns],
        place=place,
        flops=100 * theta.size,
        lead=(0, LEVELS),
        sends=32,
    )
    rows_a, rows_b, cols_a, cols_b, *corners = lax.optimization_barrier((rows_a, rows_b, cols_a, cols_b, *corners))
    rows_a = lax.ppermute(rows_a, TROW, swaps(0))
    rows_b = lax.ppermute(rows_b, TROW, swaps(1))
    cols_a = lax.ppermute(cols_a, TCOL, swaps(0))
    cols_b = lax.ppermute(cols_b, TCOL, swaps(1))
    own, sums = staged(
        krylov_kernel,
        (surface_cot, bottom, (rows_a, lines, 16), (rows_b, lines, 16), (cols_a, 0, 2), (cols_b, 0, 2), *corners),
        [(128, 384), (256, 128)],
        place=place,
    )
    x_open, y_open, theta_drop, salt_drop = staged(
        forward_kernel,
        (land_mask, bottom, rows_a, rows_b, cols_a, cols_b, velocity_x, velocity_y, theta, salt)
        + (stencil(((-1, -1), (0, 7), (1, 7), (2, -1)), 384), forcing, kappa, inv, ratio),
        [(depth, 24, 256), (depth, 16, 384), kappa.shape, kappa.shape],
        place=place,
        flops=200 * theta.size,
        lead=(0, LEVELS),
        sends=16,
        scratch=[((32 * depth, 768), BF16), ((32 * depth, 384), F32), (whole, F32), (whole, F32)],
    )
    sums = lax.all_to_all(sums, ALL, 0, 0, tiled=True)
    return tuple(
        staged(
            backward_kernel,
            (sums, own, land_mask, bottom, rows_a, rows_b, cols_a, cols_b, w, a, c)
            + (theta_drop, salt_drop, x_open, y_open, stencil(((-2, -1), (-1, 7), (0, 7), (1, -1)), 256)),
            [whole, whole, kappa.shape, forcing.shape],
            place=place,
            scratch=[((32 * depth, 768), BF16), ((32 * depth, 256), F32)],
            sends=12,
            lead=(depth - LEVELS, LEVELS),
        )
    )


def solution(mesh):
    split = Mesh(mesh.devices.reshape(4, 2, 2, 2, 8), ALL)
    block = P(None, TROW, TCOL)
    flat = P(TROW, TCOL)
    return jax.shard_map(
        shards,
        mesh=split,
        in_specs=(block,) * 6 + (flat, flat, block, block, flat),
        out_specs=(block, block, block, flat),
        check_vma=False,
    )
```

```python
import math

import jax
import jax.numpy as jnp
import numpy as np
from jax import lax
from jax.experimental import pallas as pl
from jax.experimental.pallas import tpu as pltpu
from jax.sharding import Mesh
from jax.sharding import PartitionSpec as P

TROW = ("trow_0", "trow_1", "trow_2")
TCOL = ("tcol_0", "tcol_1")
ALL = TROW + TCOL
CENTRE = 4.75
KRYLOV = 4
PAIRS = [(i, j) for i in range(KRYLOV) for j in range(i, KRYLOV)]
F32 = jnp.float32
VM = pl.BlockSpec(memory_space=pltpu.VMEM)
SM = pl.BlockSpec(memory_space=pltpu.SMEM)
HB = pl.BlockSpec(memory_space=pltpu.HBM)
PARAMS = pltpu.CompilerParams(vmem_limit_bytes=58 * 1024 * 1024)


def iota(shape, dim):
    return lax.broadcasted_iota(jnp.int32, shape, dim)


def two_sum(a, b):
    s = a + b
    t = s - a
    return s, (a - (s - t)) + (b - t)


def quick_two_sum(a, b):
    s = a + b
    return s, b - (s - a)


def halves(a):
    t = a * 4097.0
    high = t - (t - a)
    return high, a - high


def two_prod(a, b, a_parts, b_parts):
    p = a * b
    ah, al = a_parts
    bh, bl = b_parts
    return p, ((ah * bh - p) + ah * bl + al * bh) + al * bl


def df_add(a, b):
    s, e = two_sum(a[0], b[0])
    return quick_two_sum(s, e + (a[1] + b[1]))


def df_mul(a, b):
    p, e = two_prod(a[0], b[0], halves(a[0]), halves(b[0]))
    return quick_two_sum(p, e + (a[0] * b[1] + a[1] * b[0]))


def df_div(a, b):
    inverse = 1.0 / b[0]
    q1 = a[0] * inverse
    back = df_mul((q1, jnp.zeros_like(q1)), b)
    rest = df_add(a, (-back[0], -back[1]))
    return quick_two_sum(q1, rest[0] * inverse)


class Loaded:
    def __init__(self, source, ref, parts, take_sem):
        self.ref = ref
        self.copies = []
        for part in parts:
            if part is None:
                self.copies.append(pltpu.make_async_copy(source, ref, take_sem()))
            else:
                self.copies.append(pltpu.make_async_copy(source.at[pl.ds(*part)], ref.at[pl.ds(*part)], take_sem()))

    def start(self, n):
        if n < len(self.copies):
            self.copies[n].start()
            self.waiting = list(self.copies)

    def first(self):
        if len(self.waiting) == len(self.copies):
            self.waiting.pop(0).wait()
        return self.ref

    def get(self):
        while self.waiting:
            self.waiting.pop(0).wait()
        return self.ref


class Stored:
    def __init__(self, target, ref, take_sem, pending):
        self.target, self.ref, self.take_sem, self.pending = target, ref, take_sem, pending

    def send(self, start=None, count=None):
        source, target = self.ref, self.target
        if start is not None:
            source, target = source.at[pl.ds(start, count)], target.at[pl.ds(start, count)]
        copy = pltpu.make_async_copy(source, target, self.take_sem())
        copy.start()
        self.pending.append(copy)


def staged(kernel, args, outs, place=None, scratch=(), sends=None, after=(), flops=0, lead=None, into=None):
    smem = [] if place is None else [place]

    def parts_of(shape):
        if lead is None or len(shape) < 3 or shape[0] < 24:
            return [None]
        start, stop = lead[0], min(lead[0] + lead[1], shape[0])
        return [(start, stop - start), (0, start) if start else (stop, shape[0] - stop)]

    cuts = [a[1:] if isinstance(a, tuple) else None for a in args]
    args = [a[0] if isinstance(a, tuple) else a for a in args]
    n_in, n_out = len(args), len(outs)
    sends = sends or n_out
    staging = [pltpu.VMEM(a.shape if cut is None else (cut[1],) + a.shape[1:], a.dtype) for a, cut in zip(args, cuts)]
    held = outs if into is None else [(count,) + tuple(x.shape[1:]) for x, (start, count) in into]
    staging += [pltpu.VMEM(s, F32) for s in held]
    over = [] if into is None else [x for x, _ in into]

    def body(*refs):
        refs = list(refs)
        places = [refs.pop(0) for _ in smem]
        sources = [refs.pop(0) for _ in range(n_in)]
        sources = [s if cut is None else s.at[pl.ds(*cut)] for s, cut in zip(sources, cuts)]
        for _ in (*after, *over):
            refs.pop(0)
        targets = [refs.pop(0) for _ in range(n_out)]
        buffers = [refs.pop(0) for _ in range(n_in)]
        holds = [refs.pop(0) for _ in range(n_out)]
        in_sems, out_sems = refs.pop(-2), refs.pop(-1)
        numbers = iter(range(2 * n_in))
        ins = [Loaded(s, b, parts_of(b.shape), lambda: in_sems.at[next(numbers)]) for s, b in zip(sources, buffers)]
        for n in (0, 1):
            for x in ins:
                x.start(n)
        pending = []
        given = []
        for n in range(n_out):
            target = targets[n] if into is None else targets[n].at[pl.ds(*into[n][1])]
            given.append(Stored(target, holds[n], lambda: out_sems.at[len(pending)], pending))
        kernel(ins, given, *places, *refs)
        for x in ins:
            x.get()
        for copy in pending:
            copy.wait()

    return pl.pallas_call(
        body,
        out_shape=[jax.ShapeDtypeStruct(s, F32) for s in outs],
        in_specs=[SM] * len(smem) + [HB] * (n_in + len(after) + len(over)),
        out_specs=[HB] * n_out,
        input_output_aliases={len(smem) + n_in + len(after) + n: n for n in range(len(over))},
        scratch_shapes=staging
        + [pltpu.VMEM(s, t) for s, t in scratch]
        + [pltpu.SemaphoreType.DMA((2 * n_in,)), pltpu.SemaphoreType.DMA((sends,))],
        cost_estimate=pl.CostEstimate(
            flops=flops, bytes_accessed=4 * (sum(a.size for a in args) + sum(map(math.prod, outs))), transcendentals=0
        ),
        compiler_params=PARAMS,
    )(*smem, *args, *after, *over)


def sides_of(cols_a, cols_b, n, odd_col):
    west = jnp.where(odd_col, cols_a[n], cols_b[n])
    east = jnp.where(odd_col, cols_b[n], cols_a[n])
    return jnp.where(iota((16, 128), 1) < 64, pltpu.roll(east, 10, 1), pltpu.roll(west, 2, 1))


def ends_kernel(ins, outs, place_ref):
    cols_a, cols_b = [x.get() for x in ins]
    odd_row = (place_ref[0] & 1) == 1
    odd_col = (place_ref[1] & 1) == 1
    for n in (0, 1):
        sides = sides_of(cols_a, cols_b, n, odd_col)
        lanes = slice(128 * n, 128 * n + 128)
        outs[0].ref[:, lanes] = jnp.where(odd_row, sides[0:8], sides[8:16])
        outs[1].ref[:, lanes] = jnp.where(odd_row, sides[8:16], sides[0:8])
    for out in outs:
        out.send()


def merge_rows(a, b, step):
    shape = a[0].shape
    first = (iota(shape, 0) & step) == 0

    def part(x, y):
        mixed = jnp.where(first, y, x)
        if step == 4:
            other = pltpu.roll(mixed, 4, 0)
        else:
            other = jnp.where(first, pltpu.roll(mixed, 8 - step, 0), pltpu.roll(mixed, step, 0))
        return jnp.where(first, x, y), other

    kept_high, other_high = part(a[0], b[0])
    kept_low, other_low = part(a[1], b[1])
    return df_add((kept_high, kept_low), (other_high, other_low))


def krylov_kernel(ins, outs, place_ref):
    cot_in, bottom_in, rows_a_in, rows_b_in, cols_a_in, cols_b_in = ins
    own_out, sums_out = outs
    own_ref, sums_ref = own_out.ref, sums_out.ref
    r = place_ref[0]
    c = place_ref[1]
    odd_row = (r & 1) == 1
    odd_col = (c & 1) == 1
    shape = (32, 384)
    row = iota(shape, 0)
    lane = iota(shape, 1)
    inside = ((row >= 8) | (r > 0)) & ((row < 24) | (r < 15))
    inside = inside & ((lane < 256) | ((lane < 264) & (c < 15)) | ((lane >= 376) & (c > 0)))
    rows_a, rows_b, cols_a, cols_b = [x.get() for x in (rows_a_in, rows_b_in, cols_a_in, cols_b_in)]

    def window(main, n):
        at = slice(8 * n, 8 * n + 8)
        above = jnp.where(odd_row, rows_a[at], rows_b[at])
        below = jnp.where(odd_row, rows_b[at], rows_a[at])
        lanes = slice(128 * n, 128 * n + 128)
        above_ends = jnp.where(odd_row, rows_a[16:24, lanes], rows_b[16:24, lanes])
        below_ends = jnp.where(odd_row, rows_b[16:24, lanes], rows_a[16:24, lanes])
        return jnp.concatenate(
            [
                jnp.concatenate([above, above_ends], axis=1),
                jnp.concatenate([main, sides_of(cols_a, cols_b, n, odd_col)], axis=1),
                jnp.concatenate([below, below_ends], axis=1),
            ],
            axis=0,
        )

    start = jnp.where(inside, window(cot_in.get()[...], 0), 0.0)
    bottom = window(bottom_in.get()[...].astype(F32), 1)
    shifted = (4.2 + bottom / 25.0) - CENTRE

    def apply_shifted(v):
        beside = pltpu.roll(v, 31, 0) + pltpu.roll(v, 1, 0) + pltpu.roll(v, 383, 1) + pltpu.roll(v, 1, 1)
        return jnp.where(inside, shifted * v - beside, 0.0)

    vectors = [start]
    images = []
    for step in range(KRYLOV):
        moved = apply_shifted(vectors[-1])
        images.append(moved + CENTRE * vectors[-1])
        if step == 0:
            vectors.append(moved * 0.25)
        elif step + 1 < KRYLOV:
            vectors.append(moved * 0.5 - vectors[-2])

    for k, v in enumerate(vectors):
        own_ref[32 * k : 32 * k + 32] = v
    own_out.send()

    cut = [v[8:24, 0:256] for v in vectors]
    images = [w[8:24, 0:256] for w in images]
    cut_parts = [halves(v) for v in cut]
    image_parts = [halves(w) for w in images]

    def tile(x, at):
        i, j = divmod(at, 2)
        return x[8 * i : 8 * i + 8, 128 * j : 128 * j + 128]

    def dot(x, x_parts, y, y_parts):
        total = None
        for at in range(4):
            p, e = two_prod(
                tile(x, at),
                tile(y, at),
                [tile(h, at) for h in x_parts],
                [tile(h, at) for h in y_parts],
            )
            if total is None:
                total = (p, e)
            else:
                s, f = two_sum(total[0], p)
                total = (s, total[1] + (e + f))
        return total

    dots = [dot(cut[i], cut_parts[i], images[j], image_parts[j]) for i, j in PAIRS]
    dots += [dot(cut[i], cut_parts[i], cut[0], cut_parts[0]) for i in range(KRYLOV)]
    zero = jnp.zeros((8, 128), F32)
    dots += [(zero, zero)] * (16 - len(dots))
    packed = []
    for base in (0, 8):
        group = dots[base : base + 8]
        for step in (4, 2, 1):
            group = [merge_rows(group[i], group[i + step], step) for i in range(step)]
        total = group[0]
        for step in (64, 32, 16, 8, 4, 2, 1):
            total = df_add(total, (pltpu.roll(total[0], step, 1), pltpu.roll(total[1], step, 1)))
        packed.append(total)
    small_row = iota((8, 128), 0)
    small_lane = iota((8, 128), 1)
    spread = zero
    for part in (0, 1):
        for base in (0, 1):
            chosen = jnp.zeros((8, 128), jnp.bool_)
            for i in range(KRYLOV):
                for j in range(KRYLOV + 1):
                    index = len(PAIRS) + i if j == KRYLOV else PAIRS.index((min(i, j), max(i, j)))
                    if index // 8 == base:
                        chosen = chosen | (
                            (small_row == index % 8) & (small_lane == 32 * part + 8 * i + j)
                        )
            spread = spread + jnp.where(chosen, packed[base][part], 0.0)
    line = jnp.sum(spread, axis=0, keepdims=True)
    sums_ref[...] = jnp.broadcast_to(line, (256, 128))

    sums_out.send()


ROW_TURNS = (0, 4, 2, 6)
FIELDS = 6
LEVELS = 5


def packed_rows(parts, from_above):
    row = iota((8, 256), 0)
    order = (2, 1, 3, 0) if from_above else (0, 2, 1, 3)
    turned = [pltpu.roll(p, t, 0) if t else p for p, t in zip(parts, ROW_TURNS)]
    out = turned[order[3]]
    for n in (2, 1, 0):
        out = jnp.where(row < 2 * n + 2, turned[order[n]], out)
    return out


def packed_cols(parts, spare):
    group = (iota((16, 128), 1) + 2) & 127
    out = spare
    for m in range(len(parts) - 1, -1, -1):
        out = jnp.where(group < 4 * m + 4, pltpu.roll(parts[m], 4 * m, 1) if m else parts[m], out)
    return out


def columns_kernel(ins, outs, place_ref):
    depth = ins[0].ref.shape[0]
    land_in, kappa_in, bottom_in, tcot_in, scot_in, theta_in, salt_in, ux_in, uy_in, surface_in = ins
    a_out, c_out, w_out, inv_out, ratio_out, rows_a_out, rows_b_out, cols_a_out, cols_b_out = outs
    a_ref, c_ref, w_ref, inv_ref, ratio_ref, rows_a_ref, rows_b_ref, cols_a_ref, cols_b_ref = [x.ref for x in outs]
    odd_row = (place_ref[0] & 1) == 1
    odd_col = (place_ref[1] & 1) == 1

    def put_rows(at, down, up):
        rows_a_ref[at : at + 8] = jnp.where(odd_row, up, down)
        rows_b_ref[at : at + 8] = jnp.where(odd_row, down, up)

    def put_cols(g, right, left):
        cols_a_ref[g] = jnp.where(odd_col, left, right)
        cols_b_ref[g] = jnp.where(odd_col, right, left)

    bottom = bottom_in.get()[...]
    lines = 8 * depth + 8 * ((depth + 1) // 2)
    spare = []
    for n, field in enumerate((surface_in.get()[...], bottom.astype(F32))):
        put_rows(lines + 8 * n, field[8:16], field[0:8])
        spare.append((pltpu.roll(field[:, 128:256], 126, 1), pltpu.roll(field[:, 0:128], 118, 1)))
    early = (land_in, kappa_in, tcot_in, scot_in)
    land_ref, kappa_ref, tcot_ref, scot_ref = [x.first() for x in early]

    def wet_at(k):
        return jnp.where(k < bottom, land_ref[k].astype(F32), 0.0)

    wet = wet_at(0)
    ratio = None
    couple_last = None
    state = None
    for k in range(depth):
        if k == LEVELS - 1:
            for x in early:
                x.get()
        diagonal = jnp.ones((16, 256), F32)
        if k > 0:
            diagonal = diagonal + couple_last - couple_last * ratio
        if k < depth - 1:
            wet_next = wet_at(k + 1)
            couple = kappa_ref[k] * wet * wet_next
            diagonal = diagonal + couple
        inverse = 1.0 / diagonal
        rhs = (tcot_ref[k], scot_ref[k], wet)
        if k == 0:
            state = tuple(x * inverse for x in rhs)
        else:
            state = tuple((x + couple_last * s) * inverse for x, s in zip(rhs, state))
        a_ref[k], c_ref[k], w_ref[k] = state
        inv_ref[k] = inverse
        if k < depth - 1:
            ratio = couple * inverse
            ratio_ref[k] = ratio
            couple_last = couple
            wet = wet_next
    inv_out.send()
    ratio_out.send()
    theta_ref = theta_in.get()
    salt_ref = salt_in.get()
    ux_ref = ux_in.get()
    uy_ref = uy_in.get()
    row8 = iota((8, 256), 0)
    lane = iota((16, 128), 1)
    tails = {}
    last_parts, first_parts = [], []
    for k in range(depth - 1, -1, -1):
        wet = wet_at(k)
        if k < depth - 1:
            ratio = ratio_ref[k]
            state = tuple(x + ratio * s for x, s in zip((a_ref[k], c_ref[k], w_ref[k]), state))
            a_ref[k], c_ref[k], w_ref[k] = state
        fields = (theta_ref[k] * wet, salt_ref[k] * wet) + state
        put_rows(
            8 * k,
            packed_rows([f[8:16] for f in fields[:4]], True),
            packed_rows([f[0:8] for f in fields[:4]], False),
        )
        flow = ux_ref[k] * wet
        open_low = flow[8:16] * pltpu.roll(wet[8:16], 7, 0)
        open_high = flow[0:8] * pltpu.roll(wet[0:8], 7, 0)
        face_low = jnp.where(row8 == 6, open_low, flow[8:16])
        face_high = jnp.where(row8 == 0, open_high, pltpu.roll(wet[0:8], 1, 0))
        tails[k] = ((state[2][8:16], face_low), (state[2][0:8], face_high))
        if k % 2 == 0:
            later = tails.pop(k + 1, tails[k])
            this = tails.pop(k)
            put_rows(8 * depth + 4 * k, packed_rows(this[0] + later[0], True), packed_rows(this[1] + later[1], False))
        flow = uy_ref[k] * wet
        open_last = flow[:, 128:256] * pltpu.roll(wet[:, 128:256], 127, 1)
        open_first = flow[:, 0:128] * pltpu.roll(wet[:, 0:128], 127, 1)
        last = [f[:, 128:256] for f in fields] + [jnp.where(lane == 126, open_last, flow[:, 128:256])]
        first = [f[:, 0:128] for f in fields] + [
            jnp.where(lane == 0, open_first, pltpu.roll(wet[:, 0:128], 1, 1))
        ]
        last_parts = last + last_parts
        first_parts = first + first_parts
        if k % LEVELS == 0:
            g = k // LEVELS
            put_cols(g, packed_cols(last_parts, spare[g % 2][0]), packed_cols(first_parts, spare[g % 2][1]))
            last_parts, first_parts = [], []
            for out in (a_out, c_out, w_out):
                out.send(k, LEVELS)
    cols_a_out.send()
    cols_b_out.send()
    rows_a_out.send(0, lines + 16)
    rows_b_out.send(0, lines + 16)


SCALE = 1.0 / 12.0
BF16 = jnp.bfloat16


class Edges:
    def __init__(self, place_ref, depth, rows_a, rows_b, cols_a, cols_b):
        r = place_ref[0]
        c = place_ref[1]
        self.depth, self.rows_a, self.rows_b, self.cols_a, self.cols_b = depth, rows_a, rows_b, cols_a, cols_b
        self.row8 = iota((8, 256), 0)
        self.lane16 = iota((16, 128), 1)
        has_up = jnp.where(r > 0, 1.0, 0.0)
        has_down = jnp.where(r < 15, 1.0, 0.0)
        has_left = jnp.where(c > 0, 1.0, 0.0)
        has_right = jnp.where(c < 15, 1.0, 0.0)
        above_rows = (self.row8 >> 1) & 1
        self.row_flags = (
            jnp.where(above_rows == 1, has_up, has_down),
            jnp.where(above_rows == 1, has_down, has_up),
        )
        self.rows_from_a = (above_rows == (r & 1), above_rows != (r & 1))
        west_lanes = (self.lane16 >> 1) & 1
        self.lane_flag = jnp.where(west_lanes == 1, has_left, has_right)
        self.cols_from_a = west_lanes == (c & 1)

    def row_pair(self, at, second):
        n = 1 if second else 0
        pair = jnp.where(self.rows_from_a[n], self.rows_a[at : at + 8], self.rows_b[at : at + 8])
        return pair * self.row_flags[n]

    def turned_rows(self, pair, f):
        turn = (8 - ROW_TURNS[f]) % 8
        return pltpu.roll(pair, turn, 0) if turn else pair

    def tail_rows(self, k, f):
        pair = self.row_pair(8 * self.depth + 8 * (k // 2), k % 2 == 1)
        return self.turned_rows(pair, f + 2 * (k % 2))

    def cols(self, k, f):
        g = k // LEVELS
        pair = jnp.where(self.cols_from_a, self.cols_a[g], self.cols_b[g]) * self.lane_flag
        turn = 4 * (FIELDS * (k % LEVELS) + f)
        return pltpu.roll(pair, 128 - turn, 1) if turn else pair


def next_of(x, axis):
    return pltpu.roll(x, x.shape[axis] - 1, axis)


def last_of(x, axis):
    return pltpu.roll(x, 1, axis)


def two_parts(x):
    high = x.astype(BF16)
    return jnp.concatenate([high, (x - high.astype(F32)).astype(BF16)], axis=1)


def stencil(offsets, columns):
    out = np.zeros((384, columns), np.float32)
    for j in range(columns):
        for offset, value in offsets:
            out[(j + offset) % 384, j] += value
    return jnp.asarray(np.concatenate([out, out]), BF16)


def forward_kernel(ins, outs, place_ref, parts_ref, filtered_ref, theta_sweep_ref, salt_sweep_ref):
    (
        land_in,
        bottom_in,
        rows_a_in,
        rows_b_in,
        cols_a_in,
        cols_b_in,
        ux_in,
        uy_in,
        theta_in,
        salt_in,
        filter_in,
        forcing_in,
        kappa_in,
        inv_in,
        ratio_in,
    ) = ins
    x_out, y_out, theta_out, salt_out = outs
    x_open_ref, y_open_ref, theta_drop_ref, salt_drop_ref = [x.ref for x in outs]
    depth = theta_in.ref.shape[0]
    bottom = bottom_in.get()[...]
    land_ref = land_in.first()
    edges = Edges(place_ref, depth, *[x.get() for x in (rows_a_in, rows_b_in, cols_a_in, cols_b_in)])
    row8, lane16 = edges.row8, edges.lane16
    early = (ux_in, uy_in, theta_in, salt_in, land_in)
    ux_ref, uy_ref, theta_ref, salt_ref, _ = [x.first() for x in early]

    def wet_at(k):
        return jnp.where(k < bottom, land_ref[k].astype(F32), 0.0)

    for k in range(depth):
        if k == LEVELS:
            for x in early:
                x.get()
        wet = wet_at(k)
        faces = edges.tail_rows(k, 1)
        wide = jnp.concatenate([wet, pltpu.roll(faces, 7, 0)], axis=0)
        later = next_of(wide, 0)
        x_open = jnp.concatenate(
            [ux_ref[k] * wet * later[0:16], jnp.where(row8 == 7, faces * later[16:24], faces)], axis=0
        )
        x_open_ref[k] = x_open * SCALE
        faces = edges.cols(k, 5)
        wide = jnp.concatenate([wet, pltpu.roll(faces, 127, 1)], axis=1)
        later = next_of(wide, 1)
        y_open = jnp.concatenate(
            [uy_ref[k] * wet * later[:, 0:256], jnp.where(lane16 == 127, faces * later[:, 256:384], faces)], axis=1
        )
        y_open_ref[k] = y_open * SCALE
        for f, ref in ((0, theta_ref), (1, salt_ref)):
            wide = jnp.concatenate([ref[k] * wet, edges.cols(k, f)], axis=1)
            at = 16 * (depth * f + k)
            parts_ref[at : at + 16] = two_parts(wide)
    x_out.send()
    y_out.send()
    filtered_ref[...] = jnp.dot(parts_ref[...], filter_in.get()[...], preferred_element_type=F32)
    forcing_ref, kappa_ref, inv_ref, ratio_ref = [x.get() for x in (forcing_in, kappa_in, inv_in, ratio_in)]

    couple_last = None
    state = None
    wet = wet_at(0)
    for k in range(depth):
        rows = edges.row_pair(8 * k, False)
        x_open = x_open_ref[k]
        y_open = y_open_ref[k]
        advected = []
        for f, ref in ((0, theta_ref), (1, salt_ref)):
            q = ref[k]
            wide = jnp.concatenate([q * wet, edges.turned_rows(rows, f)], axis=0)
            pair = wide + next_of(wide, 0)
            flux = x_open * (8.0 * pair - last_of(pair, 0) - next_of(pair, 0))
            change = (flux - last_of(flux, 0))[0:16]
            at = 16 * (depth * f + k)
            flux = y_open * filtered_ref[at : at + 16]
            change = change + (flux - last_of(flux, 1))[:, 0:256]
            advected.append(q - change)
        if k == 0:
            advected[0] = advected[0] + forcing_ref[...] * wet
        inverse = inv_ref[k]
        if k == 0:
            state = tuple(x * inverse for x in advected)
        else:
            state = tuple((x + couple_last * s) * inverse for x, s in zip(advected, state))
        theta_sweep_ref[k], salt_sweep_ref[k] = state
        if k < depth - 1:
            wet_next = wet_at(k + 1)
            couple_last = kappa_ref[k] * wet * wet_next
            wet = wet_next
    wet_later = wet
    for k in range(depth - 2, -1, -1):
        wet = wet_at(k)
        ratio = ratio_ref[k]
        new = (theta_sweep_ref[k] + ratio * state[0], salt_sweep_ref[k] + ratio * state[1])
        opened = wet * wet_later
        theta_drop_ref[k] = opened * (state[0] - new[0])
        salt_drop_ref[k] = opened * (state[1] - new[1])
        state = new
        wet_later = wet
        if k % LEVELS == 0:
            theta_out.send(k, min(LEVELS, depth - 1 - k))
            salt_out.send(k, min(LEVELS, depth - 1 - k))


def backward_kernel(ins, outs, place_ref, parts_ref, filtered_ref):
    (
        sums_in,
        own_in,
        land_in,
        bottom_in,
        rows_a_in,
        rows_b_in,
        cols_a_in,
        cols_b_in,
        w_in,
        a_in,
        c_in,
        theta_drop_in,
        salt_drop_in,
        x_open_in,
        y_open_in,
        filter_in,
    ) = ins
    theta_out, salt_out, kappa_out, forcing_out = outs
    theta_grad_ref, salt_grad_ref, kappa_grad_ref, forcing_grad_ref = [x.ref for x in outs]
    depth = w_in.ref.shape[0]
    sums_ref = sums_in.get()
    own_ref = own_in.get()

    small = (8, 128)
    small_row = iota(small, 0)
    total = (sums_ref[0:8], jnp.zeros(small, F32))
    for at in range(1, 32):
        s, e = two_sum(total[0], sums_ref[8 * at : 8 * at + 8])
        total = (s, total[1] + e)
    for step in (4, 2, 1):
        s, e = two_sum(total[0], pltpu.roll(total[0], step, 0))
        total = (s, (total[1] + pltpu.roll(total[1], step, 0)) + e)
    low = total[1] + pltpu.roll(total[0] + total[1], 96, 1)
    total = quick_two_sum(total[0], low)

    def as_rows(x):
        out = x
        for i in range(1, KRYLOV):
            out = jnp.where(small_row == i, pltpu.roll(x, 128 - 8 * i, 1), out)
        return out

    system = (as_rows(total[0]), as_rows(total[1]))

    def row_of(x, k):
        return jnp.broadcast_to(x[k : k + 1, :], small)

    def lane_of(x, k):
        return jnp.broadcast_to(x[:, k : k + 1], small)

    keep = []
    weights = []
    scales = [lane_of(row_of(system[0], k), k) for k in range(KRYLOV)]
    for k in range(KRYLOV):
        across = (row_of(system[0], k), row_of(system[1], k))
        pivot = (lane_of(across[0], k), lane_of(across[1], k))
        fine = pivot[0] > 1e-13 * scales[k]
        keep.append(fine)
        pivot = (jnp.where(fine, pivot[0], 1.0), jnp.where(fine, pivot[1], 0.0))
        factor = df_div((lane_of(system[0], k), lane_of(system[1], k)), pivot)
        used = fine & (small_row != k)
        factor = (jnp.where(used, factor[0], 0.0), jnp.where(used, factor[1], 0.0))
        product = df_mul(factor, across)
        system = df_add(system, (-product[0], -product[1]))
    for k in range(KRYLOV):
        pivot = lane_of(row_of(system[0], k), k)
        value = lane_of(row_of(system[0], k), KRYLOV)
        value = jnp.where(keep[k], value / jnp.where(keep[k], pivot, 1.0), 0.0)
        weights.append(value[0:1, 0:1])

    def combined(ref, rows):
        out = weights[0] * ref[0:rows]
        for k in range(1, KRYLOV):
            out = out + weights[k] * ref[rows * k : rows * k + rows]
        return out

    surface = combined(own_ref, 32)
    zeta = surface[8:24, 0:256]
    bottom = bottom_in.get()[...]
    land_ref = land_in.first()
    edges = Edges(place_ref, depth, *[x.get() for x in (rows_a_in, rows_b_in, cols_a_in, cols_b_in)])
    zeta_rows = jnp.where(edges.row8 < 4, surface[24:32, 0:256], surface[0:8, 0:256])
    zeta_cols = surface[8:24, 256:384]

    def wet_at(k):
        return jnp.where(k < bottom, land_ref[k].astype(F32), 0.0)

    early = (w_in, a_in, c_in, theta_drop_in, salt_drop_in, x_open_in, y_open_in, land_in)
    w_ref, a_ref, c_ref, theta_drop_ref, salt_drop_ref, x_open_ref, y_open_ref, _ = [x.first() for x in early]
    share = (0.2, -0.15)
    mu_later = None
    for k in range(depth - 1, -1, -1):
        if k == depth - LEVELS - 1:
            for x in early:
                x.get()
        wet = wet_at(k)
        rise = zeta * w_ref[k]
        mu = (a_ref[k] + share[0] * rise, c_ref[k] + share[1] * rise)
        if k < depth - 1:
            kappa_grad_ref[k] = theta_drop_ref[k] * (mu[0] - mu_later[0]) + salt_drop_ref[k] * (mu[1] - mu_later[1])
        rows = edges.row_pair(8 * k, True)
        row_rise = zeta_rows * edges.tail_rows(k, 0)
        col_rise = zeta_cols * edges.cols(k, 4)
        x_open = x_open_ref[k]
        y_open = y_open_ref[k]
        for n, ref in ((0, theta_grad_ref), (1, salt_grad_ref)):
            wide = jnp.concatenate([mu[n], edges.cols(k, 2 + n) + share[n] * col_rise], axis=1)
            at = 16 * (depth * n + k)
            parts_ref[at : at + 16] = two_parts(y_open * (wide - next_of(wide, 1)))
            wide = jnp.concatenate([mu[n], edges.turned_rows(rows, 2 + n) + share[n] * row_rise], axis=0)
            h = x_open * (wide - next_of(wide, 0))
            pair = h + last_of(h, 0)
            change = (8.0 * pair - last_of(pair, 0) - next_of(pair, 0))[0:16]
            ref[k] = mu[n] - wet * change
        if k == 0:
            forcing_grad_ref[...] = zeta + wet * mu[0]
        mu_later = mu
    kappa_out.send()
    forcing_out.send()
    filtered_ref[...] = jnp.dot(parts_ref[...], filter_in.get()[...], preferred_element_type=F32)
    for n, ref, out in ((0, theta_grad_ref, theta_out), (1, salt_grad_ref, salt_out)):
        for k in range(depth):
            at = 16 * (depth * n + k)
            ref[k] = ref[k] - wet_at(k) * filtered_ref[at : at + 16]
            if k % 5 == 4:
                out.send(k - 4, 5)


def swaps(first):
    return [(i, (i + 1 if (i - first) % 2 == 0 else i - 1) % 16) for i in range(16)]


def shards(
    theta,
    salt,
    velocity_x,
    velocity_y,
    land_mask,
    kappa,
    forcing,
    bottom,
    theta_cot,
    salt_cot,
    surface_cot,
):
    depth = theta.shape[0]
    whole = theta.shape
    place = jnp.stack([lax.axis_index(TROW), lax.axis_index(TCOL)]).astype(jnp.int32)
    lines = 8 * depth + 8 * ((depth + 1) // 2)
    columns = (depth // LEVELS, 16, 128)
    a, c, w, inv, ratio, rows_a, rows_b, cols_a, cols_b = staged(
        columns_kernel,
        (land_mask, kappa, bottom, theta_cot, salt_cot, theta, salt, velocity_x, velocity_y, surface_cot),
        [whole] * 4 + [kappa.shape, (lines + 24, 256), (lines + 24, 256), columns, columns],
        place=place,
        flops=100 * theta.size,
        lead=(0, LEVELS),
        sends=32,
    )
    cols_a = lax.ppermute(cols_a, TCOL, swaps(0))
    cols_b = lax.ppermute(cols_b, TCOL, swaps(1))
    rows_a, rows_b = staged(
        ends_kernel,
        ((cols_a, 0, 2), (cols_b, 0, 2)),
        [rows_a.shape, rows_b.shape],
        place=place,
        into=((rows_a, (lines + 16, 8)), (rows_b, (lines + 16, 8))),
    )
    rows_a = lax.ppermute(rows_a, TROW, swaps(0))
    rows_b = lax.ppermute(rows_b, TROW, swaps(1))
    own, sums = staged(
        krylov_kernel,
        (surface_cot, bottom, (rows_a, lines, 24), (rows_b, lines, 24), (cols_a, 0, 2), (cols_b, 0, 2)),
        [(128, 384), (256, 128)],
        place=place,
    )
    x_open, y_open, theta_drop, salt_drop = staged(
        forward_kernel,
        (land_mask, bottom, rows_a, rows_b, cols_a, cols_b, velocity_x, velocity_y, theta, salt)
        + (stencil(((-1, -1), (0, 7), (1, 7), (2, -1)), 384), forcing, kappa, inv, ratio),
        [(depth, 24, 256), (depth, 16, 384), kappa.shape, kappa.shape],
        place=place,
        flops=200 * theta.size,
        lead=(0, LEVELS),
        sends=16,
        scratch=[((32 * depth, 768), BF16), ((32 * depth, 384), F32), (whole, F32), (whole, F32)],
    )
    sums = lax.all_to_all(sums, ALL, 0, 0, tiled=True)
    return tuple(
        staged(
            backward_kernel,
            (sums, own, land_mask, bottom, rows_a, rows_b, cols_a, cols_b, w, a, c)
            + (theta_drop, salt_drop, x_open, y_open, stencil(((-2, -1), (-1, 7), (0, 7), (1, -1)), 256)),
            [whole, whole, kappa.shape, forcing.shape],
            place=place,
            scratch=[((32 * depth, 768), BF16), ((32 * depth, 256), F32)],
            sends=12,
            lead=(depth - LEVELS, LEVELS),
        )
    )


def solution(mesh):
    split = Mesh(mesh.devices.reshape(4, 2, 2, 2, 8), ALL)
    block = P(None, TROW, TCOL)
    flat = P(TROW, TCOL)
    return jax.shard_map(
        shards,
        mesh=split,
        in_specs=(block,) * 6 + (flat, flat, block, block, flat),
        out_specs=(block, block, block, flat),
        check_vma=False,
    )
```

```python
import math

import jax
import jax.numpy as jnp
import numpy as np
from jax import lax
from jax.experimental import pallas as pl
from jax.experimental.pallas import tpu as pltpu
from jax.sharding import Mesh
from jax.sharding import PartitionSpec as P

TROW = ("trow_0", "trow_1", "trow_2")
TCOL = ("tcol_0", "tcol_1")
ALL = TROW + TCOL
CENTRE = 4.75
KRYLOV = 4
PAIRS = [(i, j) for i in range(KRYLOV) for j in range(i, KRYLOV)]
F32 = jnp.float32
VM = pl.BlockSpec(memory_space=pltpu.VMEM)
SM = pl.BlockSpec(memory_space=pltpu.SMEM)
HB = pl.BlockSpec(memory_space=pltpu.HBM)
PARAMS = pltpu.CompilerParams(vmem_limit_bytes=58 * 1024 * 1024)


def iota(shape, dim):
    return lax.broadcasted_iota(jnp.int32, shape, dim)


def two_sum(a, b):
    s = a + b
    t = s - a
    return s, (a - (s - t)) + (b - t)


def quick_two_sum(a, b):
    s = a + b
    return s, b - (s - a)


def halves(a):
    t = a * 4097.0
    high = t - (t - a)
    return high, a - high


def two_prod(a, b, a_parts, b_parts):
    p = a * b
    ah, al = a_parts
    bh, bl = b_parts
    return p, ((ah * bh - p) + ah * bl + al * bh) + al * bl


def df_add(a, b):
    s, e = two_sum(a[0], b[0])
    return quick_two_sum(s, e + (a[1] + b[1]))


def df_mul(a, b):
    p, e = two_prod(a[0], b[0], halves(a[0]), halves(b[0]))
    return quick_two_sum(p, e + (a[0] * b[1] + a[1] * b[0]))


def df_div(a, b):
    inverse = 1.0 / b[0]
    q1 = a[0] * inverse
    back = df_mul((q1, jnp.zeros_like(q1)), b)
    rest = df_add(a, (-back[0], -back[1]))
    return quick_two_sum(q1, rest[0] * inverse)


class Loaded:
    def __init__(self, source, ref, parts, take_sem):
        self.ref = ref
        self.copies = []
        for part in parts:
            if part is None:
                self.copies.append(pltpu.make_async_copy(source, ref, take_sem()))
            else:
                self.copies.append(pltpu.make_async_copy(source.at[pl.ds(*part)], ref.at[pl.ds(*part)], take_sem()))

    def start(self, n):
        if n < len(self.copies):
            self.copies[n].start()
            self.waiting = list(self.copies)

    def first(self):
        if len(self.waiting) == len(self.copies):
            self.waiting.pop(0).wait()
        return self.ref

    def get(self):
        while self.waiting:
            self.waiting.pop(0).wait()
        return self.ref


class Stored:
    def __init__(self, target, ref, take_sem, pending):
        self.target, self.ref, self.take_sem, self.pending = target, ref, take_sem, pending

    def send(self, start=None, count=None):
        source, target = self.ref, self.target
        if start is not None:
            source, target = source.at[pl.ds(start, count)], target.at[pl.ds(start, count)]
        copy = pltpu.make_async_copy(source, target, self.take_sem())
        copy.start()
        self.pending.append(copy)


def staged(kernel, args, outs, place=None, scratch=(), sends=None, after=(), flops=0, lead=None):
    smem = [] if place is None else [place]

    def parts_of(shape):
        if lead is None or len(shape) < 3 or shape[0] < 24:
            return [None]
        start, stop = lead[0], min(lead[0] + lead[1], shape[0])
        return [(start, stop - start), (0, start) if start else (stop, shape[0] - stop)]

    cuts = [a[1:] if isinstance(a, tuple) else None for a in args]
    args = [a[0] if isinstance(a, tuple) else a for a in args]
    n_in, n_out = len(args), len(outs)
    sends = sends or n_out
    staging = [pltpu.VMEM(a.shape if cut is None else (cut[1],) + a.shape[1:], a.dtype) for a, cut in zip(args, cuts)]
    staging += [pltpu.VMEM(s, F32) for s in outs]

    def body(*refs):
        refs = list(refs)
        places = [refs.pop(0) for _ in smem]
        sources = [refs.pop(0) for _ in range(n_in)]
        sources = [s if cut is None else s.at[pl.ds(*cut)] for s, cut in zip(sources, cuts)]
        for _ in after:
            refs.pop(0)
        targets = [refs.pop(0) for _ in range(n_out)]
        buffers = [refs.pop(0) for _ in range(n_in)]
        holds = [refs.pop(0) for _ in range(n_out)]
        in_sems, out_sems = refs.pop(-2), refs.pop(-1)
        numbers = iter(range(2 * n_in))
        ins = [Loaded(s, b, parts_of(b.shape), lambda: in_sems.at[next(numbers)]) for s, b in zip(sources, buffers)]
        for n in (0, 1):
            for x in ins:
                x.start(n)
        pending = []
        given = []
        for n in range(n_out):
            given.append(Stored(targets[n], holds[n], lambda: out_sems.at[len(pending)], pending))
        kernel(ins, given, *places, *refs)
        for x in ins:
            x.get()
        for copy in pending:
            copy.wait()

    return pl.pallas_call(
        body,
        out_shape=[jax.ShapeDtypeStruct(s, F32) for s in outs],
        in_specs=[SM] * len(smem) + [HB] * (n_in + len(after)),
        out_specs=[HB] * n_out,
        scratch_shapes=staging
        + [pltpu.VMEM(s, t) for s, t in scratch]
        + [pltpu.SemaphoreType.DMA((2 * n_in,)), pltpu.SemaphoreType.DMA((sends,))],
        cost_estimate=pl.CostEstimate(
            flops=flops, bytes_accessed=4 * (sum(a.size for a in args) + sum(map(math.prod, outs))), transcendentals=0
        ),
        compiler_params=PARAMS,
    )(*smem, *args, *after)


def merge_rows(a, b, step):
    shape = a[0].shape
    first = (iota(shape, 0) & step) == 0

    def part(x, y):
        mixed = jnp.where(first, y, x)
        if step == 4:
            other = pltpu.roll(mixed, 4, 0)
        else:
            other = jnp.where(first, pltpu.roll(mixed, 8 - step, 0), pltpu.roll(mixed, step, 0))
        return jnp.where(first, x, y), other

    kept_high, other_high = part(a[0], b[0])
    kept_low, other_low = part(a[1], b[1])
    return df_add((kept_high, kept_low), (other_high, other_low))


def krylov_kernel(ins, outs, place_ref):
    cot_in, bottom_in, rows_in, west_in, east_in, left_in, right_in = ins
    near_out, own_out, sums_out = outs
    near_ref, own_ref, sums_ref = [x.ref for x in outs]
    r = place_ref[0]
    c = place_ref[1]
    shape = (24, 384)
    row = iota(shape, 0)
    lane = iota(shape, 1)
    edge = iota((16, 128), 1)
    inside = ((row >= 8) | (r > 0)) & ((lane < 256) | ((lane < 264) & (c < 15)) | ((lane >= 376) & (c > 0)))
    rows, west, east, left, right = [x.get() for x in ins[2:]]

    def window(main, n):
        at = slice(8 * n, 8 * n + 8)
        ends = jnp.where(edge[0:8] < 64, right[at], left[at])
        sides = jnp.where(edge < 64, pltpu.roll(east[n], 10, 1), pltpu.roll(west[n], 2, 1))
        top = jnp.concatenate([rows[at], ends], axis=1)
        return jnp.concatenate([top, jnp.concatenate([main, sides], axis=1)], axis=0)

    start = jnp.where(inside, window(cot_in.get()[...], 0), 0.0)
    bottom = window(bottom_in.get()[...].astype(F32), 1)
    shifted = (4.2 + bottom / 25.0) - CENTRE

    def apply_shifted(v):
        below = jnp.where(row == 23, 0.0, pltpu.roll(v, 23, 0))
        beside = below + pltpu.roll(v, 1, 0) + pltpu.roll(v, 383, 1) + pltpu.roll(v, 1, 1)
        return jnp.where(inside, shifted * v - beside, 0.0)

    vectors = [start]
    images = []
    for step in range(KRYLOV):
        moved = apply_shifted(vectors[-1])
        images.append(moved + CENTRE * vectors[-1])
        if step == 0:
            vectors.append(moved * 0.25)
        elif step + 1 < KRYLOV:
            vectors.append(moved * 0.5 - vectors[-2])

    for k, v in enumerate(vectors):
        own_ref[24 * k : 24 * k + 24] = v
        near_ref[8 * k : 8 * k + 8] = pltpu.roll(v[0:16], 12, 0)[0:8]
    near_out.send()
    own_out.send()

    domain = (row >= 4) & (row < jnp.where(r == 15, 24, 20))
    cut = [jnp.where(domain, v, 0.0)[:, 0:256] for v in vectors]
    images = [w[:, 0:256] for w in images]
    cut_parts = [halves(v) for v in cut]
    image_parts = [halves(w) for w in images]

    def tile(x, at):
        i, j = divmod(at, 2)
        return x[8 * i : 8 * i + 8, 128 * j : 128 * j + 128]

    def dot(x, x_parts, y, y_parts):
        total = None
        for at in range(6):
            p, e = two_prod(
                tile(x, at),
                tile(y, at),
                [tile(h, at) for h in x_parts],
                [tile(h, at) for h in y_parts],
            )
            if total is None:
                total = (p, e)
            else:
                s, f = two_sum(total[0], p)
                total = (s, total[1] + (e + f))
        return total

    dots = [dot(cut[i], cut_parts[i], images[j], image_parts[j]) for i, j in PAIRS]
    dots += [dot(cut[i], cut_parts[i], cut[0], cut_parts[0]) for i in range(KRYLOV)]
    zero = jnp.zeros((8, 128), F32)
    dots += [(zero, zero)] * (16 - len(dots))
    packed = []
    for base in (0, 8):
        group = dots[base : base + 8]
        for step in (4, 2, 1):
            group = [merge_rows(group[i], group[i + step], step) for i in range(step)]
        total = group[0]
        for step in (64, 32, 16, 8, 4, 2, 1):
            total = df_add(total, (pltpu.roll(total[0], step, 1), pltpu.roll(total[1], step, 1)))
        packed.append(total)
    small_row = iota((8, 128), 0)
    small_lane = iota((8, 128), 1)
    spread = zero
    for part in (0, 1):
        for base in (0, 1):
            chosen = jnp.zeros((8, 128), jnp.bool_)
            for i in range(KRYLOV):
                for j in range(KRYLOV + 1):
                    index = len(PAIRS) + i if j == KRYLOV else PAIRS.index((min(i, j), max(i, j)))
                    if index // 8 == base:
                        chosen = chosen | (
                            (small_row == index % 8) & (small_lane == 32 * part + 8 * i + j)
                        )
            spread = spread + jnp.where(chosen, packed[base][part], 0.0)
    line = jnp.sum(spread, axis=0, keepdims=True)
    sums_ref[...] = jnp.broadcast_to(line, (256, 128))

    sums_out.send()


ROW_TURNS = (0, 4, 2, 6)
FIELDS = 6
LEVELS = 5


def packed_rows(parts, from_above):
    row = iota((8, 256), 0)
    order = (2, 1, 3, 0) if from_above else (0, 2, 1, 3)
    turned = [pltpu.roll(p, t, 0) if t else p for p, t in zip(parts, ROW_TURNS)]
    out = turned[order[3]]
    for n in (2, 1, 0):
        out = jnp.where(row < 2 * n + 2, turned[order[n]], out)
    return out


def packed_cols(parts, spare):
    group = (iota((16, 128), 1) + 2) & 127
    out = spare
    for m in range(len(parts) - 1, -1, -1):
        out = jnp.where(group < 4 * m + 4, pltpu.roll(parts[m], 4 * m, 1) if m else parts[m], out)
    return out


def columns_kernel(ins, outs):
    depth = ins[0].ref.shape[0]
    land_in, kappa_in, bottom_in, tcot_in, scot_in, theta_in, salt_in, ux_in, uy_in, surface_in = ins
    a_out, c_out, w_out, inv_out, ratio_out, down_out, up_out, right_out, left_out, corner_out, cross_out = outs
    a_ref, c_ref, w_ref, inv_ref, ratio_ref, down_ref, up_ref, right_ref, left_ref, corner_ref, cross_ref = [x.ref for x in outs]
    bottom = bottom_in.get()[...]
    lines = 8 * depth + 8 * ((depth + 1) // 2)
    spare = []
    for n, field in enumerate((surface_in.get()[...], bottom.astype(F32))):
        down_ref[lines + 8 * n : lines + 8 * n + 8] = field[8:16]
        spare.append((pltpu.roll(field[:, 128:256], 126, 1), pltpu.roll(field[:, 0:128], 118, 1)))
        corner_ref[8 * n : 8 * n + 8] = field[8:16, 128:256]
        cross_ref[8 * n : 8 * n + 8] = field[8:16, 0:128]
    corner_out.send()
    cross_out.send()
    early = (land_in, kappa_in, tcot_in, scot_in)
    land_ref, kappa_ref, tcot_ref, scot_ref = [x.first() for x in early]

    def wet_at(k):
        return jnp.where(k < bottom, land_ref[k].astype(F32), 0.0)

    wet = wet_at(0)
    ratio = None
    couple_last = None
    state = None
    for k in range(depth):
        if k == LEVELS - 1:
            for x in early:
                x.get()
        diagonal = jnp.ones((16, 256), F32)
        if k > 0:
            diagonal = diagonal + couple_last - couple_last * ratio
        if k < depth - 1:
            wet_next = wet_at(k + 1)
            couple = kappa_ref[k] * wet * wet_next
            diagonal = diagonal + couple
        inverse = 1.0 / diagonal
        rhs = (tcot_ref[k], scot_ref[k], wet)
        if k == 0:
            state = tuple(x * inverse for x in rhs)
        else:
            state = tuple((x + couple_last * s) * inverse for x, s in zip(rhs, state))
        a_ref[k], c_ref[k], w_ref[k] = state
        inv_ref[k] = inverse
        if k < depth - 1:
            ratio = couple * inverse
            ratio_ref[k] = ratio
            couple_last = couple
            wet = wet_next
    inv_out.send()
    ratio_out.send()
    theta_ref = theta_in.get()
    salt_ref = salt_in.get()
    ux_ref = ux_in.get()
    uy_ref = uy_in.get()
    row8 = iota((8, 256), 0)
    lane = iota((16, 128), 1)
    tails = {}
    last_parts, first_parts = [], []
    for k in range(depth - 1, -1, -1):
        wet = wet_at(k)
        if k < depth - 1:
            ratio = ratio_ref[k]
            state = tuple(x + ratio * s for x, s in zip((a_ref[k], c_ref[k], w_ref[k]), state))
            a_ref[k], c_ref[k], w_ref[k] = state
        fields = (theta_ref[k] * wet, salt_ref[k] * wet) + state
        down_ref[8 * k : 8 * k + 8] = packed_rows([f[8:16] for f in fields[:4]], True)
        up_ref[8 * k : 8 * k + 8] = packed_rows([f[0:8] for f in fields[:4]], False)
        flow = ux_ref[k] * wet
        open_low = flow[8:16] * pltpu.roll(wet[8:16], 7, 0)
        open_high = flow[0:8] * pltpu.roll(wet[0:8], 7, 0)
        face_low = jnp.where(row8 == 6, open_low, flow[8:16])
        face_high = jnp.where(row8 == 0, open_high, pltpu.roll(wet[0:8], 1, 0))
        tails[k] = ((state[2][8:16], face_low), (state[2][0:8], face_high))
        if k % 2 == 0:
            later = tails.pop(k + 1, tails[k])
            this = tails.pop(k)
            at = 8 * depth + 4 * k
            down_ref[at : at + 8] = packed_rows(this[0] + later[0], True)
            up_ref[at : at + 8] = packed_rows(this[1] + later[1], False)
        flow = uy_ref[k] * wet
        open_last = flow[:, 128:256] * pltpu.roll(wet[:, 128:256], 127, 1)
        open_first = flow[:, 0:128] * pltpu.roll(wet[:, 0:128], 127, 1)
        last = [f[:, 128:256] for f in fields] + [jnp.where(lane == 126, open_last, flow[:, 128:256])]
        first = [f[:, 0:128] for f in fields] + [
            jnp.where(lane == 0, open_first, pltpu.roll(wet[:, 0:128], 1, 1))
        ]
        last_parts = last + last_parts
        first_parts = first + first_parts
        if k % LEVELS == 0:
            g = k // LEVELS
            right_ref[g] = packed_cols(last_parts, spare[g % 2][0])
            left_ref[g] = packed_cols(first_parts, spare[g % 2][1])
            last_parts, first_parts = [], []
            for out in (a_out, c_out, w_out):
                out.send(k, LEVELS)
    for out in (down_out, right_out, up_out, left_out):
        out.send()


SCALE = 1.0 / 12.0
BF16 = jnp.bfloat16


class Edges:
    def __init__(self, place_ref, depth, above, below, west, east):
        r = place_ref[0]
        c = place_ref[1]
        self.depth, self.above, self.below, self.west, self.east = depth, above, below, west, east
        self.row8 = iota((8, 256), 0)
        self.lane16 = iota((16, 128), 1)
        has_up = jnp.where(r > 0, 1.0, 0.0)
        has_down = jnp.where(r < 15, 1.0, 0.0)
        has_left = jnp.where(c > 0, 1.0, 0.0)
        has_right = jnp.where(c < 15, 1.0, 0.0)
        self.above_rows = (self.row8 & 2) != 0
        self.row_flags = (
            jnp.where(self.above_rows, has_up, has_down),
            jnp.where(self.above_rows, has_down, has_up),
        )
        self.west_lanes = (self.lane16 & 2) != 0
        self.lane_flag = jnp.where(self.west_lanes, has_left, has_right)

    def row_pair(self, at, second):
        above = self.above[at : at + 8]
        below = self.below[at : at + 8]
        if second:
            return jnp.where(self.above_rows, below, above) * self.row_flags[1]
        return jnp.where(self.above_rows, above, below) * self.row_flags[0]

    def turned_rows(self, pair, f):
        turn = (8 - ROW_TURNS[f]) % 8
        return pltpu.roll(pair, turn, 0) if turn else pair

    def tail_rows(self, k, f):
        pair = self.row_pair(8 * self.depth + 8 * (k // 2), k % 2 == 1)
        return self.turned_rows(pair, f + 2 * (k % 2))

    def cols(self, k, f):
        g = k // LEVELS
        pair = jnp.where(self.west_lanes, self.west[g], self.east[g]) * self.lane_flag
        turn = 4 * (FIELDS * (k % LEVELS) + f)
        return pltpu.roll(pair, 128 - turn, 1) if turn else pair


def next_of(x, axis):
    return pltpu.roll(x, x.shape[axis] - 1, axis)


def last_of(x, axis):
    return pltpu.roll(x, 1, axis)


def two_parts(x):
    high = x.astype(BF16)
    return jnp.concatenate([high, (x - high.astype(F32)).astype(BF16)], axis=1)


def stencil(offsets, columns):
    out = np.zeros((384, columns), np.float32)
    for j in range(columns):
        for offset, value in offsets:
            out[(j + offset) % 384, j] += value
    return jnp.asarray(np.concatenate([out, out]), BF16)


def forward_kernel(ins, outs, place_ref, parts_ref, filtered_ref, theta_sweep_ref, salt_sweep_ref):
    (
        land_in,
        bottom_in,
        above_in,
        below_in,
        west_in,
        east_in,
        ux_in,
        uy_in,
        theta_in,
        salt_in,
        filter_in,
        forcing_in,
        kappa_in,
        inv_in,
        ratio_in,
    ) = ins
    x_out, y_out, theta_out, salt_out = outs
    x_open_ref, y_open_ref, theta_drop_ref, salt_drop_ref = [x.ref for x in outs]
    depth = theta_in.ref.shape[0]
    bottom = bottom_in.get()[...]
    land_ref = land_in.first()
    edges = Edges(place_ref, depth, *[x.get() for x in (above_in, below_in, west_in, east_in)])
    row8, lane16 = edges.row8, edges.lane16
    early = (ux_in, uy_in, theta_in, salt_in, land_in)
    ux_ref, uy_ref, theta_ref, salt_ref, _ = [x.first() for x in early]

    def wet_at(k):
        return jnp.where(k < bottom, land_ref[k].astype(F32), 0.0)

    for k in range(depth):
        if k == LEVELS:
            for x in early:
                x.get()
        wet = wet_at(k)
        faces = edges.tail_rows(k, 1)
        wide = jnp.concatenate([wet, pltpu.roll(faces, 7, 0)], axis=0)
        later = next_of(wide, 0)
        x_open = jnp.concatenate(
            [ux_ref[k] * wet * later[0:16], jnp.where(row8 == 7, faces * later[16:24], faces)], axis=0
        )
        x_open_ref[k] = x_open * SCALE
        faces = edges.cols(k, 5)
        wide = jnp.concatenate([wet, pltpu.roll(faces, 127, 1)], axis=1)
        later = next_of(wide, 1)
        y_open = jnp.concatenate(
            [uy_ref[k] * wet * later[:, 0:256], jnp.where(lane16 == 127, faces * later[:, 256:384], faces)], axis=1
        )
        y_open_ref[k] = y_open * SCALE
        for f, ref in ((0, theta_ref), (1, salt_ref)):
            wide = jnp.concatenate([ref[k] * wet, edges.cols(k, f)], axis=1)
            at = 16 * (depth * f + k)
            parts_ref[at : at + 16] = two_parts(wide)
    x_out.send()
    y_out.send()
    filtered_ref[...] = jnp.dot(parts_ref[...], filter_in.get()[...], preferred_element_type=F32)
    forcing_ref, kappa_ref, inv_ref, ratio_ref = [x.get() for x in (forcing_in, kappa_in, inv_in, ratio_in)]

    couple_last = None
    state = None
    wet = wet_at(0)
    for k in range(depth):
        rows = edges.row_pair(8 * k, False)
        x_open = x_open_ref[k]
        y_open = y_open_ref[k]
        advected = []
        for f, ref in ((0, theta_ref), (1, salt_ref)):
            q = ref[k]
            wide = jnp.concatenate([q * wet, edges.turned_rows(rows, f)], axis=0)
            pair = wide + next_of(wide, 0)
            flux = x_open * (8.0 * pair - last_of(pair, 0) - next_of(pair, 0))
            change = (flux - last_of(flux, 0))[0:16]
            at = 16 * (depth * f + k)
            flux = y_open * filtered_ref[at : at + 16]
            change = change + (flux - last_of(flux, 1))[:, 0:256]
            advected.append(q - change)
        if k == 0:
            advected[0] = advected[0] + forcing_ref[...] * wet
        inverse = inv_ref[k]
        if k == 0:
            state = tuple(x * inverse for x in advected)
        else:
            state = tuple((x + couple_last * s) * inverse for x, s in zip(advected, state))
        theta_sweep_ref[k], salt_sweep_ref[k] = state
        if k < depth - 1:
            wet_next = wet_at(k + 1)
            couple_last = kappa_ref[k] * wet * wet_next
            wet = wet_next
    wet_later = wet
    for k in range(depth - 2, -1, -1):
        wet = wet_at(k)
        ratio = ratio_ref[k]
        new = (theta_sweep_ref[k] + ratio * state[0], salt_sweep_ref[k] + ratio * state[1])
        opened = wet * wet_later
        theta_drop_ref[k] = opened * (state[0] - new[0])
        salt_drop_ref[k] = opened * (state[1] - new[1])
        state = new
        wet_later = wet
        if k % LEVELS == 0:
            theta_out.send(k, min(LEVELS, depth - 1 - k))
            salt_out.send(k, min(LEVELS, depth - 1 - k))


def backward_kernel(ins, outs, place_ref, parts_ref, filtered_ref):
    (
        sums_in,
        own_in,
        near_in,
        land_in,
        bottom_in,
        above_in,
        below_in,
        west_in,
        east_in,
        w_in,
        a_in,
        c_in,
        theta_drop_in,
        salt_drop_in,
        x_open_in,
        y_open_in,
        filter_in,
    ) = ins
    theta_out, salt_out, kappa_out, forcing_out = outs
    theta_grad_ref, salt_grad_ref, kappa_grad_ref, forcing_grad_ref = [x.ref for x in outs]
    depth = w_in.ref.shape[0]
    r = place_ref[0]
    has_down = jnp.where(r < 15, 1.0, 0.0)
    sums_ref, own_ref, near_ref = [x.get() for x in (sums_in, own_in, near_in)]

    small = (8, 128)
    small_row = iota(small, 0)
    total = (sums_ref[0:8], jnp.zeros(small, F32))
    for at in range(1, 32):
        s, e = two_sum(total[0], sums_ref[8 * at : 8 * at + 8])
        total = (s, total[1] + e)
    for step in (4, 2, 1):
        s, e = two_sum(total[0], pltpu.roll(total[0], step, 0))
        total = (s, (total[1] + pltpu.roll(total[1], step, 0)) + e)
    low = total[1] + pltpu.roll(total[0] + total[1], 96, 1)
    total = quick_two_sum(total[0], low)

    def as_rows(x):
        out = x
        for i in range(1, KRYLOV):
            out = jnp.where(small_row == i, pltpu.roll(x, 128 - 8 * i, 1), out)
        return out

    system = (as_rows(total[0]), as_rows(total[1]))

    def row_of(x, k):
        return jnp.broadcast_to(x[k : k + 1, :], small)

    def lane_of(x, k):
        return jnp.broadcast_to(x[:, k : k + 1], small)

    keep = []
    weights = []
    scales = [lane_of(row_of(system[0], k), k) for k in range(KRYLOV)]
    for k in range(KRYLOV):
        across = (row_of(system[0], k), row_of(system[1], k))
        pivot = (lane_of(across[0], k), lane_of(across[1], k))
        fine = pivot[0] > 1e-13 * scales[k]
        keep.append(fine)
        pivot = (jnp.where(fine, pivot[0], 1.0), jnp.where(fine, pivot[1], 0.0))
        factor = df_div((lane_of(system[0], k), lane_of(system[1], k)), pivot)
        used = fine & (small_row != k)
        factor = (jnp.where(used, factor[0], 0.0), jnp.where(used, factor[1], 0.0))
        product = df_mul(factor, across)
        system = df_add(system, (-product[0], -product[1]))
    for k in range(KRYLOV):
        pivot = lane_of(row_of(system[0], k), k)
        value = lane_of(row_of(system[0], k), KRYLOV)
        value = jnp.where(keep[k], value / jnp.where(keep[k], pivot, 1.0), 0.0)
        weights.append(value[0:1, 0:1])

    def combined(ref, rows):
        out = weights[0] * ref[0:rows]
        for k in range(1, KRYLOV):
            out = out + weights[k] * ref[rows * k : rows * k + rows]
        return out

    def rows_joined(upper, lower):
        turned = pltpu.roll(lower, 4, 0)
        row8 = iota(turned.shape, 0)
        middle = jnp.where((row8 >= 5) & (r < 15), turned, upper[16:24])
        return jnp.concatenate([upper[0:16], middle, turned * has_down], axis=0)

    surface = rows_joined(combined(own_ref, 24), combined(near_ref, 8))
    zeta = surface[8:24, 0:256]
    bottom = bottom_in.get()[...]
    land_ref = land_in.first()
    edges = Edges(place_ref, depth, *[x.get() for x in (above_in, below_in, west_in, east_in)])
    zeta_rows = jnp.where(edges.row8 < 4, surface[24:32, 0:256], surface[0:8, 0:256])
    zeta_cols = surface[8:24, 256:384]

    def wet_at(k):
        return jnp.where(k < bottom, land_ref[k].astype(F32), 0.0)

    early = (w_in, a_in, c_in, theta_drop_in, salt_drop_in, x_open_in, y_open_in, land_in)
    w_ref, a_ref, c_ref, theta_drop_ref, salt_drop_ref, x_open_ref, y_open_ref, _ = [x.first() for x in early]
    share = (0.2, -0.15)
    mu_later = None
    for k in range(depth - 1, -1, -1):
        if k == depth - LEVELS - 1:
            for x in early:
                x.get()
        wet = wet_at(k)
        rise = zeta * w_ref[k]
        mu = (a_ref[k] + share[0] * rise, c_ref[k] + share[1] * rise)
        if k < depth - 1:
            kappa_grad_ref[k] = theta_drop_ref[k] * (mu[0] - mu_later[0]) + salt_drop_ref[k] * (mu[1] - mu_later[1])
        rows = edges.row_pair(8 * k, True)
        row_rise = zeta_rows * edges.tail_rows(k, 0)
        col_rise = zeta_cols * edges.cols(k, 4)
        x_open = x_open_ref[k]
        y_open = y_open_ref[k]
        for n, ref in ((0, theta_grad_ref), (1, salt_grad_ref)):
            wide = jnp.concatenate([mu[n], edges.cols(k, 2 + n) + share[n] * col_rise], axis=1)
            at = 16 * (depth * n + k)
            parts_ref[at : at + 16] = two_parts(y_open * (wide - next_of(wide, 1)))
            wide = jnp.concatenate([mu[n], edges.turned_rows(rows, 2 + n) + share[n] * row_rise], axis=0)
            h = x_open * (wide - next_of(wide, 0))
            pair = h + last_of(h, 0)
            change = (8.0 * pair - last_of(pair, 0) - next_of(pair, 0))[0:16]
            ref[k] = mu[n] - wet * change
        if k == 0:
            forcing_grad_ref[...] = zeta + wet * mu[0]
        mu_later = mu
    kappa_out.send()
    forcing_out.send()
    filtered_ref[...] = jnp.dot(parts_ref[...], filter_in.get()[...], preferred_element_type=F32)
    for n, ref, out in ((0, theta_grad_ref, theta_out), (1, salt_grad_ref, salt_out)):
        for k in range(depth):
            at = 16 * (depth * n + k)
            ref[k] = ref[k] - wet_at(k) * filtered_ref[at : at + 16]
            if k % 5 == 4:
                out.send(k - 4, 5)


def around(count, step):
    return [(i, (i + step) % count) for i in range(count)]


def across(down, right):
    return [
        (16 * i + j, 16 * ((i + down) % 16) + (j + right) % 16) for i in range(16) for j in range(16)
    ]


def shards(
    theta,
    salt,
    velocity_x,
    velocity_y,
    land_mask,
    kappa,
    forcing,
    bottom,
    theta_cot,
    salt_cot,
    surface_cot,
):
    depth = theta.shape[0]
    whole = theta.shape
    place = jnp.stack([lax.axis_index(TROW), lax.axis_index(TCOL)]).astype(jnp.int32)
    lines = 8 * depth + 8 * ((depth + 1) // 2)
    columns = (depth // LEVELS, 16, 128)
    a, c, w, inv, ratio, down, up, right, left, corner, cross = staged(
        columns_kernel,
        (land_mask, kappa, bottom, theta_cot, salt_cot, theta, salt, velocity_x, velocity_y, surface_cot),
        [whole] * 4
        + [kappa.shape, (lines + 16, 256), (lines, 256), columns, columns, (16, 128), (16, 128)],
        flops=100 * theta.size,
        lead=(0, LEVELS),
        sends=32,
    )
    above = lax.ppermute(down, TROW, around(16, 1))
    west = lax.ppermute(right, TCOL, around(16, 1))
    corner = lax.ppermute(corner, ALL, across(1, 1))
    cross = lax.ppermute(cross, ALL, across(1, -1))
    below = lax.ppermute(up, TROW, around(16, -1))
    east = lax.ppermute(left, TCOL, around(16, -1))
    near, own, sums = staged(
        krylov_kernel,
        (surface_cot, bottom, (above, lines, 16), (west, 0, 2), (east, 0, 2), corner, cross),
        [(32, 384), (96, 384), (256, 128)],
        place=place,
        after=(),
    )
    near = lax.ppermute(near, TROW, around(16, -1))
    x_open, y_open, theta_drop, salt_drop = staged(
        forward_kernel,
        (land_mask, bottom, above, below, west, east, velocity_x, velocity_y, theta, salt)
        + (stencil(((-1, -1), (0, 7), (1, 7), (2, -1)), 384), forcing, kappa, inv, ratio),
        [(depth, 24, 256), (depth, 16, 384), kappa.shape, kappa.shape],
        place=place,
        flops=200 * theta.size,
        lead=(0, LEVELS),
        sends=16,
        scratch=[((32 * depth, 768), BF16), ((32 * depth, 384), F32), (whole, F32), (whole, F32)],
    )
    sums = lax.all_to_all(sums, ALL, 0, 0, tiled=True)
    return tuple(
        staged(
            backward_kernel,
            (sums, own, near, land_mask, bottom, above, below, west, east, w, a, c)
            + (theta_drop, salt_drop, x_open, y_open, stencil(((-2, -1), (-1, 7), (0, 7), (1, -1)), 256)),
            [whole, whole, kappa.shape, forcing.shape],
            place=place,
            scratch=[((32 * depth, 768), BF16), ((32 * depth, 256), F32)],
            sends=12,
            lead=(depth - LEVELS, LEVELS),
        )
    )


def solution(mesh):
    split = Mesh(mesh.devices.reshape(4, 2, 2, 2, 8), ALL)
    block = P(None, TROW, TCOL)
    flat = P(TROW, TCOL)
    return jax.shard_map(
        shards,
        mesh=split,
        in_specs=(block,) * 6 + (flat, flat, block, block, flat),
        out_specs=(block, block, block, flat),
        check_vma=False,
    )
```

```python
import math

import jax
import jax.numpy as jnp
import numpy as np
from jax import lax
from jax.experimental import pallas as pl
from jax.experimental.pallas import tpu as pltpu
from jax.sharding import Mesh
from jax.sharding import PartitionSpec as P

TROW = ("trow_0", "trow_1", "trow_2")
TCOL = ("tcol_0", "tcol_1")
ALL = TROW + TCOL
CENTRE = 4.75
KRYLOV = 4
PAIRS = [(i, j) for i in range(KRYLOV) for j in range(i, KRYLOV)]
F32 = jnp.float32
VM = pl.BlockSpec(memory_space=pltpu.VMEM)
SM = pl.BlockSpec(memory_space=pltpu.SMEM)
HB = pl.BlockSpec(memory_space=pltpu.HBM)
PARAMS = pltpu.CompilerParams(vmem_limit_bytes=58 * 1024 * 1024)


def iota(shape, dim):
    return lax.broadcasted_iota(jnp.int32, shape, dim)


def two_sum(a, b):
    s = a + b
    t = s - a
    return s, (a - (s - t)) + (b - t)


def quick_two_sum(a, b):
    s = a + b
    return s, b - (s - a)


def halves(a):
    t = a * 4097.0
    high = t - (t - a)
    return high, a - high


def two_prod(a, b, a_parts, b_parts):
    p = a * b
    ah, al = a_parts
    bh, bl = b_parts
    return p, ((ah * bh - p) + ah * bl + al * bh) + al * bl


def df_add(a, b):
    s, e = two_sum(a[0], b[0])
    return quick_two_sum(s, e + (a[1] + b[1]))


def df_mul(a, b):
    p, e = two_prod(a[0], b[0], halves(a[0]), halves(b[0]))
    return quick_two_sum(p, e + (a[0] * b[1] + a[1] * b[0]))


def df_div(a, b):
    inverse = 1.0 / b[0]
    q1 = a[0] * inverse
    back = df_mul((q1, jnp.zeros_like(q1)), b)
    rest = df_add(a, (-back[0], -back[1]))
    return quick_two_sum(q1, rest[0] * inverse)


class Loaded:
    def __init__(self, source, ref, parts, take_sem):
        self.ref = ref
        self.copies = []
        for part in parts:
            if part is None:
                self.copies.append(pltpu.make_async_copy(source, ref, take_sem()))
            else:
                self.copies.append(pltpu.make_async_copy(source.at[pl.ds(*part)], ref.at[pl.ds(*part)], take_sem()))

    def start(self, n):
        if n < len(self.copies):
            self.copies[n].start()
            self.waiting = list(self.copies)

    def first(self):
        if len(self.waiting) == len(self.copies):
            self.waiting.pop(0).wait()
        return self.ref

    def get(self):
        while self.waiting:
            self.waiting.pop(0).wait()
        return self.ref


class Stored:
    def __init__(self, target, ref, take_sem, pending):
        self.target, self.ref, self.take_sem, self.pending = target, ref, take_sem, pending

    def send(self, start=None, count=None):
        source, target = self.ref, self.target
        if start is not None:
            source, target = source.at[pl.ds(start, count)], target.at[pl.ds(start, count)]
        copy = pltpu.make_async_copy(source, target, self.take_sem())
        copy.start()
        self.pending.append(copy)


def staged(kernel, args, outs, place=None, scratch=(), sends=None, after=(), flops=0, lead=None):
    smem = [] if place is None else [place]

    def parts_of(shape):
        if lead is None or len(shape) < 3 or shape[0] < 24:
            return [None]
        start, stop = lead[0], min(lead[0] + lead[1], shape[0])
        return [(start, stop - start), (0, start) if start else (stop, shape[0] - stop)]

    cuts = [a[1:] if isinstance(a, tuple) else None for a in args]
    args = [a[0] if isinstance(a, tuple) else a for a in args]
    n_in, n_out = len(args), len(outs)
    sends = sends or n_out
    staging = [pltpu.VMEM(a.shape if cut is None else (cut[1],) + a.shape[1:], a.dtype) for a, cut in zip(args, cuts)]
    staging += [pltpu.VMEM(s, F32) for s in outs]

    def body(*refs):
        refs = list(refs)
        places = [refs.pop(0) for _ in smem]
        sources = [refs.pop(0) for _ in range(n_in)]
        sources = [s if cut is None else s.at[pl.ds(*cut)] for s, cut in zip(sources, cuts)]
        for _ in after:
            refs.pop(0)
        targets = [refs.pop(0) for _ in range(n_out)]
        buffers = [refs.pop(0) for _ in range(n_in)]
        holds = [refs.pop(0) for _ in range(n_out)]
        in_sems, out_sems = refs.pop(-2), refs.pop(-1)
        numbers = iter(range(2 * n_in))
        ins = [Loaded(s, b, parts_of(b.shape), lambda: in_sems.at[next(numbers)]) for s, b in zip(sources, buffers)]
        for n in (0, 1):
            for x in ins:
                x.start(n)
        pending = []
        given = []
        for n in range(n_out):
            given.append(Stored(targets[n], holds[n], lambda: out_sems.at[len(pending)], pending))
        kernel(ins, given, *places, *refs)
        for x in ins:
            x.get()
        for copy in pending:
            copy.wait()

    return pl.pallas_call(
        body,
        out_shape=[jax.ShapeDtypeStruct(s, F32) for s in outs],
        in_specs=[SM] * len(smem) + [HB] * (n_in + len(after)),
        out_specs=[HB] * n_out,
        scratch_shapes=staging
        + [pltpu.VMEM(s, t) for s, t in scratch]
        + [pltpu.SemaphoreType.DMA((2 * n_in,)), pltpu.SemaphoreType.DMA((sends,))],
        cost_estimate=pl.CostEstimate(
            flops=flops, bytes_accessed=4 * (sum(a.size for a in args) + sum(map(math.prod, outs))), transcendentals=0
        ),
        compiler_params=PARAMS,
    )(*smem, *args, *after)


def merge_rows(a, b, step):
    shape = a[0].shape
    first = (iota(shape, 0) & step) == 0

    def part(x, y):
        mixed = jnp.where(first, y, x)
        if step == 4:
            other = pltpu.roll(mixed, 4, 0)
        else:
            other = jnp.where(first, pltpu.roll(mixed, 8 - step, 0), pltpu.roll(mixed, step, 0))
        return jnp.where(first, x, y), other

    kept_high, other_high = part(a[0], b[0])
    kept_low, other_low = part(a[1], b[1])
    return df_add((kept_high, kept_low), (other_high, other_low))


def krylov_kernel(ins, outs, place_ref):
    cot_in, bottom_in, rows_in, west_in, east_in, left_in, right_in = ins
    near_out, own_out, sums_out = outs
    near_ref, own_ref, sums_ref = [x.ref for x in outs]
    r = place_ref[0]
    c = place_ref[1]
    shape = (24, 384)
    row = iota(shape, 0)
    lane = iota(shape, 1)
    edge = iota((16, 128), 1)
    inside = ((row >= 8) | (r > 0)) & ((lane < 256) | ((lane < 264) & (c < 15)) | ((lane >= 376) & (c > 0)))
    rows, west, east, left, right = [x.get() for x in ins[2:]]

    def window(main, n):
        at = slice(8 * n, 8 * n + 8)
        ends = jnp.where(edge[0:8] < 64, right[at], left[at])
        sides = jnp.where(edge < 64, pltpu.roll(east[n], 10, 1), pltpu.roll(west[n], 2, 1))
        top = jnp.concatenate([rows[at], ends], axis=1)
        return jnp.concatenate([top, jnp.concatenate([main, sides], axis=1)], axis=0)

    start = jnp.where(inside, window(cot_in.get()[...], 0), 0.0)
    bottom = window(bottom_in.get()[...].astype(F32), 1)
    shifted = (4.2 + bottom / 25.0) - CENTRE

    def apply_shifted(v):
        below = jnp.where(row == 23, 0.0, pltpu.roll(v, 23, 0))
        beside = below + pltpu.roll(v, 1, 0) + pltpu.roll(v, 383, 1) + pltpu.roll(v, 1, 1)
        return jnp.where(inside, shifted * v - beside, 0.0)

    vectors = [start]
    images = []
    for step in range(KRYLOV):
        moved = apply_shifted(vectors[-1])
        images.append(moved + CENTRE * vectors[-1])
        if step == 0:
            vectors.append(moved * 0.25)
        elif step + 1 < KRYLOV:
            vectors.append(moved * 0.5 - vectors[-2])

    for k, v in enumerate(vectors):
        own_ref[24 * k : 24 * k + 24] = v
        near_ref[8 * k : 8 * k + 8] = pltpu.roll(v[0:16], 12, 0)[0:8]
    near_out.send()
    own_out.send()

    domain = (row >= 4) & (row < jnp.where(r == 15, 24, 20))
    cut = [jnp.where(domain, v, 0.0)[:, 0:256] for v in vectors]
    images = [w[:, 0:256] for w in images]
    cut_parts = [halves(v) for v in cut]
    image_parts = [halves(w) for w in images]

    def tile(x, at):
        i, j = divmod(at, 2)
        return x[8 * i : 8 * i + 8, 128 * j : 128 * j + 128]

    def dot(x, x_parts, y, y_parts):
        total = None
        for at in range(6):
            p, e = two_prod(
                tile(x, at),
                tile(y, at),
                [tile(h, at) for h in x_parts],
                [tile(h, at) for h in y_parts],
            )
            if total is None:
                total = (p, e)
            else:
                s, f = two_sum(total[0], p)
                total = (s, total[1] + (e + f))
        return total

    dots = [dot(cut[i], cut_parts[i], images[j], image_parts[j]) for i, j in PAIRS]
    dots += [dot(cut[i], cut_parts[i], cut[0], cut_parts[0]) for i in range(KRYLOV)]
    zero = jnp.zeros((8, 128), F32)
    dots += [(zero, zero)] * (16 - len(dots))
    packed = []
    for base in (0, 8):
        group = dots[base : base + 8]
        for step in (4, 2, 1):
            group = [merge_rows(group[i], group[i + step], step) for i in range(step)]
        total = group[0]
        for step in (64, 32, 16, 8, 4, 2, 1):
            total = df_add(total, (pltpu.roll(total[0], step, 1), pltpu.roll(total[1], step, 1)))
        packed.append(total)
    small_row = iota((8, 128), 0)
    small_lane = iota((8, 128), 1)
    spread = zero
    for part in (0, 1):
        for base in (0, 1):
            chosen = jnp.zeros((8, 128), jnp.bool_)
            for i in range(KRYLOV):
                for j in range(KRYLOV + 1):
                    index = len(PAIRS) + i if j == KRYLOV else PAIRS.index((min(i, j), max(i, j)))
                    if index // 8 == base:
                        chosen = chosen | (
                            (small_row == index % 8) & (small_lane == 32 * part + 8 * i + j)
                        )
            spread = spread + jnp.where(chosen, packed[base][part], 0.0)
    line = jnp.sum(spread, axis=0, keepdims=True)
    sums_ref[...] = jnp.broadcast_to(line, (256, 128))

    sums_out.send()


ROW_TURNS = (0, 4, 2, 6)
FIELDS = 6
LEVELS = 5


def packed_rows(parts, from_above):
    row = iota((8, 256), 0)
    order = (2, 1, 3, 0) if from_above else (0, 2, 1, 3)
    turned = [pltpu.roll(p, t, 0) if t else p for p, t in zip(parts, ROW_TURNS)]
    out = turned[order[3]]
    for n in (2, 1, 0):
        out = jnp.where(row < 2 * n + 2, turned[order[n]], out)
    return out


def packed_cols(parts, spare):
    group = (iota((16, 128), 1) + 2) & 127
    out = spare
    for m in range(len(parts) - 1, -1, -1):
        out = jnp.where(group < 4 * m + 4, pltpu.roll(parts[m], 4 * m, 1) if m else parts[m], out)
    return out


def columns_kernel(ins, outs):
    depth = ins[0].ref.shape[0]
    land_in, kappa_in, bottom_in, tcot_in, scot_in, theta_in, salt_in, ux_in, uy_in, surface_in = ins
    a_out, c_out, w_out, inv_out, ratio_out, down_out, up_out, right_out, left_out, corner_out = outs
    a_ref, c_ref, w_ref, inv_ref, ratio_ref, down_ref, up_ref, right_ref, left_ref, corner_ref = [x.ref for x in outs]
    bottom = bottom_in.get()[...]
    lines = 8 * depth + 8 * ((depth + 1) // 2)
    spare = []
    for n, field in enumerate((surface_in.get()[...], bottom.astype(F32))):
        down_ref[lines + 8 * n : lines + 8 * n + 8] = field[8:16]
        spare.append((pltpu.roll(field[:, 128:256], 126, 1), pltpu.roll(field[:, 0:128], 118, 1)))
        corner_ref[8 * n : 8 * n + 8] = field[8:16, 128:256]
    corner_out.send()
    early = (land_in, kappa_in, tcot_in, scot_in)
    land_ref, kappa_ref, tcot_ref, scot_ref = [x.first() for x in early]

    def wet_at(k):
        return jnp.where(k < bottom, land_ref[k].astype(F32), 0.0)

    wet = wet_at(0)
    ratio = None
    couple_last = None
    state = None
    for k in range(depth):
        if k == LEVELS - 1:
            for x in early:
                x.get()
        diagonal = jnp.ones((16, 256), F32)
        if k > 0:
            diagonal = diagonal + couple_last - couple_last * ratio
        if k < depth - 1:
            wet_next = wet_at(k + 1)
            couple = kappa_ref[k] * wet * wet_next
            diagonal = diagonal + couple
        inverse = 1.0 / diagonal
        rhs = (tcot_ref[k], scot_ref[k], wet)
        if k == 0:
            state = tuple(x * inverse for x in rhs)
        else:
            state = tuple((x + couple_last * s) * inverse for x, s in zip(rhs, state))
        a_ref[k], c_ref[k], w_ref[k] = state
        inv_ref[k] = inverse
        if k < depth - 1:
            ratio = couple * inverse
            ratio_ref[k] = ratio
            couple_last = couple
            wet = wet_next
    inv_out.send()
    ratio_out.send()
    theta_ref = theta_in.get()
    salt_ref = salt_in.get()
    ux_ref = ux_in.get()
    uy_ref = uy_in.get()
    row8 = iota((8, 256), 0)
    lane = iota((16, 128), 1)
    tails = {}
    last_parts, first_parts = [], []
    for k in range(depth - 1, -1, -1):
        wet = wet_at(k)
        if k < depth - 1:
            ratio = ratio_ref[k]
            state = tuple(x + ratio * s for x, s in zip((a_ref[k], c_ref[k], w_ref[k]), state))
            a_ref[k], c_ref[k], w_ref[k] = state
        fields = (theta_ref[k] * wet, salt_ref[k] * wet) + state
        down_ref[8 * k : 8 * k + 8] = packed_rows([f[8:16] for f in fields[:4]], True)
        up_ref[8 * k : 8 * k + 8] = packed_rows([f[0:8] for f in fields[:4]], False)
        flow = ux_ref[k] * wet
        open_low = flow[8:16] * pltpu.roll(wet[8:16], 7, 0)
        open_high = flow[0:8] * pltpu.roll(wet[0:8], 7, 0)
        face_low = jnp.where(row8 == 6, open_low, flow[8:16])
        face_high = jnp.where(row8 == 0, open_high, pltpu.roll(wet[0:8], 1, 0))
        tails[k] = ((state[2][8:16], face_low), (state[2][0:8], face_high))
        if k % 2 == 0:
            later = tails.pop(k + 1, tails[k])
            this = tails.pop(k)
            at = 8 * depth + 4 * k
            down_ref[at : at + 8] = packed_rows(this[0] + later[0], True)
            up_ref[at : at + 8] = packed_rows(this[1] + later[1], False)
        flow = uy_ref[k] * wet
        open_last = flow[:, 128:256] * pltpu.roll(wet[:, 128:256], 127, 1)
        open_first = flow[:, 0:128] * pltpu.roll(wet[:, 0:128], 127, 1)
        last = [f[:, 128:256] for f in fields] + [jnp.where(lane == 126, open_last, flow[:, 128:256])]
        first = [f[:, 0:128] for f in fields] + [
            jnp.where(lane == 0, open_first, pltpu.roll(wet[:, 0:128], 1, 1))
        ]
        last_parts = last + last_parts
        first_parts = first + first_parts
        if k % LEVELS == 0:
            g = k // LEVELS
            right_ref[g] = packed_cols(last_parts, spare[g % 2][0])
            left_ref[g] = packed_cols(first_parts, spare[g % 2][1])
            last_parts, first_parts = [], []
            for out in (a_out, c_out, w_out):
                out.send(k, LEVELS)
    for out in (down_out, right_out, up_out, left_out):
        out.send()


SCALE = 1.0 / 12.0
BF16 = jnp.bfloat16


class Edges:
    def __init__(self, place_ref, depth, above, below, west, east):
        r = place_ref[0]
        c = place_ref[1]
        self.depth, self.above, self.below, self.west, self.east = depth, above, below, west, east
        self.row8 = iota((8, 256), 0)
        self.lane16 = iota((16, 128), 1)
        has_up = jnp.where(r > 0, 1.0, 0.0)
        has_down = jnp.where(r < 15, 1.0, 0.0)
        has_left = jnp.where(c > 0, 1.0, 0.0)
        has_right = jnp.where(c < 15, 1.0, 0.0)
        self.above_rows = (self.row8 & 2) != 0
        self.row_flags = (
            jnp.where(self.above_rows, has_up, has_down),
            jnp.where(self.above_rows, has_down, has_up),
        )
        self.west_lanes = (self.lane16 & 2) != 0
        self.lane_flag = jnp.where(self.west_lanes, has_left, has_right)

    def row_pair(self, at, second):
        above = self.above[at : at + 8]
        below = self.below[at : at + 8]
        if second:
            return jnp.where(self.above_rows, below, above) * self.row_flags[1]
        return jnp.where(self.above_rows, above, below) * self.row_flags[0]

    def turned_rows(self, pair, f):
        turn = (8 - ROW_TURNS[f]) % 8
        return pltpu.roll(pair, turn, 0) if turn else pair

    def tail_rows(self, k, f):
        pair = self.row_pair(8 * self.depth + 8 * (k // 2), k % 2 == 1)
        return self.turned_rows(pair, f + 2 * (k % 2))

    def cols(self, k, f):
        g = k // LEVELS
        pair = jnp.where(self.west_lanes, self.west[g], self.east[g]) * self.lane_flag
        turn = 4 * (FIELDS * (k % LEVELS) + f)
        return pltpu.roll(pair, 128 - turn, 1) if turn else pair


def next_of(x, axis):
    return pltpu.roll(x, x.shape[axis] - 1, axis)


def last_of(x, axis):
    return pltpu.roll(x, 1, axis)


def two_parts(x):
    high = x.astype(BF16)
    return jnp.concatenate([high, (x - high.astype(F32)).astype(BF16)], axis=1)


def stencil(offsets, columns):
    out = np.zeros((384, columns), np.float32)
    for j in range(columns):
        for offset, value in offsets:
            out[(j + offset) % 384, j] += value
    return jnp.asarray(np.concatenate([out, out]), BF16)


def forward_kernel(ins, outs, place_ref, parts_ref, filtered_ref, theta_sweep_ref, salt_sweep_ref):
    (
        land_in,
        bottom_in,
        above_in,
        below_in,
        west_in,
        east_in,
        ux_in,
        uy_in,
        theta_in,
        salt_in,
        filter_in,
        forcing_in,
        kappa_in,
        inv_in,
        ratio_in,
    ) = ins
    x_out, y_out, theta_out, salt_out = outs
    x_open_ref, y_open_ref, theta_drop_ref, salt_drop_ref = [x.ref for x in outs]
    depth = theta_in.ref.shape[0]
    bottom = bottom_in.get()[...]
    land_ref = land_in.first()
    edges = Edges(place_ref, depth, *[x.get() for x in (above_in, below_in, west_in, east_in)])
    row8, lane16 = edges.row8, edges.lane16
    early = (ux_in, uy_in, theta_in, salt_in, land_in)
    ux_ref, uy_ref, theta_ref, salt_ref, _ = [x.first() for x in early]

    def wet_at(k):
        return jnp.where(k < bottom, land_ref[k].astype(F32), 0.0)

    for k in range(depth):
        if k == LEVELS:
            for x in early:
                x.get()
        wet = wet_at(k)
        faces = edges.tail_rows(k, 1)
        wide = jnp.concatenate([wet, pltpu.roll(faces, 7, 0)], axis=0)
        later = next_of(wide, 0)
        x_open = jnp.concatenate(
            [ux_ref[k] * wet * later[0:16], jnp.where(row8 == 7, faces * later[16:24], faces)], axis=0
        )
        x_open_ref[k] = x_open * SCALE
        faces = edges.cols(k, 5)
        wide = jnp.concatenate([wet, pltpu.roll(faces, 127, 1)], axis=1)
        later = next_of(wide, 1)
        y_open = jnp.concatenate(
            [uy_ref[k] * wet * later[:, 0:256], jnp.where(lane16 == 127, faces * later[:, 256:384], faces)], axis=1
        )
        y_open_ref[k] = y_open * SCALE
        for f, ref in ((0, theta_ref), (1, salt_ref)):
            wide = jnp.concatenate([ref[k] * wet, edges.cols(k, f)], axis=1)
            at = 16 * (depth * f + k)
            parts_ref[at : at + 16] = two_parts(wide)
    x_out.send()
    y_out.send()
    filtered_ref[...] = jnp.dot(parts_ref[...], filter_in.get()[...], preferred_element_type=F32)
    forcing_ref, kappa_ref, inv_ref, ratio_ref = [x.get() for x in (forcing_in, kappa_in, inv_in, ratio_in)]

    couple_last = None
    state = None
    wet = wet_at(0)
    for k in range(depth):
        rows = edges.row_pair(8 * k, False)
        x_open = x_open_ref[k]
        y_open = y_open_ref[k]
        advected = []
        for f, ref in ((0, theta_ref), (1, salt_ref)):
            q = ref[k]
            wide = jnp.concatenate([q * wet, edges.turned_rows(rows, f)], axis=0)
            pair = wide + next_of(wide, 0)
            flux = x_open * (8.0 * pair - last_of(pair, 0) - next_of(pair, 0))
            change = (flux - last_of(flux, 0))[0:16]
            at = 16 * (depth * f + k)
            flux = y_open * filtered_ref[at : at + 16]
            change = change + (flux - last_of(flux, 1))[:, 0:256]
            advected.append(q - change)
        if k == 0:
            advected[0] = advected[0] + forcing_ref[...] * wet
        inverse = inv_ref[k]
        if k == 0:
            state = tuple(x * inverse for x in advected)
        else:
            state = tuple((x + couple_last * s) * inverse for x, s in zip(advected, state))
        theta_sweep_ref[k], salt_sweep_ref[k] = state
        if k < depth - 1:
            wet_next = wet_at(k + 1)
            couple_last = kappa_ref[k] * wet * wet_next
            wet = wet_next
    wet_later = wet
    for k in range(depth - 2, -1, -1):
        wet = wet_at(k)
        ratio = ratio_ref[k]
        new = (theta_sweep_ref[k] + ratio * state[0], salt_sweep_ref[k] + ratio * state[1])
        opened = wet * wet_later
        theta_drop_ref[k] = opened * (state[0] - new[0])
        salt_drop_ref[k] = opened * (state[1] - new[1])
        state = new
        wet_later = wet
        if k % LEVELS == 0:
            theta_out.send(k, min(LEVELS, depth - 1 - k))
            salt_out.send(k, min(LEVELS, depth - 1 - k))


def backward_kernel(ins, outs, place_ref, parts_ref, filtered_ref):
    (
        sums_in,
        own_in,
        near_in,
        land_in,
        bottom_in,
        above_in,
        below_in,
        west_in,
        east_in,
        w_in,
        a_in,
        c_in,
        theta_drop_in,
        salt_drop_in,
        x_open_in,
        y_open_in,
        filter_in,
    ) = ins
    theta_out, salt_out, kappa_out, forcing_out = outs
    theta_grad_ref, salt_grad_ref, kappa_grad_ref, forcing_grad_ref = [x.ref for x in outs]
    depth = w_in.ref.shape[0]
    r = place_ref[0]
    has_down = jnp.where(r < 15, 1.0, 0.0)
    sums_ref, own_ref, near_ref = [x.get() for x in (sums_in, own_in, near_in)]

    small = (8, 128)
    small_row = iota(small, 0)
    terms = [(sums_ref[8 * at : 8 * at + 8], None) for at in range(32)]
    while len(terms) > 1:
        joined = []
        for x, y in zip(terms[::2], terms[1::2]):
            s, e = two_sum(x[0], y[0])
            joined.append((s, e if x[1] is None else (x[1] + y[1]) + e))
        terms = joined
    total = terms[0]
    for step in (4, 2, 1):
        s, e = two_sum(total[0], pltpu.roll(total[0], step, 0))
        total = (s, (total[1] + pltpu.roll(total[1], step, 0)) + e)
    low = total[1] + pltpu.roll(total[0] + total[1], 96, 1)
    total = quick_two_sum(total[0], low)

    def as_rows(x):
        out = x
        for i in range(1, KRYLOV):
            out = jnp.where(small_row == i, pltpu.roll(x, 128 - 8 * i, 1), out)
        return out

    system = (as_rows(total[0]), as_rows(total[1]))

    def row_of(x, k):
        return jnp.broadcast_to(x[k : k + 1, :], small)

    def lane_of(x, k):
        return jnp.broadcast_to(x[:, k : k + 1], small)

    keep = []
    weights = []
    scales = [lane_of(row_of(system[0], k), k) for k in range(KRYLOV)]
    for k in range(KRYLOV):
        across = (row_of(system[0], k), row_of(system[1], k))
        pivot = (lane_of(across[0], k), lane_of(across[1], k))
        fine = pivot[0] > 1e-13 * scales[k]
        keep.append(fine)
        pivot = (jnp.where(fine, pivot[0], 1.0), jnp.where(fine, pivot[1], 0.0))
        factor = df_div((lane_of(system[0], k), lane_of(system[1], k)), pivot)
        used = fine & (small_row != k)
        factor = (jnp.where(used, factor[0], 0.0), jnp.where(used, factor[1], 0.0))
        product = df_mul(factor, across)
        system = df_add(system, (-product[0], -product[1]))
    for k in range(KRYLOV):
        pivot = lane_of(row_of(system[0], k), k)
        value = lane_of(row_of(system[0], k), KRYLOV)
        value = jnp.where(keep[k], value / jnp.where(keep[k], pivot, 1.0), 0.0)
        weights.append(value[0:1, 0:1])

    def combined(ref, rows):
        out = weights[0] * ref[0:rows]
        for k in range(1, KRYLOV):
            out = out + weights[k] * ref[rows * k : rows * k + rows]
        return out

    def rows_joined(upper, lower):
        turned = pltpu.roll(lower, 4, 0)
        row8 = iota(turned.shape, 0)
        middle = jnp.where((row8 >= 5) & (r < 15), turned, upper[16:24])
        return jnp.concatenate([upper[0:16], middle, turned * has_down], axis=0)

    surface = rows_joined(combined(own_ref, 24), combined(near_ref, 8))
    zeta = surface[8:24, 0:256]
    bottom = bottom_in.get()[...]
    land_ref = land_in.first()
    edges = Edges(place_ref, depth, *[x.get() for x in (above_in, below_in, west_in, east_in)])
    zeta_rows = jnp.where(edges.row8 < 4, surface[24:32, 0:256], surface[0:8, 0:256])
    zeta_cols = surface[8:24, 256:384]

    def wet_at(k):
        return jnp.where(k < bottom, land_ref[k].astype(F32), 0.0)

    early = (w_in, a_in, c_in, theta_drop_in, salt_drop_in, x_open_in, y_open_in, land_in)
    w_ref, a_ref, c_ref, theta_drop_ref, salt_drop_ref, x_open_ref, y_open_ref, _ = [x.first() for x in early]
    share = (0.2, -0.15)
    mu_later = None
    for k in range(depth - 1, -1, -1):
        if k == depth - LEVELS - 1:
            for x in early:
                x.get()
        wet = wet_at(k)
        rise = zeta * w_ref[k]
        mu = (a_ref[k] + share[0] * rise, c_ref[k] + share[1] * rise)
        if k < depth - 1:
            kappa_grad_ref[k] = theta_drop_ref[k] * (mu[0] - mu_later[0]) + salt_drop_ref[k] * (mu[1] - mu_later[1])
        rows = edges.row_pair(8 * k, True)
        row_rise = zeta_rows * edges.tail_rows(k, 0)
        col_rise = zeta_cols * edges.cols(k, 4)
        x_open = x_open_ref[k]
        y_open = y_open_ref[k]
        for n, ref in ((0, theta_grad_ref), (1, salt_grad_ref)):
            wide = jnp.concatenate([mu[n], edges.cols(k, 2 + n) + share[n] * col_rise], axis=1)
            at = 16 * (depth * n + k)
            parts_ref[at : at + 16] = two_parts(y_open * (wide - next_of(wide, 1)))
            wide = jnp.concatenate([mu[n], edges.turned_rows(rows, 2 + n) + share[n] * row_rise], axis=0)
            h = x_open * (wide - next_of(wide, 0))
            pair = h + last_of(h, 0)
            change = (8.0 * pair - last_of(pair, 0) - next_of(pair, 0))[0:16]
            ref[k] = mu[n] - wet * change
        if k == 0:
            forcing_grad_ref[...] = zeta + wet * mu[0]
        mu_later = mu
    kappa_out.send()
    forcing_out.send()
    filtered_ref[...] = jnp.dot(parts_ref[...], filter_in.get()[...], preferred_element_type=F32)
    for n, ref, out in ((0, theta_grad_ref, theta_out), (1, salt_grad_ref, salt_out)):
        for k in range(depth):
            at = 16 * (depth * n + k)
            ref[k] = ref[k] - wet_at(k) * filtered_ref[at : at + 16]
            if k % 5 == 4:
                out.send(k - 4, 5)


def around(count, step):
    return [(i, (i + step) % count) for i in range(count)]


def across(down, right):
    return [
        (16 * i + j, 16 * ((i + down) % 16) + (j + right) % 16) for i in range(16) for j in range(16)
    ]


def shards(
    theta,
    salt,
    velocity_x,
    velocity_y,
    land_mask,
    kappa,
    forcing,
    bottom,
    theta_cot,
    salt_cot,
    surface_cot,
):
    depth = theta.shape[0]
    whole = theta.shape
    place = jnp.stack([lax.axis_index(TROW), lax.axis_index(TCOL)]).astype(jnp.int32)
    lines = 8 * depth + 8 * ((depth + 1) // 2)
    columns = (depth // LEVELS, 16, 128)
    cross = jnp.concatenate([surface_cot[8:16, 0:128], bottom[8:16, 0:128].astype(F32)])
    cross = lax.ppermute(cross, ALL, across(1, -1))
    a, c, w, inv, ratio, down, up, right, left, corner = staged(
        columns_kernel,
        (land_mask, kappa, bottom, theta_cot, salt_cot, theta, salt, velocity_x, velocity_y, surface_cot),
        [whole] * 4
        + [kappa.shape, (lines + 16, 256), (lines, 256), columns, columns, (16, 128)],
        flops=100 * theta.size,
        lead=(0, LEVELS),
        sends=32,
    )
    down, up, right, left, corner, cross = lax.optimization_barrier((down, up, right, left, corner, cross))
    above = lax.ppermute(down, TROW, around(16, 1))
    west = lax.ppermute(right, TCOL, around(16, 1))
    corner = lax.ppermute(corner, ALL, across(1, 1))
    below = lax.ppermute(up, TROW, around(16, -1))
    east = lax.ppermute(left, TCOL, around(16, -1))
    near, own, sums = staged(
        krylov_kernel,
        (surface_cot, bottom, (above, lines, 16), (west, 0, 2), (east, 0, 2), corner, cross),
        [(32, 384), (96, 384), (256, 128)],
        place=place,
        after=(),
    )
    near = lax.ppermute(near, TROW, around(16, -1))
    x_open, y_open, theta_drop, salt_drop = staged(
        forward_kernel,
        (land_mask, bottom, above, below, west, east, velocity_x, velocity_y, theta, salt)
        + (stencil(((-1, -1), (0, 7), (1, 7), (2, -1)), 384), forcing, kappa, inv, ratio),
        [(depth, 24, 256), (depth, 16, 384), kappa.shape, kappa.shape],
        place=place,
        flops=200 * theta.size,
        lead=(0, LEVELS),
        sends=16,
        scratch=[((32 * depth, 768), BF16), ((32 * depth, 384), F32), (whole, F32), (whole, F32)],
    )
    sums = lax.all_to_all(sums, ALL, 0, 0, tiled=True)
    return tuple(
        staged(
            backward_kernel,
            (sums, own, near, land_mask, bottom, above, below, west, east, w, a, c)
            + (theta_drop, salt_drop, x_open, y_open, stencil(((-2, -1), (-1, 7), (0, 7), (1, -1)), 256)),
            [whole, whole, kappa.shape, forcing.shape],
            place=place,
            scratch=[((32 * depth, 768), BF16), ((32 * depth, 256), F32)],
            sends=12,
            lead=(depth - LEVELS, LEVELS),
        )
    )


def solution(mesh):
    split = Mesh(mesh.devices.reshape(4, 2, 2, 2, 8), ALL)
    block = P(None, TROW, TCOL)
    flat = P(TROW, TCOL)
    return jax.shard_map(
        shards,
        mesh=split,
        in_specs=(block,) * 6 + (flat, flat, block, block, flat),
        out_specs=(block, block, block, flat),
        check_vma=False,
    )
```

```python
import math

import jax
import jax.numpy as jnp
import numpy as np
from jax import lax
from jax.experimental import pallas as pl
from jax.experimental.pallas import tpu as pltpu
from jax.sharding import Mesh
from jax.sharding import PartitionSpec as P

TROW = ("trow_0", "trow_1", "trow_2")
TCOL = ("tcol_0", "tcol_1")
ALL = TROW + TCOL
CENTRE = 4.75
KRYLOV = 4
PAIRS = [(i, j) for i in range(KRYLOV) for j in range(i, KRYLOV)]
F32 = jnp.float32
VM = pl.BlockSpec(memory_space=pltpu.VMEM)
SM = pl.BlockSpec(memory_space=pltpu.SMEM)
HB = pl.BlockSpec(memory_space=pltpu.HBM)
PARAMS = pltpu.CompilerParams(vmem_limit_bytes=58 * 1024 * 1024)


def iota(shape, dim):
    return lax.broadcasted_iota(jnp.int32, shape, dim)


def two_sum(a, b):
    s = a + b
    t = s - a
    return s, (a - (s - t)) + (b - t)


def quick_two_sum(a, b):
    s = a + b
    return s, b - (s - a)


def halves(a):
    t = a * 4097.0
    high = t - (t - a)
    return high, a - high


def two_prod(a, b, a_parts, b_parts):
    p = a * b
    ah, al = a_parts
    bh, bl = b_parts
    return p, ((ah * bh - p) + ah * bl + al * bh) + al * bl


def df_add(a, b):
    s, e = two_sum(a[0], b[0])
    return quick_two_sum(s, e + (a[1] + b[1]))


def df_mul(a, b):
    p, e = two_prod(a[0], b[0], halves(a[0]), halves(b[0]))
    return quick_two_sum(p, e + (a[0] * b[1] + a[1] * b[0]))


def df_div(a, b):
    inverse = 1.0 / b[0]
    q1 = a[0] * inverse
    back = df_mul((q1, jnp.zeros_like(q1)), b)
    rest = df_add(a, (-back[0], -back[1]))
    return quick_two_sum(q1, rest[0] * inverse)


class Loaded:
    def __init__(self, source, ref, parts, take_sem):
        self.ref = ref
        self.copies = []
        for part in parts:
            if part is None:
                self.copies.append(pltpu.make_async_copy(source, ref, take_sem()))
            else:
                self.copies.append(pltpu.make_async_copy(source.at[pl.ds(*part)], ref.at[pl.ds(*part)], take_sem()))

    def start(self, n):
        if n < len(self.copies):
            self.copies[n].start()
            self.waiting = list(self.copies)

    def first(self):
        if len(self.waiting) == len(self.copies):
            self.waiting.pop(0).wait()
        return self.ref

    def get(self):
        while self.waiting:
            self.waiting.pop(0).wait()
        return self.ref


class Stored:
    def __init__(self, target, ref, take_sem, pending):
        self.target, self.ref, self.take_sem, self.pending = target, ref, take_sem, pending

    def send(self, start=None, count=None):
        source, target = self.ref, self.target
        if start is not None:
            source, target = source.at[pl.ds(start, count)], target.at[pl.ds(start, count)]
        copy = pltpu.make_async_copy(source, target, self.take_sem())
        copy.start()
        self.pending.append(copy)


def staged(kernel, args, outs, place=None, scratch=(), sends=None, after=(), flops=0, lead=None):
    smem = [] if place is None else [place]

    def parts_of(shape):
        if lead is None or len(shape) < 3 or shape[0] < 24:
            return [None]
        start, stop = lead[0], min(lead[0] + lead[1], shape[0])
        return [(start, stop - start), (0, start) if start else (stop, shape[0] - stop)]

    cuts = [a[1:] if isinstance(a, tuple) else None for a in args]
    args = [a[0] if isinstance(a, tuple) else a for a in args]
    n_in, n_out = len(args), len(outs)
    sends = sends or n_out
    staging = [pltpu.VMEM(a.shape if cut is None else (cut[1],) + a.shape[1:], a.dtype) for a, cut in zip(args, cuts)]
    staging += [pltpu.VMEM(s, F32) for s in outs]

    def body(*refs):
        refs = list(refs)
        places = [refs.pop(0) for _ in smem]
        sources = [refs.pop(0) for _ in range(n_in)]
        sources = [s if cut is None else s.at[pl.ds(*cut)] for s, cut in zip(sources, cuts)]
        for _ in after:
            refs.pop(0)
        targets = [refs.pop(0) for _ in range(n_out)]
        buffers = [refs.pop(0) for _ in range(n_in)]
        holds = [refs.pop(0) for _ in range(n_out)]
        in_sems, out_sems = refs.pop(-2), refs.pop(-1)
        numbers = iter(range(2 * n_in))
        ins = [Loaded(s, b, parts_of(b.shape), lambda: in_sems.at[next(numbers)]) for s, b in zip(sources, buffers)]
        for n in (0, 1):
            for x in ins:
                x.start(n)
        pending = []
        given = []
        for n in range(n_out):
            given.append(Stored(targets[n], holds[n], lambda: out_sems.at[len(pending)], pending))
        kernel(ins, given, *places, *refs)
        for x in ins:
            x.get()
        for copy in pending:
            copy.wait()

    return pl.pallas_call(
        body,
        out_shape=[jax.ShapeDtypeStruct(s, F32) for s in outs],
        in_specs=[SM] * len(smem) + [HB] * (n_in + len(after)),
        out_specs=[HB] * n_out,
        scratch_shapes=staging
        + [pltpu.VMEM(s, t) for s, t in scratch]
        + [pltpu.SemaphoreType.DMA((2 * n_in,)), pltpu.SemaphoreType.DMA((sends,))],
        cost_estimate=pl.CostEstimate(
            flops=flops, bytes_accessed=4 * (sum(a.size for a in args) + sum(map(math.prod, outs))), transcendentals=0
        ),
        compiler_params=PARAMS,
    )(*smem, *args, *after)


def merge_rows(a, b, step):
    shape = a[0].shape
    first = (iota(shape, 0) & step) == 0

    def part(x, y):
        mixed = jnp.where(first, y, x)
        if step == 4:
            other = pltpu.roll(mixed, 4, 0)
        else:
            other = jnp.where(first, pltpu.roll(mixed, 8 - step, 0), pltpu.roll(mixed, step, 0))
        return jnp.where(first, x, y), other

    kept_high, other_high = part(a[0], b[0])
    kept_low, other_low = part(a[1], b[1])
    return df_add((kept_high, kept_low), (other_high, other_low))


def krylov_kernel(ins, outs, place_ref):
    cot_in, bottom_in = ins[:2]
    near_out, own_out, sums_out = outs
    near_ref, own_ref, sums_ref = [x.ref for x in outs]
    r = place_ref[0]
    c = place_ref[1]
    shape = (24, 384)
    row = iota(shape, 0)
    lane = iota(shape, 1)
    edge = iota((16, 128), 1)
    inside = ((row >= 8) | (r > 0)) & ((lane < 256) | ((lane < 264) & (c < 15)) | ((lane >= 376) & (c > 0)))
    rows, left, west, right, east = [x.get() for x in ins[2:]]

    def window(main, n):
        at = slice(8 * n, 8 * n + 8)
        ends = jnp.where(edge[0:8] < 64, right[at], left[at])
        sides = jnp.where(edge < 64, pltpu.roll(east[n], 10, 1), pltpu.roll(west[n], 2, 1))
        top = jnp.concatenate([rows[at], ends], axis=1)
        return jnp.concatenate([top, jnp.concatenate([main, sides], axis=1)], axis=0)

    start = jnp.where(inside, window(cot_in.get()[...], 0), 0.0)
    bottom = window(bottom_in.get()[...].astype(F32), 1)
    shifted = (4.2 + bottom / 25.0) - CENTRE

    def apply_shifted(v):
        below = jnp.where(row == 23, 0.0, pltpu.roll(v, 23, 0))
        beside = below + pltpu.roll(v, 1, 0) + pltpu.roll(v, 383, 1) + pltpu.roll(v, 1, 1)
        return jnp.where(inside, shifted * v - beside, 0.0)

    vectors = [start]
    images = []
    for step in range(KRYLOV):
        moved = apply_shifted(vectors[-1])
        images.append(moved + CENTRE * vectors[-1])
        if step == 0:
            vectors.append(moved * 0.25)
        elif step + 1 < KRYLOV:
            vectors.append(moved * 0.5 - vectors[-2])

    for k, v in enumerate(vectors):
        own_ref[24 * k : 24 * k + 24] = v
        near_ref[8 * k : 8 * k + 8] = pltpu.roll(v[0:16], 12, 0)[0:8]
    near_out.send()
    own_out.send()

    domain = (row >= 4) & (row < jnp.where(r == 15, 24, 20))
    cut = [jnp.where(domain, v, 0.0)[:, 0:256] for v in vectors]
    images = [w[:, 0:256] for w in images]
    cut_parts = [halves(v) for v in cut]
    image_parts = [halves(w) for w in images]

    def tile(x, at):
        i, j = divmod(at, 2)
        return x[8 * i : 8 * i + 8, 128 * j : 128 * j + 128]

    def dot(x, x_parts, y, y_parts):
        total = None
        for at in range(6):
            p, e = two_prod(
                tile(x, at),
                tile(y, at),
                [tile(h, at) for h in x_parts],
                [tile(h, at) for h in y_parts],
            )
            if total is None:
                total = (p, e)
            else:
                s, f = two_sum(total[0], p)
                total = (s, total[1] + (e + f))
        return total

    dots = [dot(cut[i], cut_parts[i], images[j], image_parts[j]) for i, j in PAIRS]
    dots += [dot(cut[i], cut_parts[i], cut[0], cut_parts[0]) for i in range(KRYLOV)]
    zero = jnp.zeros((8, 128), F32)
    dots += [(zero, zero)] * (16 - len(dots))
    packed = []
    for base in (0, 8):
        group = dots[base : base + 8]
        for step in (4, 2, 1):
            group = [merge_rows(group[i], group[i + step], step) for i in range(step)]
        total = group[0]
        for step in (64, 32, 16, 8, 4, 2, 1):
            total = df_add(total, (pltpu.roll(total[0], step, 1), pltpu.roll(total[1], step, 1)))
        packed.append(total)
    small_row = iota((8, 128), 0)
    small_lane = iota((8, 128), 1)
    spread = zero
    for part in (0, 1):
        for base in (0, 1):
            chosen = jnp.zeros((8, 128), jnp.bool_)
            for i in range(KRYLOV):
                for j in range(KRYLOV + 1):
                    index = len(PAIRS) + i if j == KRYLOV else PAIRS.index((min(i, j), max(i, j)))
                    if index // 8 == base:
                        chosen = chosen | (
                            (small_row == index % 8) & (small_lane == 32 * part + 8 * i + j)
                        )
            spread = spread + jnp.where(chosen, packed[base][part], 0.0)
    line = jnp.sum(spread, axis=0, keepdims=True)
    sums_ref[...] = jnp.broadcast_to(line, (256, 128))

    sums_out.send()


ROW_TURNS = (0, 4, 2, 6)
FIELDS = 6
LEVELS = 5


def packed_rows(parts, from_above):
    row = iota((8, 256), 0)
    order = (2, 1, 3, 0) if from_above else (0, 2, 1, 3)
    turned = [pltpu.roll(p, t, 0) if t else p for p, t in zip(parts, ROW_TURNS)]
    out = turned[order[3]]
    for n in (2, 1, 0):
        out = jnp.where(row < 2 * n + 2, turned[order[n]], out)
    return out


def packed_cols(parts, spare):
    group = (iota((16, 128), 1) + 2) & 127
    out = spare
    for m in range(len(parts) - 1, -1, -1):
        out = jnp.where(group < 4 * m + 4, pltpu.roll(parts[m], 4 * m, 1) if m else parts[m], out)
    return out


def columns_kernel(ins, outs):
    depth = ins[0].ref.shape[0]
    land_in, kappa_in, bottom_in, tcot_in, scot_in, theta_in, salt_in, ux_in, uy_in, surface_in = ins
    a_out, c_out, w_out, inv_out, ratio_out, down_out, up_out, right_out, left_out, corner_out, cross_out = outs
    a_ref, c_ref, w_ref, inv_ref, ratio_ref, down_ref, up_ref, right_ref, left_ref, corner_ref, cross_ref = [x.ref for x in outs]
    bottom = bottom_in.get()[...]
    lines = 8 * depth + 8 * ((depth + 1) // 2)
    spare = []
    for n, field in enumerate((surface_in.get()[...], bottom.astype(F32))):
        down_ref[lines + 8 * n : lines + 8 * n + 8] = field[8:16]
        spare.append((pltpu.roll(field[:, 128:256], 126, 1), pltpu.roll(field[:, 0:128], 118, 1)))
        corner_ref[8 * n : 8 * n + 8] = field[8:16, 128:256]
        cross_ref[8 * n : 8 * n + 8] = field[8:16, 0:128]
    cross_ref[16:80] = jnp.zeros((64, 128), F32)
    corner_out.send()
    cross_out.send()
    early = (land_in, kappa_in, tcot_in, scot_in)
    land_ref, kappa_ref, tcot_ref, scot_ref = [x.first() for x in early]

    def wet_at(k):
        return jnp.where(k < bottom, land_ref[k].astype(F32), 0.0)

    wet = wet_at(0)
    ratio = None
    couple_last = None
    state = None
    for k in range(depth):
        if k == LEVELS - 1:
            for x in early:
                x.get()
        diagonal = jnp.ones((16, 256), F32)
        if k > 0:
            diagonal = diagonal + couple_last - couple_last * ratio
        if k < depth - 1:
            wet_next = wet_at(k + 1)
            couple = kappa_ref[k] * wet * wet_next
            diagonal = diagonal + couple
        inverse = 1.0 / diagonal
        rhs = (tcot_ref[k], scot_ref[k], wet)
        if k == 0:
            state = tuple(x * inverse for x in rhs)
        else:
            state = tuple((x + couple_last * s) * inverse for x, s in zip(rhs, state))
        a_ref[k], c_ref[k], w_ref[k] = state
        inv_ref[k] = inverse
        if k < depth - 1:
            ratio = couple * inverse
            ratio_ref[k] = ratio
            couple_last = couple
            wet = wet_next
    inv_out.send()
    ratio_out.send()
    theta_ref = theta_in.get()
    salt_ref = salt_in.get()
    ux_ref = ux_in.get()
    uy_ref = uy_in.get()
    row8 = iota((8, 256), 0)
    lane = iota((16, 128), 1)
    tails = {}
    last_parts, first_parts = [], []
    for k in range(depth - 1, -1, -1):
        wet = wet_at(k)
        if k < depth - 1:
            ratio = ratio_ref[k]
            state = tuple(x + ratio * s for x, s in zip((a_ref[k], c_ref[k], w_ref[k]), state))
            a_ref[k], c_ref[k], w_ref[k] = state
        fields = (theta_ref[k] * wet, salt_ref[k] * wet) + state
        down_ref[8 * k : 8 * k + 8] = packed_rows([f[8:16] for f in fields[:4]], True)
        up_ref[8 * k : 8 * k + 8] = packed_rows([f[0:8] for f in fields[:4]], False)
        flow = ux_ref[k] * wet
        open_low = flow[8:16] * pltpu.roll(wet[8:16], 7, 0)
        open_high = flow[0:8] * pltpu.roll(wet[0:8], 7, 0)
        face_low = jnp.where(row8 == 6, open_low, flow[8:16])
        face_high = jnp.where(row8 == 0, open_high, pltpu.roll(wet[0:8], 1, 0))
        tails[k] = ((state[2][8:16], face_low), (state[2][0:8], face_high))
        if k % 2 == 0:
            later = tails.pop(k + 1, tails[k])
            this = tails.pop(k)
            at = 8 * depth + 4 * k
            down_ref[at : at + 8] = packed_rows(this[0] + later[0], True)
            up_ref[at : at + 8] = packed_rows(this[1] + later[1], False)
        flow = uy_ref[k] * wet
        open_last = flow[:, 128:256] * pltpu.roll(wet[:, 128:256], 127, 1)
        open_first = flow[:, 0:128] * pltpu.roll(wet[:, 0:128], 127, 1)
        last = [f[:, 128:256] for f in fields] + [jnp.where(lane == 126, open_last, flow[:, 128:256])]
        first = [f[:, 0:128] for f in fields] + [
            jnp.where(lane == 0, open_first, pltpu.roll(wet[:, 0:128], 1, 1))
        ]
        last_parts = last + last_parts
        first_parts = first + first_parts
        if k % LEVELS == 0:
            g = k // LEVELS
            right_ref[g] = packed_cols(last_parts, spare[g % 2][0])
            left_ref[g] = packed_cols(first_parts, spare[g % 2][1])
            last_parts, first_parts = [], []
            for out in (a_out, c_out, w_out):
                out.send(k, LEVELS)
    for out in (down_out, right_out, up_out, left_out):
        out.send()


SCALE = 1.0 / 12.0
BF16 = jnp.bfloat16


class Edges:
    def __init__(self, place_ref, depth, above, below, west, east):
        r = place_ref[0]
        c = place_ref[1]
        self.depth, self.above, self.below, self.west, self.east = depth, above, below, west, east
        self.row8 = iota((8, 256), 0)
        self.lane16 = iota((16, 128), 1)
        has_up = jnp.where(r > 0, 1.0, 0.0)
        has_down = jnp.where(r < 15, 1.0, 0.0)
        has_left = jnp.where(c > 0, 1.0, 0.0)
        has_right = jnp.where(c < 15, 1.0, 0.0)
        self.above_rows = (self.row8 & 2) != 0
        self.row_flags = (
            jnp.where(self.above_rows, has_up, has_down),
            jnp.where(self.above_rows, has_down, has_up),
        )
        self.west_lanes = (self.lane16 & 2) != 0
        self.lane_flag = jnp.where(self.west_lanes, has_left, has_right)

    def row_pair(self, at, second):
        above = self.above[at : at + 8]
        below = self.below[at : at + 8]
        if second:
            return jnp.where(self.above_rows, below, above) * self.row_flags[1]
        return jnp.where(self.above_rows, above, below) * self.row_flags[0]

    def turned_rows(self, pair, f):
        turn = (8 - ROW_TURNS[f]) % 8
        return pltpu.roll(pair, turn, 0) if turn else pair

    def tail_rows(self, k, f):
        pair = self.row_pair(8 * self.depth + 8 * (k // 2), k % 2 == 1)
        return self.turned_rows(pair, f + 2 * (k % 2))

    def cols(self, k, f):
        g = k // LEVELS
        pair = jnp.where(self.west_lanes, self.west[g], self.east[g]) * self.lane_flag
        turn = 4 * (FIELDS * (k % LEVELS) + f)
        return pltpu.roll(pair, 128 - turn, 1) if turn else pair


def next_of(x, axis):
    return pltpu.roll(x, x.shape[axis] - 1, axis)


def last_of(x, axis):
    return pltpu.roll(x, 1, axis)


def two_parts(x):
    high = x.astype(BF16)
    return jnp.concatenate([high, (x - high.astype(F32)).astype(BF16)], axis=1)


def stencil(offsets, columns):
    out = np.zeros((384, columns), np.float32)
    for j in range(columns):
        for offset, value in offsets:
            out[(j + offset) % 384, j] += value
    return jnp.asarray(np.concatenate([out, out]), BF16)


def forward_kernel(ins, outs, place_ref, parts_ref, filtered_ref, theta_sweep_ref, salt_sweep_ref):
    (
        land_in,
        bottom_in,
        above_in,
        below_in,
        west_in,
        east_in,
        ux_in,
        uy_in,
        theta_in,
        salt_in,
        filter_in,
        forcing_in,
        kappa_in,
        inv_in,
        ratio_in,
    ) = ins
    x_out, y_out, theta_out, salt_out = outs
    x_open_ref, y_open_ref, theta_drop_ref, salt_drop_ref = [x.ref for x in outs]
    depth = theta_in.ref.shape[0]
    bottom = bottom_in.get()[...]
    land_ref = land_in.first()
    edges = Edges(place_ref, depth, *[x.get() for x in (above_in, below_in, west_in, east_in)])
    row8, lane16 = edges.row8, edges.lane16
    early = (ux_in, uy_in, theta_in, salt_in, land_in)
    ux_ref, uy_ref, theta_ref, salt_ref, _ = [x.first() for x in early]

    def wet_at(k):
        return jnp.where(k < bottom, land_ref[k].astype(F32), 0.0)

    for k in range(depth):
        if k == LEVELS:
            for x in early:
                x.get()
        wet = wet_at(k)
        faces = edges.tail_rows(k, 1)
        wide = jnp.concatenate([wet, pltpu.roll(faces, 7, 0)], axis=0)
        later = next_of(wide, 0)
        x_open = jnp.concatenate(
            [ux_ref[k] * wet * later[0:16], jnp.where(row8 == 7, faces * later[16:24], faces)], axis=0
        )
        x_open_ref[k] = x_open * SCALE
        faces = edges.cols(k, 5)
        wide = jnp.concatenate([wet, pltpu.roll(faces, 127, 1)], axis=1)
        later = next_of(wide, 1)
        y_open = jnp.concatenate(
            [uy_ref[k] * wet * later[:, 0:256], jnp.where(lane16 == 127, faces * later[:, 256:384], faces)], axis=1
        )
        y_open_ref[k] = y_open * SCALE
        for f, ref in ((0, theta_ref), (1, salt_ref)):
            wide = jnp.concatenate([ref[k] * wet, edges.cols(k, f)], axis=1)
            at = 16 * (depth * f + k)
            parts_ref[at : at + 16] = two_parts(wide)
    x_out.send()
    y_out.send()
    filtered_ref[...] = jnp.dot(parts_ref[...], filter_in.get()[...], preferred_element_type=F32)
    forcing_ref, kappa_ref, inv_ref, ratio_ref = [x.get() for x in (forcing_in, kappa_in, inv_in, ratio_in)]

    couple_last = None
    state = None
    wet = wet_at(0)
    for k in range(depth):
        rows = edges.row_pair(8 * k, False)
        x_open = x_open_ref[k]
        y_open = y_open_ref[k]
        advected = []
        for f, ref in ((0, theta_ref), (1, salt_ref)):
            q = ref[k]
            wide = jnp.concatenate([q * wet, edges.turned_rows(rows, f)], axis=0)
            pair = wide + next_of(wide, 0)
            flux = x_open * (8.0 * pair - last_of(pair, 0) - next_of(pair, 0))
            change = (flux - last_of(flux, 0))[0:16]
            at = 16 * (depth * f + k)
            flux = y_open * filtered_ref[at : at + 16]
            change = change + (flux - last_of(flux, 1))[:, 0:256]
            advected.append(q - change)
        if k == 0:
            advected[0] = advected[0] + forcing_ref[...] * wet
        inverse = inv_ref[k]
        if k == 0:
            state = tuple(x * inverse for x in advected)
        else:
            state = tuple((x + couple_last * s) * inverse for x, s in zip(advected, state))
        theta_sweep_ref[k], salt_sweep_ref[k] = state
        if k < depth - 1:
            wet_next = wet_at(k + 1)
            couple_last = kappa_ref[k] * wet * wet_next
            wet = wet_next
    wet_later = wet
    for k in range(depth - 2, -1, -1):
        wet = wet_at(k)
        ratio = ratio_ref[k]
        new = (theta_sweep_ref[k] + ratio * state[0], salt_sweep_ref[k] + ratio * state[1])
        opened = wet * wet_later
        theta_drop_ref[k] = opened * (state[0] - new[0])
        salt_drop_ref[k] = opened * (state[1] - new[1])
        state = new
        wet_later = wet
        if k % LEVELS == 0:
            theta_out.send(k, min(LEVELS, depth - 1 - k))
            salt_out.send(k, min(LEVELS, depth - 1 - k))


def backward_kernel(ins, outs, place_ref, parts_ref, filtered_ref):
    (
        sums_in,
        own_in,
        near_in,
        land_in,
        bottom_in,
        above_in,
        below_in,
        west_in,
        east_in,
        w_in,
        a_in,
        c_in,
        theta_drop_in,
        salt_drop_in,
        x_open_in,
        y_open_in,
        filter_in,
    ) = ins
    theta_out, salt_out, kappa_out, forcing_out = outs
    theta_grad_ref, salt_grad_ref, kappa_grad_ref, forcing_grad_ref = [x.ref for x in outs]
    depth = w_in.ref.shape[0]
    r = place_ref[0]
    has_down = jnp.where(r < 15, 1.0, 0.0)
    sums_ref, own_ref, near_ref = [x.get() for x in (sums_in, own_in, near_in)]

    small = (8, 128)
    small_row = iota(small, 0)
    terms = [(sums_ref[8 * at : 8 * at + 8], None) for at in range(32)]
    while len(terms) > 1:
        joined = []
        for x, y in zip(terms[::2], terms[1::2]):
            s, e = two_sum(x[0], y[0])
            joined.append((s, e if x[1] is None else (x[1] + y[1]) + e))
        terms = joined
    total = terms[0]
    for step in (4, 2, 1):
        s, e = two_sum(total[0], pltpu.roll(total[0], step, 0))
        total = (s, (total[1] + pltpu.roll(total[1], step, 0)) + e)
    low = total[1] + pltpu.roll(total[0] + total[1], 96, 1)
    total = quick_two_sum(total[0], low)

    def as_rows(x):
        out = x
        for i in range(1, KRYLOV):
            out = jnp.where(small_row == i, pltpu.roll(x, 128 - 8 * i, 1), out)
        return out

    system = (as_rows(total[0]), as_rows(total[1]))

    def row_of(x, k):
        return jnp.broadcast_to(x[k : k + 1, :], small)

    def lane_of(x, k):
        return jnp.broadcast_to(x[:, k : k + 1], small)

    keep = []
    weights = []
    scales = [lane_of(row_of(system[0], k), k) for k in range(KRYLOV)]
    for k in range(KRYLOV):
        across = (row_of(system[0], k), row_of(system[1], k))
        pivot = (lane_of(across[0], k), lane_of(across[1], k))
        fine = pivot[0] > 1e-13 * scales[k]
        keep.append(fine)
        pivot = (jnp.where(fine, pivot[0], 1.0), jnp.where(fine, pivot[1], 0.0))
        factor = df_div((lane_of(system[0], k), lane_of(system[1], k)), pivot)
        used = fine & (small_row != k)
        factor = (jnp.where(used, factor[0], 0.0), jnp.where(used, factor[1], 0.0))
        product = df_mul(factor, across)
        system = df_add(system, (-product[0], -product[1]))
    for k in range(KRYLOV):
        pivot = lane_of(row_of(system[0], k), k)
        value = lane_of(row_of(system[0], k), KRYLOV)
        value = jnp.where(keep[k], value / jnp.where(keep[k], pivot, 1.0), 0.0)
        weights.append(value[0:1, 0:1])

    def combined(ref, rows):
        out = weights[0] * ref[0:rows]
        for k in range(1, KRYLOV):
            out = out + weights[k] * ref[rows * k : rows * k + rows]
        return out

    def rows_joined(upper, lower):
        turned = pltpu.roll(lower, 4, 0)
        row8 = iota(turned.shape, 0)
        middle = jnp.where((row8 >= 5) & (r < 15), turned, upper[16:24])
        return jnp.concatenate([upper[0:16], middle, turned * has_down], axis=0)

    surface = rows_joined(combined(own_ref, 24), combined(near_ref, 8))
    zeta = surface[8:24, 0:256]
    bottom = bottom_in.get()[...]
    land_ref = land_in.first()
    edges = Edges(place_ref, depth, *[x.get() for x in (above_in, below_in, west_in, east_in)])
    zeta_rows = jnp.where(edges.row8 < 4, surface[24:32, 0:256], surface[0:8, 0:256])
    zeta_cols = surface[8:24, 256:384]

    def wet_at(k):
        return jnp.where(k < bottom, land_ref[k].astype(F32), 0.0)

    early = (w_in, a_in, c_in, theta_drop_in, salt_drop_in, x_open_in, y_open_in, land_in)
    w_ref, a_ref, c_ref, theta_drop_ref, salt_drop_ref, x_open_ref, y_open_ref, _ = [x.first() for x in early]
    share = (0.2, -0.15)
    mu_later = None
    for k in range(depth - 1, -1, -1):
        if k == depth - LEVELS - 1:
            for x in early:
                x.get()
        wet = wet_at(k)
        rise = zeta * w_ref[k]
        mu = (a_ref[k] + share[0] * rise, c_ref[k] + share[1] * rise)
        if k < depth - 1:
            kappa_grad_ref[k] = theta_drop_ref[k] * (mu[0] - mu_later[0]) + salt_drop_ref[k] * (mu[1] - mu_later[1])
        rows = edges.row_pair(8 * k, True)
        row_rise = zeta_rows * edges.tail_rows(k, 0)
        col_rise = zeta_cols * edges.cols(k, 4)
        x_open = x_open_ref[k]
        y_open = y_open_ref[k]
        for n, ref in ((0, theta_grad_ref), (1, salt_grad_ref)):
            wide = jnp.concatenate([mu[n], edges.cols(k, 2 + n) + share[n] * col_rise], axis=1)
            at = 16 * (depth * n + k)
            parts_ref[at : at + 16] = two_parts(y_open * (wide - next_of(wide, 1)))
            wide = jnp.concatenate([mu[n], edges.turned_rows(rows, 2 + n) + share[n] * row_rise], axis=0)
            h = x_open * (wide - next_of(wide, 0))
            pair = h + last_of(h, 0)
            change = (8.0 * pair - last_of(pair, 0) - next_of(pair, 0))[0:16]
            ref[k] = mu[n] - wet * change
        if k == 0:
            forcing_grad_ref[...] = zeta + wet * mu[0]
        mu_later = mu
    kappa_out.send()
    forcing_out.send()
    filtered_ref[...] = jnp.dot(parts_ref[...], filter_in.get()[...], preferred_element_type=F32)
    for n, ref, out in ((0, theta_grad_ref, theta_out), (1, salt_grad_ref, salt_out)):
        for k in range(depth):
            at = 16 * (depth * n + k)
            ref[k] = ref[k] - wet_at(k) * filtered_ref[at : at + 16]
            if k % 5 == 4:
                out.send(k - 4, 5)


def around(count, step):
    return [(i, (i + step) % count) for i in range(count)]


def across(down, right):
    return [
        (16 * i + j, 16 * ((i + down) % 16) + (j + right) % 16) for i in range(16) for j in range(16)
    ]


def shards(
    theta,
    salt,
    velocity_x,
    velocity_y,
    land_mask,
    kappa,
    forcing,
    bottom,
    theta_cot,
    salt_cot,
    surface_cot,
):
    depth = theta.shape[0]
    whole = theta.shape
    place = jnp.stack([lax.axis_index(TROW), lax.axis_index(TCOL)]).astype(jnp.int32)
    lines = 8 * depth + 8 * ((depth + 1) // 2)
    columns = (depth // LEVELS, 16, 128)
    a, c, w, inv, ratio, down, up, right, left, corner, cross = staged(
        columns_kernel,
        (land_mask, kappa, bottom, theta_cot, salt_cot, theta, salt, velocity_x, velocity_y, surface_cot),
        [whole] * 4
        + [kappa.shape, (lines + 16, 256), (lines, 256), columns, columns, (16, 128), (80, 128)],
        flops=100 * theta.size,
        lead=(0, LEVELS),
        sends=32,
    )
    corner = lax.ppermute(corner, ALL, across(1, 1))
    west = lax.ppermute(right, TCOL, around(16, 1))
    cross = lax.ppermute(cross, ALL, across(1, -1))
    east = lax.ppermute(left, TCOL, around(16, -1))
    above = lax.ppermute(down, TROW, around(16, 1))
    below = lax.ppermute(up, TROW, around(16, -1))
    near, own, sums = staged(
        krylov_kernel,
        (surface_cot, bottom, (above, lines, 16), corner, (west, 0, 2), (cross, 0, 16), (east, 0, 2)),
        [(32, 384), (96, 384), (256, 128)],
        place=place,
        after=(),
    )
    near = lax.ppermute(near, TROW, around(16, -1))
    x_open, y_open, theta_drop, salt_drop = staged(
        forward_kernel,
        (land_mask, bottom, above, below, west, east, velocity_x, velocity_y, theta, salt)
        + (stencil(((-1, -1), (0, 7), (1, 7), (2, -1)), 384), forcing, kappa, inv, ratio),
        [(depth, 24, 256), (depth, 16, 384), kappa.shape, kappa.shape],
        place=place,
        flops=200 * theta.size,
        lead=(0, LEVELS),
        sends=16,
        scratch=[((32 * depth, 768), BF16), ((32 * depth, 384), F32), (whole, F32), (whole, F32)],
    )
    sums = lax.all_to_all(sums, ALL, 0, 0, tiled=True)
    return tuple(
        staged(
            backward_kernel,
            (sums, own, near, land_mask, bottom, above, below, west, east, w, a, c)
            + (theta_drop, salt_drop, x_open, y_open, stencil(((-2, -1), (-1, 7), (0, 7), (1, -1)), 256)),
            [whole, whole, kappa.shape, forcing.shape],
            place=place,
            scratch=[((32 * depth, 768), BF16), ((32 * depth, 256), F32)],
            sends=12,
            lead=(depth - LEVELS, LEVELS),
        )
    )


def solution(mesh):
    split = Mesh(mesh.devices.reshape(4, 2, 2, 2, 8), ALL)
    block = P(None, TROW, TCOL)
    flat = P(TROW, TCOL)
    return jax.shard_map(
        shards,
        mesh=split,
        in_specs=(block,) * 6 + (flat, flat, block, block, flat),
        out_specs=(block, block, block, flat),
        check_vma=False,
    )
```

```python
import math

import jax
import jax.numpy as jnp
import numpy as np
from jax import lax
from jax.experimental import pallas as pl
from jax.experimental.pallas import tpu as pltpu
from jax.sharding import Mesh
from jax.sharding import PartitionSpec as P

TROW = ("trow_0", "trow_1", "trow_2")
TCOL = ("tcol_0", "tcol_1")
ALL = TROW + TCOL
CENTRE = 4.75
KRYLOV = 4
PAIRS = [(i, j) for i in range(KRYLOV) for j in range(i, KRYLOV)]
F32 = jnp.float32
VM = pl.BlockSpec(memory_space=pltpu.VMEM)
HB = pl.BlockSpec(memory_space=pltpu.HBM)
PARAMS = pltpu.CompilerParams(vmem_limit_bytes=58 * 1024 * 1024)


def iota(shape, dim):
    return lax.broadcasted_iota(jnp.int32, shape, dim)


def two_sum(a, b):
    s = a + b
    t = s - a
    return s, (a - (s - t)) + (b - t)


def quick_two_sum(a, b):
    s = a + b
    return s, b - (s - a)


def halves(a):
    t = a * 4097.0
    high = t - (t - a)
    return high, a - high


def two_prod(a, b, a_parts, b_parts):
    p = a * b
    ah, al = a_parts
    bh, bl = b_parts
    return p, ((ah * bh - p) + ah * bl + al * bh) + al * bl


def df_add(a, b):
    s, e = two_sum(a[0], b[0])
    return quick_two_sum(s, e + (a[1] + b[1]))


def df_mul(a, b):
    p, e = two_prod(a[0], b[0], halves(a[0]), halves(b[0]))
    return quick_two_sum(p, e + (a[0] * b[1] + a[1] * b[0]))


def df_div(a, b):
    inverse = 1.0 / b[0]
    q1 = a[0] * inverse
    back = df_mul((q1, jnp.zeros_like(q1)), b)
    rest = df_add(a, (-back[0], -back[1]))
    return quick_two_sum(q1, rest[0] * inverse)


class Loaded:
    def __init__(self, source, ref, parts, take_sem):
        self.ref = ref
        self.copies = []
        for part in parts:
            if part is None:
                self.copies.append(pltpu.make_async_copy(source, ref, take_sem()))
            else:
                self.copies.append(pltpu.make_async_copy(source.at[pl.ds(*part)], ref.at[pl.ds(*part)], take_sem()))

    def start(self, n):
        if n < len(self.copies):
            self.copies[n].start()
            self.waiting = list(self.copies)

    def first(self):
        if len(self.waiting) == len(self.copies):
            self.waiting.pop(0).wait()
        return self.ref

    def get(self):
        while self.waiting:
            self.waiting.pop(0).wait()
        return self.ref


class Stored:
    def __init__(self, target, ref, take_sem, pending):
        self.target, self.ref, self.take_sem, self.pending = target, ref, take_sem, pending

    def send(self, start=None, count=None):
        source, target = self.ref, self.target
        if start is not None:
            source, target = source.at[pl.ds(start, count)], target.at[pl.ds(start, count)]
        copy = pltpu.make_async_copy(source, target, self.take_sem())
        copy.start()
        self.pending.append(copy)


def staged(kernel, args, outs, place=False, scratch=(), sends=None, after=(), flops=0, lead=None):
    def parts_of(shape):
        if lead is None or len(shape) < 3 or shape[0] < 24:
            return [None]
        start, stop = lead[0], min(lead[0] + lead[1], shape[0])
        return [(start, stop - start), (0, start) if start else (stop, shape[0] - stop)]

    cuts = [a[1:] if isinstance(a, tuple) else None for a in args]
    args = [a[0] if isinstance(a, tuple) else a for a in args]
    n_in, n_out = len(args), len(outs)
    sends = sends or n_out
    staging = [pltpu.VMEM(a.shape if cut is None else (cut[1],) + a.shape[1:], a.dtype) for a, cut in zip(args, cuts)]
    staging += [pltpu.VMEM(s, F32) for s in outs]

    def body(*refs):
        refs = list(refs)
        places = [(lax.axis_index(TROW), lax.axis_index(TCOL))] if place else []
        sources = [refs.pop(0) for _ in range(n_in)]
        sources = [s if cut is None else s.at[pl.ds(*cut)] for s, cut in zip(sources, cuts)]
        for _ in after:
            refs.pop(0)
        targets = [refs.pop(0) for _ in range(n_out)]
        buffers = [refs.pop(0) for _ in range(n_in)]
        holds = [refs.pop(0) for _ in range(n_out)]
        in_sems, out_sems = refs.pop(-2), refs.pop(-1)
        numbers = iter(range(2 * n_in))
        ins = [Loaded(s, b, parts_of(b.shape), lambda: in_sems.at[next(numbers)]) for s, b in zip(sources, buffers)]
        for n in (0, 1):
            for x in ins:
                x.start(n)
        pending = []
        given = []
        for n in range(n_out):
            given.append(Stored(targets[n], holds[n], lambda: out_sems.at[len(pending)], pending))
        kernel(ins, given, *places, *refs)
        for x in ins:
            x.get()
        for copy in pending:
            copy.wait()

    return pl.pallas_call(
        body,
        out_shape=[jax.ShapeDtypeStruct(s, F32) for s in outs],
        in_specs=[HB] * (n_in + len(after)),
        out_specs=[HB] * n_out,
        scratch_shapes=staging
        + [pltpu.VMEM(s, t) for s, t in scratch]
        + [pltpu.SemaphoreType.DMA((2 * n_in,)), pltpu.SemaphoreType.DMA((sends,))],
        cost_estimate=pl.CostEstimate(
            flops=flops, bytes_accessed=4 * (sum(a.size for a in args) + sum(map(math.prod, outs))), transcendentals=0
        ),
        compiler_params=PARAMS,
    )(*args, *after)


def merge_rows(a, b, step):
    shape = a[0].shape
    first = (iota(shape, 0) & step) == 0

    def part(x, y):
        mixed = jnp.where(first, y, x)
        if step == 4:
            other = pltpu.roll(mixed, 4, 0)
        else:
            other = jnp.where(first, pltpu.roll(mixed, 8 - step, 0), pltpu.roll(mixed, step, 0))
        return jnp.where(first, x, y), other

    kept_high, other_high = part(a[0], b[0])
    kept_low, other_low = part(a[1], b[1])
    return df_add((kept_high, kept_low), (other_high, other_low))


def krylov_kernel(ins, outs, place_ref):
    cot_in, bottom_in = ins[:2]
    near_out, own_out, sums_out = outs
    near_ref, own_ref, sums_ref = [x.ref for x in outs]
    r = place_ref[0]
    c = place_ref[1]
    shape = (24, 384)
    row = iota(shape, 0)
    lane = iota(shape, 1)
    edge = iota((16, 128), 1)
    inside = ((row >= 8) | (r > 0)) & ((lane < 256) | ((lane < 264) & (c < 15)) | ((lane >= 376) & (c > 0)))
    rows, left, west, right, east = [x.get() for x in ins[2:]]

    def window(main, n):
        at = slice(8 * n, 8 * n + 8)
        ends = jnp.where(edge[0:8] < 64, right[at], left[at])
        sides = jnp.where(edge < 64, pltpu.roll(east[n], 10, 1), pltpu.roll(west[n], 2, 1))
        top = jnp.concatenate([rows[at], ends], axis=1)
        return jnp.concatenate([top, jnp.concatenate([main, sides], axis=1)], axis=0)

    start = jnp.where(inside, window(cot_in.get()[...], 0), 0.0)
    bottom = window(bottom_in.get()[...].astype(F32), 1)
    shifted = (4.2 + bottom / 25.0) - CENTRE

    def apply_shifted(v):
        below = jnp.where(row == 23, 0.0, pltpu.roll(v, 23, 0))
        beside = below + pltpu.roll(v, 1, 0) + pltpu.roll(v, 383, 1) + pltpu.roll(v, 1, 1)
        return jnp.where(inside, shifted * v - beside, 0.0)

    vectors = [start]
    images = []
    for step in range(KRYLOV):
        moved = apply_shifted(vectors[-1])
        images.append(moved + CENTRE * vectors[-1])
        if step == 0:
            vectors.append(moved * 0.25)
        elif step + 1 < KRYLOV:
            vectors.append(moved * 0.5 - vectors[-2])

    for k, v in enumerate(vectors):
        own_ref[24 * k : 24 * k + 24] = v
        near_ref[8 * k : 8 * k + 8] = pltpu.roll(v[0:16], 12, 0)[0:8]
    near_out.send()
    own_out.send()

    domain = (row >= 4) & (row < jnp.where(r == 15, 24, 20))
    cut = [jnp.where(domain, v, 0.0)[:, 0:256] for v in vectors]
    images = [w[:, 0:256] for w in images]
    cut_parts = [halves(v) for v in cut]
    image_parts = [halves(w) for w in images]

    def tile(x, at):
        i, j = divmod(at, 2)
        return x[8 * i : 8 * i + 8, 128 * j : 128 * j + 128]

    def dot(x, x_parts, y, y_parts):
        total = None
        for at in range(6):
            p, e = two_prod(
                tile(x, at),
                tile(y, at),
                [tile(h, at) for h in x_parts],
                [tile(h, at) for h in y_parts],
            )
            if total is None:
                total = (p, e)
            else:
                s, f = two_sum(total[0], p)
                total = (s, total[1] + (e + f))
        return total

    dots = [dot(cut[i], cut_parts[i], images[j], image_parts[j]) for i, j in PAIRS]
    dots += [dot(cut[i], cut_parts[i], cut[0], cut_parts[0]) for i in range(KRYLOV)]
    zero = jnp.zeros((8, 128), F32)
    dots += [(zero, zero)] * (16 - len(dots))
    packed = []
    for base in (0, 8):
        group = dots[base : base + 8]
        for step in (4, 2, 1):
            group = [merge_rows(group[i], group[i + step], step) for i in range(step)]
        total = group[0]
        for step in (64, 32, 16, 8, 4, 2, 1):
            total = df_add(total, (pltpu.roll(total[0], step, 1), pltpu.roll(total[1], step, 1)))
        packed.append(total)
    small_row = iota((8, 128), 0)
    small_lane = iota((8, 128), 1)
    spread = zero
    for part in (0, 1):
        for base in (0, 1):
            chosen = jnp.zeros((8, 128), jnp.bool_)
            for i in range(KRYLOV):
                for j in range(KRYLOV + 1):
                    index = len(PAIRS) + i if j == KRYLOV else PAIRS.index((min(i, j), max(i, j)))
                    if index // 8 == base:
                        chosen = chosen | (
                            (small_row == index % 8) & (small_lane == 32 * part + 8 * i + j)
                        )
            spread = spread + jnp.where(chosen, packed[base][part], 0.0)
    line = jnp.sum(spread, axis=0, keepdims=True)
    sums_ref[...] = jnp.broadcast_to(line, (256, 128))

    sums_out.send()


ROW_TURNS = (0, 4, 2, 6)
FIELDS = 6
LEVELS = 5


def packed_rows(parts, from_above):
    row = iota((8, 256), 0)
    order = (2, 1, 3, 0) if from_above else (0, 2, 1, 3)
    turned = [pltpu.roll(p, t, 0) if t else p for p, t in zip(parts, ROW_TURNS)]
    out = turned[order[3]]
    for n in (2, 1, 0):
        out = jnp.where(row < 2 * n + 2, turned[order[n]], out)
    return out


def packed_cols(parts, spare):
    group = (iota((16, 128), 1) + 2) & 127
    out = spare
    for m in range(len(parts) - 1, -1, -1):
        out = jnp.where(group < 4 * m + 4, pltpu.roll(parts[m], 4 * m, 1) if m else parts[m], out)
    return out


def columns_kernel(ins, outs):
    depth = ins[0].ref.shape[0]
    land_in, kappa_in, bottom_in, tcot_in, scot_in, theta_in, salt_in, ux_in, uy_in, surface_in = ins
    a_out, c_out, w_out, inv_out, ratio_out, down_out, up_out, right_out, left_out, corner_out, cross_out = outs
    a_ref, c_ref, w_ref, inv_ref, ratio_ref, down_ref, up_ref, right_ref, left_ref, corner_ref, cross_ref = [x.ref for x in outs]
    bottom = bottom_in.get()[...]
    lines = 8 * depth + 8 * ((depth + 1) // 2)
    spare = []
    for n, field in enumerate((surface_in.get()[...], bottom.astype(F32))):
        down_ref[lines + 8 * n : lines + 8 * n + 8] = field[8:16]
        spare.append((pltpu.roll(field[:, 128:256], 126, 1), pltpu.roll(field[:, 0:128], 118, 1)))
        corner_ref[8 * n : 8 * n + 8] = field[8:16, 128:256]
        cross_ref[8 * n : 8 * n + 8] = field[8:16, 0:128]
    cross_ref[16:80] = jnp.zeros((64, 128), F32)
    corner_out.send()
    cross_out.send()
    early = (land_in, kappa_in, tcot_in, scot_in)
    land_ref, kappa_ref, tcot_ref, scot_ref = [x.first() for x in early]

    def wet_at(k):
        return jnp.where(k < bottom, land_ref[k].astype(F32), 0.0)

    wet = wet_at(0)
    ratio = None
    couple_last = None
    state = None
    for k in range(depth):
        if k == LEVELS - 1:
            for x in early:
                x.get()
        diagonal = jnp.ones((16, 256), F32)
        if k > 0:
            diagonal = diagonal + couple_last - couple_last * ratio
        if k < depth - 1:
            wet_next = wet_at(k + 1)
            couple = kappa_ref[k] * wet * wet_next
            diagonal = diagonal + couple
        inverse = 1.0 / diagonal
        rhs = (tcot_ref[k], scot_ref[k], wet)
        if k == 0:
            state = tuple(x * inverse for x in rhs)
        else:
            state = tuple((x + couple_last * s) * inverse for x, s in zip(rhs, state))
        a_ref[k], c_ref[k], w_ref[k] = state
        inv_ref[k] = inverse
        if k < depth - 1:
            ratio = couple * inverse
            ratio_ref[k] = ratio
            couple_last = couple
            wet = wet_next
    inv_out.send()
    ratio_out.send()
    theta_ref = theta_in.get()
    salt_ref = salt_in.get()
    ux_ref = ux_in.get()
    uy_ref = uy_in.get()
    row8 = iota((8, 256), 0)
    lane = iota((16, 128), 1)
    tails = {}
    last_parts, first_parts = [], []
    for k in range(depth - 1, -1, -1):
        wet = wet_at(k)
        if k < depth - 1:
            ratio = ratio_ref[k]
            state = tuple(x + ratio * s for x, s in zip((a_ref[k], c_ref[k], w_ref[k]), state))
            a_ref[k], c_ref[k], w_ref[k] = state
        fields = (theta_ref[k] * wet, salt_ref[k] * wet) + state
        down_ref[8 * k : 8 * k + 8] = packed_rows([f[8:16] for f in fields[:4]], True)
        up_ref[8 * k : 8 * k + 8] = packed_rows([f[0:8] for f in fields[:4]], False)
        flow = ux_ref[k] * wet
        open_low = flow[8:16] * pltpu.roll(wet[8:16], 7, 0)
        open_high = flow[0:8] * pltpu.roll(wet[0:8], 7, 0)
        face_low = jnp.where(row8 == 6, open_low, flow[8:16])
        face_high = jnp.where(row8 == 0, open_high, pltpu.roll(wet[0:8], 1, 0))
        tails[k] = ((state[2][8:16], face_low), (state[2][0:8], face_high))
        if k % 2 == 0:
            later = tails.pop(k + 1, tails[k])
            this = tails.pop(k)
            at = 8 * depth + 4 * k
            down_ref[at : at + 8] = packed_rows(this[0] + later[0], True)
            up_ref[at : at + 8] = packed_rows(this[1] + later[1], False)
        flow = uy_ref[k] * wet
        open_last = flow[:, 128:256] * pltpu.roll(wet[:, 128:256], 127, 1)
        open_first = flow[:, 0:128] * pltpu.roll(wet[:, 0:128], 127, 1)
        last = [f[:, 128:256] for f in fields] + [jnp.where(lane == 126, open_last, flow[:, 128:256])]
        first = [f[:, 0:128] for f in fields] + [
            jnp.where(lane == 0, open_first, pltpu.roll(wet[:, 0:128], 1, 1))
        ]
        last_parts = last + last_parts
        first_parts = first + first_parts
        if k % LEVELS == 0:
            g = k // LEVELS
            right_ref[g] = packed_cols(last_parts, spare[g % 2][0])
            left_ref[g] = packed_cols(first_parts, spare[g % 2][1])
            last_parts, first_parts = [], []
            for out in (a_out, c_out, w_out):
                out.send(k, LEVELS)
    for out in (down_out, right_out, up_out, left_out):
        out.send()


SCALE = 1.0 / 12.0
BF16 = jnp.bfloat16


class Edges:
    def __init__(self, place_ref, depth, above, below, west, east):
        r = place_ref[0]
        c = place_ref[1]
        self.depth, self.above, self.below, self.west, self.east = depth, above, below, west, east
        self.row8 = iota((8, 256), 0)
        self.lane16 = iota((16, 128), 1)
        has_up = jnp.where(r > 0, 1.0, 0.0)
        has_down = jnp.where(r < 15, 1.0, 0.0)
        has_left = jnp.where(c > 0, 1.0, 0.0)
        has_right = jnp.where(c < 15, 1.0, 0.0)
        self.above_rows = (self.row8 & 2) != 0
        self.row_flags = (
            jnp.where(self.above_rows, has_up, has_down),
            jnp.where(self.above_rows, has_down, has_up),
        )
        self.west_lanes = (self.lane16 & 2) != 0
        self.lane_flag = jnp.where(self.west_lanes, has_left, has_right)

    def row_pair(self, at, second):
        above = self.above[at : at + 8]
        below = self.below[at : at + 8]
        if second:
            return jnp.where(self.above_rows, below, above) * self.row_flags[1]
        return jnp.where(self.above_rows, above, below) * self.row_flags[0]

    def turned_rows(self, pair, f):
        turn = (8 - ROW_TURNS[f]) % 8
        return pltpu.roll(pair, turn, 0) if turn else pair

    def tail_rows(self, k, f):
        pair = self.row_pair(8 * self.depth + 8 * (k // 2), k % 2 == 1)
        return self.turned_rows(pair, f + 2 * (k % 2))

    def cols(self, k, f):
        g = k // LEVELS
        pair = jnp.where(self.west_lanes, self.west[g], self.east[g]) * self.lane_flag
        turn = 4 * (FIELDS * (k % LEVELS) + f)
        return pltpu.roll(pair, 128 - turn, 1) if turn else pair


def next_of(x, axis):
    return pltpu.roll(x, x.shape[axis] - 1, axis)


def last_of(x, axis):
    return pltpu.roll(x, 1, axis)


def two_parts(x):
    high = x.astype(BF16)
    return jnp.concatenate([high, (x - high.astype(F32)).astype(BF16)], axis=1)


def stencil(offsets, columns):
    out = np.zeros((384, columns), np.float32)
    for j in range(columns):
        for offset, value in offsets:
            out[(j + offset) % 384, j] += value
    return jnp.asarray(np.concatenate([out, out]), BF16)


def forward_kernel(ins, outs, place_ref, parts_ref, filtered_ref, theta_sweep_ref, salt_sweep_ref):
    (
        land_in,
        bottom_in,
        above_in,
        below_in,
        west_in,
        east_in,
        ux_in,
        uy_in,
        theta_in,
        salt_in,
        filter_in,
        forcing_in,
        kappa_in,
        inv_in,
        ratio_in,
    ) = ins
    x_out, y_out, theta_out, salt_out = outs
    x_open_ref, y_open_ref, theta_drop_ref, salt_drop_ref = [x.ref for x in outs]
    depth = theta_in.ref.shape[0]
    bottom = bottom_in.get()[...]
    land_ref = land_in.first()
    edges = Edges(place_ref, depth, *[x.get() for x in (above_in, below_in, west_in, east_in)])
    row8, lane16 = edges.row8, edges.lane16
    early = (ux_in, uy_in, theta_in, salt_in, land_in)
    ux_ref, uy_ref, theta_ref, salt_ref, _ = [x.first() for x in early]

    def wet_at(k):
        return jnp.where(k < bottom, land_ref[k].astype(F32), 0.0)

    for k in range(depth):
        if k == LEVELS:
            for x in early:
                x.get()
        wet = wet_at(k)
        faces = edges.tail_rows(k, 1)
        wide = jnp.concatenate([wet, pltpu.roll(faces, 7, 0)], axis=0)
        later = next_of(wide, 0)
        x_open = jnp.concatenate(
            [ux_ref[k] * wet * later[0:16], jnp.where(row8 == 7, faces * later[16:24], faces)], axis=0
        )
        x_open_ref[k] = x_open * SCALE
        faces = edges.cols(k, 5)
        wide = jnp.concatenate([wet, pltpu.roll(faces, 127, 1)], axis=1)
        later = next_of(wide, 1)
        y_open = jnp.concatenate(
            [uy_ref[k] * wet * later[:, 0:256], jnp.where(lane16 == 127, faces * later[:, 256:384], faces)], axis=1
        )
        y_open_ref[k] = y_open * SCALE
        for f, ref in ((0, theta_ref), (1, salt_ref)):
            wide = jnp.concatenate([ref[k] * wet, edges.cols(k, f)], axis=1)
            at = 16 * (depth * f + k)
            parts_ref[at : at + 16] = two_parts(wide)
    x_out.send()
    y_out.send()
    filtered_ref[...] = jnp.dot(parts_ref[...], filter_in.get()[...], preferred_element_type=F32)
    forcing_ref, kappa_ref, inv_ref, ratio_ref = [x.get() for x in (forcing_in, kappa_in, inv_in, ratio_in)]

    couple_last = None
    state = None
    wet = wet_at(0)
    for k in range(depth):
        rows = edges.row_pair(8 * k, False)
        x_open = x_open_ref[k]
        y_open = y_open_ref[k]
        advected = []
        for f, ref in ((0, theta_ref), (1, salt_ref)):
            q = ref[k]
            wide = jnp.concatenate([q * wet, edges.turned_rows(rows, f)], axis=0)
            pair = wide + next_of(wide, 0)
            flux = x_open * (8.0 * pair - last_of(pair, 0) - next_of(pair, 0))
            change = (flux - last_of(flux, 0))[0:16]
            at = 16 * (depth * f + k)
            flux = y_open * filtered_ref[at : at + 16]
            change = change + (flux - last_of(flux, 1))[:, 0:256]
            advected.append(q - change)
        if k == 0:
            advected[0] = advected[0] + forcing_ref[...] * wet
        inverse = inv_ref[k]
        if k == 0:
            state = tuple(x * inverse for x in advected)
        else:
            state = tuple((x + couple_last * s) * inverse for x, s in zip(advected, state))
        theta_sweep_ref[k], salt_sweep_ref[k] = state
        if k < depth - 1:
            wet_next = wet_at(k + 1)
            couple_last = kappa_ref[k] * wet * wet_next
            wet = wet_next
    wet_later = wet
    for k in range(depth - 2, -1, -1):
        wet = wet_at(k)
        ratio = ratio_ref[k]
        new = (theta_sweep_ref[k] + ratio * state[0], salt_sweep_ref[k] + ratio * state[1])
        opened = wet * wet_later
        theta_drop_ref[k] = opened * (state[0] - new[0])
        salt_drop_ref[k] = opened * (state[1] - new[1])
        state = new
        wet_later = wet
        if k % LEVELS == 0:
            theta_out.send(k, min(LEVELS, depth - 1 - k))
            salt_out.send(k, min(LEVELS, depth - 1 - k))


def backward_kernel(ins, outs, place_ref, parts_ref, filtered_ref):
    (
        sums_in,
        own_in,
        near_in,
        land_in,
        bottom_in,
        above_in,
        below_in,
        west_in,
        east_in,
        w_in,
        a_in,
        c_in,
        theta_drop_in,
        salt_drop_in,
        x_open_in,
        y_open_in,
        filter_in,
    ) = ins
    theta_out, salt_out, kappa_out, forcing_out = outs
    theta_grad_ref, salt_grad_ref, kappa_grad_ref, forcing_grad_ref = [x.ref for x in outs]
    depth = w_in.ref.shape[0]
    r = place_ref[0]
    has_down = jnp.where(r < 15, 1.0, 0.0)
    sums_ref, own_ref, near_ref = [x.get() for x in (sums_in, own_in, near_in)]

    small = (8, 128)
    small_row = iota(small, 0)
    terms = [(sums_ref[8 * at : 8 * at + 8], None) for at in range(32)]
    while len(terms) > 1:
        joined = []
        for x, y in zip(terms[::2], terms[1::2]):
            s, e = two_sum(x[0], y[0])
            joined.append((s, e if x[1] is None else (x[1] + y[1]) + e))
        terms = joined
    total = terms[0]
    for step in (4, 2, 1):
        s, e = two_sum(total[0], pltpu.roll(total[0], step, 0))
        total = (s, (total[1] + pltpu.roll(total[1], step, 0)) + e)
    low = total[1] + pltpu.roll(total[0] + total[1], 96, 1)
    total = quick_two_sum(total[0], low)

    def as_rows(x):
        out = x
        for i in range(1, KRYLOV):
            out = jnp.where(small_row == i, pltpu.roll(x, 128 - 8 * i, 1), out)
        return out

    system = (as_rows(total[0]), as_rows(total[1]))

    def row_of(x, k):
        return jnp.broadcast_to(x[k : k + 1, :], small)

    def lane_of(x, k):
        return jnp.broadcast_to(x[:, k : k + 1], small)

    keep = []
    weights = []
    scales = [lane_of(row_of(system[0], k), k) for k in range(KRYLOV)]
    for k in range(KRYLOV):
        across = (row_of(system[0], k), row_of(system[1], k))
        pivot = (lane_of(across[0], k), lane_of(across[1], k))
        fine = pivot[0] > 1e-13 * scales[k]
        keep.append(fine)
        pivot = (jnp.where(fine, pivot[0], 1.0), jnp.where(fine, pivot[1], 0.0))
        factor = df_div((lane_of(system[0], k), lane_of(system[1], k)), pivot)
        used = fine & (small_row != k)
        factor = (jnp.where(used, factor[0], 0.0), jnp.where(used, factor[1], 0.0))
        product = df_mul(factor, across)
        system = df_add(system, (-product[0], -product[1]))
    for k in range(KRYLOV):
        pivot = lane_of(row_of(system[0], k), k)
        value = lane_of(row_of(system[0], k), KRYLOV)
        value = jnp.where(keep[k], value / jnp.where(keep[k], pivot, 1.0), 0.0)
        weights.append(value[0:1, 0:1])

    def combined(ref, rows):
        out = weights[0] * ref[0:rows]
        for k in range(1, KRYLOV):
            out = out + weights[k] * ref[rows * k : rows * k + rows]
        return out

    def rows_joined(upper, lower):
        turned = pltpu.roll(lower, 4, 0)
        row8 = iota(turned.shape, 0)
        middle = jnp.where((row8 >= 5) & (r < 15), turned, upper[16:24])
        return jnp.concatenate([upper[0:16], middle, turned * has_down], axis=0)

    surface = rows_joined(combined(own_ref, 24), combined(near_ref, 8))
    zeta = surface[8:24, 0:256]
    bottom = bottom_in.get()[...]
    land_ref = land_in.first()
    edges = Edges(place_ref, depth, *[x.get() for x in (above_in, below_in, west_in, east_in)])
    zeta_rows = jnp.where(edges.row8 < 4, surface[24:32, 0:256], surface[0:8, 0:256])
    zeta_cols = surface[8:24, 256:384]

    def wet_at(k):
        return jnp.where(k < bottom, land_ref[k].astype(F32), 0.0)

    early = (w_in, a_in, c_in, theta_drop_in, salt_drop_in, x_open_in, y_open_in, land_in)
    w_ref, a_ref, c_ref, theta_drop_ref, salt_drop_ref, x_open_ref, y_open_ref, _ = [x.first() for x in early]
    share = (0.2, -0.15)
    mu_later = None
    for k in range(depth - 1, -1, -1):
        if k == depth - LEVELS - 1:
            for x in early:
                x.get()
        wet = wet_at(k)
        rise = zeta * w_ref[k]
        mu = (a_ref[k] + share[0] * rise, c_ref[k] + share[1] * rise)
        if k < depth - 1:
            kappa_grad_ref[k] = theta_drop_ref[k] * (mu[0] - mu_later[0]) + salt_drop_ref[k] * (mu[1] - mu_later[1])
        rows = edges.row_pair(8 * k, True)
        row_rise = zeta_rows * edges.tail_rows(k, 0)
        col_rise = zeta_cols * edges.cols(k, 4)
        x_open = x_open_ref[k]
        y_open = y_open_ref[k]
        for n, ref in ((0, theta_grad_ref), (1, salt_grad_ref)):
            wide = jnp.concatenate([mu[n], edges.cols(k, 2 + n) + share[n] * col_rise], axis=1)
            at = 16 * (depth * n + k)
            parts_ref[at : at + 16] = two_parts(y_open * (wide - next_of(wide, 1)))
            wide = jnp.concatenate([mu[n], edges.turned_rows(rows, 2 + n) + share[n] * row_rise], axis=0)
            h = x_open * (wide - next_of(wide, 0))
            pair = h + last_of(h, 0)
            change = (8.0 * pair - last_of(pair, 0) - next_of(pair, 0))[0:16]
            ref[k] = mu[n] - wet * change
        if k == 0:
            forcing_grad_ref[...] = zeta + wet * mu[0]
        mu_later = mu
    kappa_out.send()
    forcing_out.send()
    filtered_ref[...] = jnp.dot(parts_ref[...], filter_in.get()[...], preferred_element_type=F32)
    for n, ref, out in ((0, theta_grad_ref, theta_out), (1, salt_grad_ref, salt_out)):
        for k in range(depth):
            at = 16 * (depth * n + k)
            ref[k] = ref[k] - wet_at(k) * filtered_ref[at : at + 16]
            if k % 5 == 4:
                out.send(k - 4, 5)


def around(count, step):
    return [(i, (i + step) % count) for i in range(count)]


def across(down, right):
    return [
        (16 * i + j, 16 * ((i + down) % 16) + (j + right) % 16) for i in range(16) for j in range(16)
    ]


def shards(
    theta,
    salt,
    velocity_x,
    velocity_y,
    land_mask,
    kappa,
    forcing,
    bottom,
    theta_cot,
    salt_cot,
    surface_cot,
):
    depth = theta.shape[0]
    whole = theta.shape
    lines = 8 * depth + 8 * ((depth + 1) // 2)
    columns = (depth // LEVELS, 16, 128)
    a, c, w, inv, ratio, down, up, right, left, corner, cross = staged(
        columns_kernel,
        (land_mask, kappa, bottom, theta_cot, salt_cot, theta, salt, velocity_x, velocity_y, surface_cot),
        [whole] * 4
        + [kappa.shape, (lines + 16, 256), (lines, 256), columns, columns, (16, 128), (80, 128)],
        flops=100 * theta.size,
        lead=(0, LEVELS),
        sends=32,
    )
    corner = lax.ppermute(corner, ALL, across(1, 1))
    west = lax.ppermute(right, TCOL, around(16, 1))
    cross = lax.ppermute(cross, ALL, across(1, -1))
    east = lax.ppermute(left, TCOL, around(16, -1))
    above = lax.ppermute(down, TROW, around(16, 1))
    below = lax.ppermute(up, TROW, around(16, -1))
    near, own, sums = staged(
        krylov_kernel,
        (surface_cot, bottom, (above, lines, 16), corner, (west, 0, 2), (cross, 0, 16), (east, 0, 2)),
        [(32, 384), (96, 384), (256, 128)],
        place=True,
        after=(),
    )
    near = lax.ppermute(near, TROW, around(16, -1))
    x_open, y_open, theta_drop, salt_drop = staged(
        forward_kernel,
        (land_mask, bottom, above, below, west, east, velocity_x, velocity_y, theta, salt)
        + (stencil(((-1, -1), (0, 7), (1, 7), (2, -1)), 384), forcing, kappa, inv, ratio),
        [(depth, 24, 256), (depth, 16, 384), kappa.shape, kappa.shape],
        place=True,
        flops=200 * theta.size,
        lead=(0, LEVELS),
        sends=16,
        scratch=[((32 * depth, 768), BF16), ((32 * depth, 384), F32), (whole, F32), (whole, F32)],
    )
    sums = lax.all_to_all(sums, ALL, 0, 0, tiled=True)
    return tuple(
        staged(
            backward_kernel,
            (sums, own, near, land_mask, bottom, above, below, west, east, w, a, c)
            + (theta_drop, salt_drop, x_open, y_open, stencil(((-2, -1), (-1, 7), (0, 7), (1, -1)), 256)),
            [whole, whole, kappa.shape, forcing.shape],
            place=True,
            scratch=[((32 * depth, 768), BF16), ((32 * depth, 256), F32)],
            sends=12,
            lead=(depth - LEVELS, LEVELS),
        )
    )


def solution(mesh):
    split = Mesh(mesh.devices.reshape(4, 2, 2, 2, 8), ALL)
    block = P(None, TROW, TCOL)
    flat = P(TROW, TCOL)
    return jax.shard_map(
        shards,
        mesh=split,
        in_specs=(block,) * 6 + (flat, flat, block, block, flat),
        out_specs=(block, block, block, flat),
        check_vma=False,
    )
```
